32 devices in a mesh: seq: 8 (over z, core), fsdp: 4 (over y, x).
Axes of the slice: x: 2, y: 2, z: 4, core: 2. Of those that a mesh axis runs over, the one named last changes fastest.
Arguments:
- hidden_in: bfloat16 [5120, 2048], P(('seq', 'fsdp')), may hold values from -6 to 6
- w_input: bfloat16 [2, 2048, 2048], P(None, 'seq', 'fsdp'), may hold values from -0.125 to 0.125
- w_forget: bfloat16 [2, 2048, 2048], P(None, 'seq', 'fsdp'), may hold values from -0.125 to 0.125
- w_gate: bfloat16 [2, 2048, 2048], P(None, 'seq', 'fsdp'), may hold values from -0.125 to 0.125
- w_out: bfloat16 [2, 2048, 2048], P(None, 'fsdp', 'seq'), may hold values from -0.125 to 0.125
- w_up: bfloat16 [2, 2048, 5632], P(None, 'seq', 'fsdp'), may hold values from -0.125 to 0.125
- w_glu: bfloat16 [2, 2048, 5632], P(None, 'seq', 'fsdp'), may hold values from -0.125 to 0.125
- w_down: bfloat16 [2, 5632, 2048], P(None, 'fsdp', 'seq'), may hold values from -0.078125 to 0.078125
- lower_bound: float32 [2, 2048], replicated, may hold values from 0.9 to 0.99999609
- norm_mix: float32 [2, 2048], replicated, may hold values from 0.5 to 1.5
- norm_ffn: float32 [2, 2048], replicated, may hold values from 0.5 to 1.5
- out_gain: float32 [2, 2048], replicated, may hold values from 0.5 to 1.5
- lengths: int32 [5], replicated, may hold values from 1 to 4480, as said below
- cotangent: bfloat16 [5120, 2048], P(('seq', 'fsdp')), may hold values from -6 to 6
Outputs:
- hidden_out: bfloat16 [5120, 2048], P(('seq', 'fsdp'))
- grad_in: float32 [5120, 2048], P(('seq', 'fsdp'))
- grad_w_input: float32 [2, 2048, 2048], P(None, 'seq', 'fsdp')
- grad_w_forget: float32 [2, 2048, 2048], P(None, 'seq', 'fsdp')
- grad_w_gate: float32 [2, 2048, 2048], P(None, 'seq', 'fsdp')
- grad_w_out: float32 [2, 2048, 2048], P(None, 'fsdp', 'seq')
- grad_w_up: float32 [2, 2048, 5632], P(None, 'seq', 'fsdp')
- grad_w_glu: float32 [2, 2048, 5632], P(None, 'seq', 'fsdp')
- grad_w_down: float32 [2, 5632, 2048], P(None, 'fsdp', 'seq')
- grad_lower_bound: float32 [2, 2048], replicated
- grad_norm_mix: float32 [2, 2048], replicated
- grad_norm_ffn: float32 [2, 2048], replicated
- grad_out_gain: float32 [2, 2048], replicated
The draws below stay inside these ranges and needn't reach their ends.
Inputs may be any that keep to these rules, and one draw needn't show every extreme that they name: `lengths`: one sequence, neither the first nor the last, has 4480 rows; the others share 640 rows.
All inputs are finite; a program needn't handle non-finite values.
Results may differ from the reference program's by a relative error of at most 0.025.
Values may be sent and summed in bfloat16 or wider, within the bound.
No kernel may reach another device: no remote copies, remote signals or barrier semaphores. Data moves between devices by JAX's collectives and lax.ppermute only.
A program may use at most 256 MiB of HBM per device.

```python
import jax
import jax.numpy as jnp
from jax import lax

D = 2048
FF = 5632
LAYERS = 2
SEQS = 5
BLOCK = 640
TOKENS = 5120


def draw_lengths(key, part):
    key = jax.random.fold_in(key, 7)
    cut_key, place_key = jax.random.split(key)
    cuts = jnp.sort(jax.random.permutation(cut_key, BLOCK - 1)[:3] + 1).astype(jnp.int32)
    edges = jnp.concatenate([jnp.zeros((1,), jnp.int32), cuts, jnp.full((1,), BLOCK, jnp.int32)])
    shorts = edges[1:] - edges[:-1]
    place = jax.random.randint(place_key, (), 1, 4)
    index = jnp.arange(SEQS, dtype=jnp.int32)
    before = shorts[jnp.clip(index, 0, 3)]
    after = shorts[jnp.clip(index - 1, 0, 3)]
    longest = jnp.full((SEQS,), TOKENS - BLOCK, jnp.int32)
    return jnp.where(index < place, before, jnp.where(index == place, longest, after)).astype(jnp.int32)


def draw_lower_bound(key, part):
    key = jax.random.fold_in(key, 11)
    low_end = 0.05 / TOKENS
    high_end = 0.1
    uniform_part = jax.random.uniform(key, (LAYERS, D), jnp.float32)
    log_low = jnp.log(jnp.float32(low_end))
    log_high = jnp.log(jnp.float32(high_end))
    return (1.0 - jnp.exp(log_low + uniform_part * (log_high - log_low))).astype(jnp.float32)


def level_of(stream_key, dims, pieces, smallest, high):
    gain, own = 1.0, jax.random.fold_in(stream_key, 6)
    for axis_at, shards_of in pieces:
        draws = jnp.exp(jax.random.uniform(jax.random.fold_in(own, axis_at), (shards_of,), jnp.float32, smallest / len(pieces), high / len(pieces)))
        gain = gain * jnp.repeat(draws, dims[axis_at] // shards_of).reshape([-1 if axis == axis_at else 1 for axis in range(len(dims))])
    return gain


def noise(own_key, shape, scale, bound, shards=(), kind=jnp.bfloat16):
    loudness = level_of(own_key, shape, shards, -0.22, 0.18) if shards else 1.0
    drawn = jax.random.normal(own_key, shape, jnp.float32) * scale * loudness
    return jnp.minimum(jnp.maximum(drawn, -bound), bound).astype(kind)


def setup_inputs(seed: int = 0) -> dict:
    key_list = jax.random.split(jax.random.key(seed), 15)
    return {
        "hidden_in": noise(key_list[0], (TOKENS, D), 1.0, 6.0, ((0, 32),)),
        "w_input": noise(key_list[1], (LAYERS, D, D), D ** -0.5, 0.125, ((1, 8), (2, 4))),
        "w_forget": noise(key_list[2], (LAYERS, D, D), D ** -0.5, 0.125, ((1, 8), (2, 4))),
        "w_gate": noise(key_list[3], (LAYERS, D, D), D ** -0.5, 0.125, ((1, 8), (2, 4))),
        "w_out": noise(key_list[4], (LAYERS, D, D), D ** -0.5, 0.125, ((1, 4), (2, 8))),
        "w_up": noise(key_list[5], (LAYERS, D, FF), D ** -0.5, 0.125, ((1, 8), (2, 4))),
        "w_glu": noise(key_list[6], (LAYERS, D, FF), D ** -0.5, 0.125, ((1, 8), (2, 4))),
        "w_down": noise(key_list[7], (LAYERS, FF, D), FF ** -0.5, 0.078125, ((1, 4), (2, 8))),
        "lower_bound": draw_lower_bound(jax.random.fold_in(key_list[14], 71), 0),
        "norm_mix": jnp.clip(1.0 + 0.1 * jax.random.normal(key_list[9], (LAYERS, D), jnp.float32), 0.5, 1.5),
        "norm_ffn": jnp.clip(1.0 + 0.1 * jax.random.normal(key_list[10], (LAYERS, D), jnp.float32), 0.5, 1.5),
        "out_gain": jnp.clip(1.0 + 0.1 * jax.random.normal(key_list[11], (LAYERS, D), jnp.float32), 0.5, 1.5),
        "lengths": draw_lengths(jax.random.fold_in(key_list[14], 71), 0),
        "cotangent": noise(key_list[13], (TOKENS, D), 1.0, 6.0, ((0, 32),)),
    }


@jax.custom_vjp
def low(v):
    return lax.optimization_barrier(v.astype(jnp.bfloat16)).astype(jnp.float32)

@jax.custom_vjp
def low_back(v):
    return v

def low_keep(v):
    return (low(v), None)

def low_pass(kept, grad):
    return (grad,)

def back_keep(v):
    return (v, None)

def back_low(kept, grad):
    return (low(grad),)
low.defvjp(low_keep, low_pass)
low_back.defvjp(back_keep, back_low)
epsilon = 1e-06

def product(left_side, right_side):
    return jnp.dot(left_side, right_side, precision=lax.Precision.HIGHEST)

def combine(earlier, later_part):
    return (earlier[0] * later_part[0], later_part[0] * earlier[1] + later_part[1])

def normalize(values):
    return values * lax.rsqrt(lax.optimization_barrier(jnp.mean(values * values, axis=-1, keepdims=True)) + epsilon)

def block_layer(stream, params, keep_mask):
    input_matrix, forget_matrix, gate_matrix, output_matrix, up_matrix, glu_matrix, down_matrix, bound_row, gain_mix, gain_ffn, gain_out = params
    normed = low(normalize(stream) * gain_mix)
    proj_input = low_back(product(normed, input_matrix))
    proj_forget = low_back(product(normed, forget_matrix))
    proj_gate = low_back(product(normed, gate_matrix))
    forget = bound_row + (1.0 - bound_row) * jax.nn.sigmoid(proj_forget)
    source = jax.nn.silu(proj_input) * (1.0 - forget)
    decay_all = forget * keep_mask[:, None]
    state_all = lax.associative_scan(combine, (decay_all, source), axis=0)[1]
    mixed_out = low(normalize(state_all) * gain_out * jax.nn.silu(proj_gate))
    middle = stream + low_back(product(mixed_out, output_matrix))
    normed_two = low(normalize(middle) * gain_ffn)
    upward = low_back(product(normed_two, up_matrix))
    gating = low_back(product(normed_two, glu_matrix))
    hidden = low(jax.nn.silu(gating) * upward)
    return middle + low_back(product(hidden, down_matrix))

def reference(hidden_in, w_input, w_forget, w_gate, w_out, w_up, w_glu, w_down, lower_bound, norm_mix, norm_ffn, out_gain, lengths, cotangent):
    starts = jnp.cumsum(lengths).astype(jnp.int32) - lengths.astype(jnp.int32)
    positions = jnp.arange(TOKENS, dtype=jnp.int32)
    keep_mask = 1.0 - jnp.any(positions[:, None] == starts[None, :], axis=1).astype(jnp.float32)

    def forward(stream, *params):
        for layer_index in range(LAYERS):
            stream = block_layer(stream, tuple((param[layer_index] for param in params)), keep_mask)
        return stream
    params = tuple((param.astype(jnp.float32) for param in (w_input, w_forget, w_gate, w_out, w_up, w_glu, w_down, lower_bound, norm_mix, norm_ffn, out_gain)))
    result, pullback = jax.vjp(forward, hidden_in.astype(jnp.float32), *params)
    grads = pullback(cotangent.astype(jnp.float32))
    return (result.astype(jnp.bfloat16), grads[0], grads[1], grads[2], grads[3], grads[4], grads[5], grads[6], grads[7], grads[8], grads[9], grads[10], grads[11])
```

```python
import functools

import jax
import jax.numpy as jnp
from jax import lax
from jax.experimental import pallas as pl
from jax.experimental.pallas import tpu as pltpu
from jax.sharding import PartitionSpec as P

LAYERS = 2
epsilon = 1e-06
STEP = 32
LANES = 256
f32 = jnp.float32
bf16 = jnp.bfloat16


def partners(step):
    return [(i, i ^ step) for i in range(lax.axis_size("fsdp"))]


def exchange(values, step):
    return lax.ppermute(values, "fsdp", partners(step))


def gather_rows(own):
    size = lax.axis_size("fsdp")
    return jnp.concatenate([own] + [exchange(own, step) for step in range(1, size)], axis=0)


def scatter_rows(part):
    size = lax.axis_size("fsdp")
    rows = part.shape[0] // size
    arrived = [exchange(part[step * rows : (step + 1) * rows], step) for step in range(1, size)]
    total = part[:rows].astype(f32)
    for piece in arrived:
        total = total + piece.astype(f32)
    return total


def total_rows(part):
    size = lax.axis_size("fsdp")
    pieces = part.reshape(size, -1)
    total = pieces
    for step in range(1, size):
        other = exchange(pieces, step)
        total = total + jnp.stack([other[k ^ step] for k in range(size)])
    return total.reshape(-1)


def dot(operand, matrix):
    return jnp.dot(operand, matrix, preferred_element_type=f32)


def trans_dot(operand, matrix):
    return lax.dot_general(operand, matrix, (((1,), (1,)), ((), ())), preferred_element_type=f32)


def outer_dot(operand, other):
    return lax.dot_general(operand, other, (((0,), (0,)), ((), ())), preferred_element_type=f32)


def rms_parts(values):
    factor = lax.rsqrt(jnp.mean(values * values, axis=-1, keepdims=True) + epsilon)
    return (values * factor, factor)


def norm_back(grad_unit, unit_rows, factor):
    return factor * (
        grad_unit - unit_rows * jnp.mean(grad_unit * unit_rows, axis=-1, keepdims=True)
    )


def dsilu(values, sigma):
    return sigma * (1.0 + values * (1.0 - sigma))


def sigmoid(values):
    return 1.0 / (1.0 + jnp.exp(-values))


def tile_base(place, index, size, per_piece):
    piece = lax.bitwise_xor(index // per_piece, place)
    return pl.multiple_of((piece * per_piece + lax.rem(index, per_piece)) * STEP, STEP)


def scan_kernel(size, place_ref, pi_ref, pf_ref, keep_ref, bound_ref, state_ref, decay_ref):
    rows, lanes = pi_ref.shape
    per_piece = rows // size // STEP
    place = place_ref[0]
    bound = bound_ref[...]
    row = lax.broadcasted_iota(jnp.int32, (8, lanes), 0)

    def step(index, carry):
        carry_decay, carry_state = carry
        base = tile_base(place, index, size, per_piece)
        here = pl.ds(base, STEP)
        forget = bound + (1.0 - bound) * sigmoid(pf_ref[here, :])
        inp = pi_ref[here, :]
        source = inp * sigmoid(inp) * (1.0 - forget)
        decay = forget * keep_ref[here, :]
        for part in range(STEP // 8):
            a = decay[part * 8 : part * 8 + 8]
            b = source[part * 8 : part * 8 + 8]
            for shift in (1, 2, 4):
                a_before = jnp.where(row >= shift, pltpu.roll(a, shift, 0), 1.0)
                b_before = jnp.where(row >= shift, pltpu.roll(b, shift, 0), 0.0)
                b = a * b_before + b
                a = a * a_before
            b = a * carry_state + b
            a = a * carry_decay
            state_ref[pl.ds(base + part * 8, 8), :] = b
            decay_ref[pl.ds(base + part * 8, 8), :] = a
            carry_decay, carry_state = a[7:8], b[7:8]
        return carry_decay, carry_state

    lax.fori_loop(
        0, rows // STEP, step, (jnp.ones((1, lanes), f32), jnp.zeros((1, lanes), f32))
    )


def back_kernel(
    size, width, place_ref, mixed_ref, state_ref, gate_ref, pf_ref, inverse_ref, inner_ref,
    keep_ref, bound_ref, gain_ref, adjoint_ref, reach_ref, grad_gate_ref, mix_ref, gain_out_ref,
):
    rows, lanes = mixed_ref.shape
    per_piece = rows // size // STEP
    place = place_ref[0]
    bound = bound_ref[...]
    gain = gain_ref[...]
    row = lax.broadcasted_iota(jnp.int32, (8, lanes), 0)
    tiles = rows // STEP

    def step(count, carry):
        carry_reach, carry_adjoint, later, gain_sum = carry
        base = tile_base(place, tiles - 1 - count, size, per_piece)
        here = pl.ds(base, STEP)
        grad_mixed = mixed_ref[here, :]
        inverse = inverse_ref[here, :]
        scaled = state_ref[here, :] * inverse
        gate = gate_ref[here, :]
        sigma = sigmoid(gate)
        silu_gate = gate * sigma
        piece = grad_mixed * scaled
        contribution = piece * silu_gate
        grad_gate_ref[here, :] = (piece * gain * dsilu(gate, sigma)).astype(bf16)
        mix_ref[here, :] = (scaled * gain * silu_gate).astype(bf16)
        grad_state = inverse * (
            grad_mixed * gain * silu_gate - scaled * (inner_ref[here, :] * (1.0 / width))
        )
        decay = (bound + (1.0 - bound) * sigmoid(pf_ref[here, :])) * keep_ref[here, :]
        for part in reversed(range(STEP // 8)):
            now = decay[part * 8 : part * 8 + 8]
            gain_sum = gain_sum + contribution[part * 8 : part * 8 + 8]
            a = jnp.where(row == 7, later, pltpu.roll(now, 7, 0))
            b = grad_state[part * 8 : part * 8 + 8]
            for shift in (1, 2, 4):
                a_after = jnp.where(row < 8 - shift, pltpu.roll(a, 8 - shift, 0), 1.0)
                b_after = jnp.where(row < 8 - shift, pltpu.roll(b, 8 - shift, 0), 0.0)
                b = a * b_after + b
                a = a * a_after
            b = a * carry_adjoint + b
            a = a * carry_reach
            adjoint_ref[pl.ds(base + part * 8, 8), :] = b
            reach_ref[pl.ds(base + part * 8, 8), :] = a
            carry_reach, carry_adjoint, later = a[0:1], b[0:1], now[0:1]
        return carry_reach, carry_adjoint, later, gain_sum

    one, zero = jnp.ones((1, lanes), f32), jnp.zeros((1, lanes), f32)
    last = lax.fori_loop(0, tiles, step, (one, zero, one, jnp.zeros((8, lanes), f32)))
    gain_out_ref[...] = jnp.sum(last[3], axis=0, keepdims=True)


def gates_kernel(
    size, place_ref, adjoint_ref, reach_ref, state_ref, pi_ref, pf_ref, keep_ref, bound_ref,
    coming_ref, entering_ref, grad_input_ref, grad_forget_ref, bound_out_ref,
):
    rows, lanes = adjoint_ref.shape
    per_piece = rows // size // STEP
    place = place_ref[0]
    bound = bound_ref[...]
    coming = coming_ref[...]
    row = lax.broadcasted_iota(jnp.int32, (STEP, lanes), 0)

    def step(index, carry):
        before, bound_sum = carry
        base = tile_base(place, index, size, per_piece)
        here = pl.ds(base, STEP)
        adjoint = adjoint_ref[here, :] + reach_ref[here, :] * coming
        state = state_ref[here, :]
        previous = jnp.where(row == 0, before, pltpu.roll(state, 1, 0))
        inp = pi_ref[here, :]
        sigma_input = sigmoid(inp)
        sigma_forget = sigmoid(pf_ref[here, :])
        forget = bound + (1.0 - bound) * sigma_forget
        grad_forget = adjoint * (keep_ref[here, :] * previous - inp * sigma_input)
        piece = grad_forget * (1.0 - sigma_forget)
        grad_input_ref[here, :] = (adjoint * (1.0 - forget) * dsilu(inp, sigma_input)).astype(bf16)
        grad_forget_ref[here, :] = (piece * (1.0 - bound) * sigma_forget).astype(bf16)
        for part in range(STEP // 8):
            bound_sum = bound_sum + piece[part * 8 : part * 8 + 8]
        return state[STEP - 1 : STEP], bound_sum

    last = lax.fori_loop(
        0, rows // STEP, step, (entering_ref[...], jnp.zeros((8, lanes), f32))
    )
    bound_out_ref[...] = jnp.sum(last[1], axis=0, keepdims=True)


def over_channels(kernel, place, operands, outs, cost):
    channels = operands[0].shape[1]
    lanes = min(LANES, channels)

    def spec(rows, whole):
        if whole:
            return pl.BlockSpec((rows, 1), lambda c, p: (0, 0))
        return pl.BlockSpec((rows, lanes), lambda c, p: (0, c))

    return pl.pallas_call(
        kernel,
        grid_spec=pltpu.PrefetchScalarGridSpec(
            num_scalar_prefetch=1,
            grid=(channels // lanes,),
            in_specs=[spec(o.shape[0], o.shape[1] == 1) for o in operands],
            out_specs=[spec(rows, False) for rows, _ in outs],
        ),
        out_shape=[jax.ShapeDtypeStruct((rows, channels), kind) for rows, kind in outs],
        compiler_params=pltpu.CompilerParams(vmem_limit_bytes=48 * 1024 * 1024),
        cost_estimate=pl.CostEstimate(
            flops=cost * operands[0].size, bytes_accessed=4 * (len(operands) + len(outs)) * operands[0].size,
            transcendentals=2 * operands[0].size,
        ),
    )(place, *operands)


def entering_of(decay, state, reverse):
    length, here = lax.axis_size("seq"), lax.axis_index("seq")
    everything = lax.all_gather(jnp.concatenate([decay, state], axis=0), "seq")
    total = jnp.zeros_like(state)
    for k in range(length):
        at = length - 1 - k if reverse else k
        reached = at > here if reverse else at < here
        new = everything[at, 0:1] * total + everything[at, 1:2]
        total = jnp.where(reached, new, total)
    return total


def total_small(rows_of_width, rows_of_channels, first_channel, channels):
    size = lax.axis_size("fsdp")
    place = lax.axis_index("fsdp")

    def columns(step):
        return lax.dynamic_slice_in_dim(
            rows_of_width, lax.bitwise_xor(place, step) * channels, channels, 1
        )

    mine = columns(0)
    for step in range(1, size):
        mine = mine + exchange(columns(step), step)
    mine = jnp.sum(lax.all_gather(jnp.concatenate([mine, rows_of_channels], axis=0), "seq"), axis=0)
    whole = jnp.zeros((mine.shape[0], channels * size), f32)
    whole = lax.dynamic_update_slice_in_dim(whole, mine, first_channel, 1)
    for step in range(1, size):
        whole = lax.dynamic_update_slice_in_dim(
            whole, exchange(mine, step), lax.bitwise_xor(place, step) * channels, 1
        )
    return whole


def local(
    hidden_in, w_input, w_forget, w_gate, w_out, w_up, w_glu, w_down,
    lower_bound, norm_mix, norm_ffn, out_gain, lengths, cotangent,
):
    row_count, model_width = hidden_in.shape
    channels = w_input.shape[2]
    hidden_units = w_up.shape[2]
    size = lax.axis_size("fsdp")
    place = lax.axis_index("fsdp")
    block_rows = row_count * size
    first_channel = place * channels
    place_array = jnp.reshape(place, (1,)).astype(jnp.int32)

    starts = jnp.cumsum(lengths) - lengths
    owners = lax.bitwise_xor(jnp.arange(size, dtype=jnp.int32), place.astype(jnp.int32))
    positions = (
        lax.axis_index("seq") * block_rows
        + (owners[:, None] * row_count + jnp.arange(row_count, dtype=jnp.int32)[None, :])
    ).reshape(-1)
    keep = (1.0 - jnp.any(positions[:, None] == starts[None, :], axis=1).astype(f32))[:, None]
    bounds = lax.dynamic_slice_in_dim(lower_bound, first_channel, channels, 1)
    gains = lax.dynamic_slice_in_dim(out_gain, first_channel, channels, 1)

    matrices = []
    for layer in range(LAYERS):
        mix_matrix = lax.all_gather(
            jnp.concatenate([w_input[layer], w_forget[layer], w_gate[layer]], axis=1),
            "seq", axis=0, tiled=True,
        )
        out_matrix = lax.all_gather(w_out[layer], "seq", axis=1, tiled=True)
        up_matrix = lax.all_gather(
            jnp.concatenate([w_up[layer], w_glu[layer]], axis=1), "seq", axis=0, tiled=True
        )
        down_matrix = lax.all_gather(w_down[layer], "seq", axis=1, tiled=True)
        matrices.append((mix_matrix, out_matrix, up_matrix, down_matrix))

    stream = hidden_in.astype(f32)
    saved = []
    for layer in range(LAYERS):
        mix_matrix, out_matrix, up_matrix, down_matrix = matrices[layer]
        bound, gain = bounds[layer][None, :], gains[layer][None, :]
        unit, _ = rms_parts(stream)
        normed = gather_rows((unit * norm_mix[layer]).astype(bf16))
        projected = dot(normed, mix_matrix)
        proj_input = projected[:, :channels]
        proj_forget = projected[:, channels : 2 * channels]
        proj_gate = projected[:, 2 * channels :]
        local_state, local_decay = over_channels(
            functools.partial(scan_kernel, size),
            place_array,
            (proj_input, proj_forget, keep, bound),
            ((block_rows, f32), (block_rows, f32)),
            40,
        )
        last_row = lax.bitwise_xor(size - 1, place) * row_count + row_count - 1
        entering = entering_of(
            lax.dynamic_slice_in_dim(local_decay, last_row, 1, 0),
            lax.dynamic_slice_in_dim(local_state, last_row, 1, 0),
            False,
        )
        state = local_state + local_decay * entering
        squares = total_rows(jnp.sum(state * state, axis=1))
        inverse = lax.rsqrt(squares / model_width + epsilon)[:, None]
        loose = (state * gain * jax.nn.silu(proj_gate)).astype(bf16)
        branch = scatter_rows(dot(loose, out_matrix).astype(bf16)) * inverse[:row_count]
        middle = stream + branch
        unit_two, _ = rms_parts(middle)
        normed_two = gather_rows((unit_two * norm_ffn[layer]).astype(bf16))
        both = dot(normed_two, up_matrix)
        upward, gating = both[:, :hidden_units], both[:, hidden_units:]
        hidden = (jax.nn.silu(gating) * upward).astype(bf16)
        saved.append(
            (stream, normed, proj_input, proj_forget, proj_gate, entering, state, inverse,
             branch, middle, normed_two, upward, gating, hidden)
        )
        stream = middle + scatter_rows(dot(hidden, down_matrix).astype(bf16))
    hidden_out = stream.astype(bf16)

    grad_x = cotangent.astype(f32)
    shards = [None] * LAYERS
    smalls = [None] * LAYERS
    for layer in reversed(range(LAYERS)):
        mix_matrix, out_matrix, up_matrix, down_matrix = matrices[layer]
        bound, gain = bounds[layer][None, :], gains[layer][None, :]
        (stream, normed, proj_input, proj_forget, proj_gate, entering, state, inverse,
         branch, middle, normed_two, upward, gating, hidden) = saved[layer]
        unit, factor = rms_parts(stream)
        unit_two, factor_two = rms_parts(middle)

        grad_y = gather_rows(grad_x.astype(bf16))
        grad_hidden = trans_dot(grad_y, down_matrix)
        down_part = outer_dot(hidden, grad_y).astype(bf16)
        sigma = jax.nn.sigmoid(gating)
        grad_both = jnp.concatenate(
            [
                (grad_hidden * gating * sigma).astype(bf16),
                (grad_hidden * upward * dsilu(gating, sigma)).astype(bf16),
            ],
            axis=1,
        )
        grad_normed_two = scatter_rows(trans_dot(grad_both, up_matrix).astype(bf16))
        up_part = outer_dot(normed_two, grad_both).astype(bf16)
        ffn_piece = jnp.sum(grad_normed_two * unit_two, axis=0)
        grad_middle = grad_x + norm_back(grad_normed_two * norm_ffn[layer], unit_two, factor_two)

        grad_m_own = grad_middle.astype(bf16)
        grad_m = gather_rows(grad_m_own)
        inner = gather_rows(jnp.sum(grad_m_own.astype(f32) * branch, axis=1))[:, None]
        grad_mixed = trans_dot(grad_m, out_matrix)
        adjoint, reach, grad_gate, mixed, gain_piece = over_channels(
            functools.partial(back_kernel, size, model_width),
            place_array,
            (grad_mixed, state, proj_gate, proj_forget, inverse, inner, keep, bound, gain),
            ((block_rows, f32), (block_rows, f32), (block_rows, bf16), (block_rows, bf16), (1, f32)),
            60,
        )
        out_part = outer_dot(mixed, grad_m).astype(bf16)
        first_row = place * row_count
        first_decay = (
            bound
            + (1.0 - bound)
            * jax.nn.sigmoid(lax.dynamic_slice_in_dim(proj_forget, first_row, 1, 0))
        ) * lax.dynamic_slice_in_dim(keep, first_row, 1, 0)
        coming = entering_of(
            first_decay * lax.dynamic_slice_in_dim(reach, first_row, 1, 0),
            first_decay * lax.dynamic_slice_in_dim(adjoint, first_row, 1, 0),
            True,
        )
        grad_input, grad_forget, bound_piece = over_channels(
            functools.partial(gates_kernel, size),
            place_array,
            (adjoint, reach, state, proj_input, proj_forget, keep, bound, coming, entering),
            ((block_rows, bf16), (block_rows, bf16), (1, f32)),
            40,
        )
        grad_three = jnp.concatenate([grad_input, grad_forget, grad_gate], axis=1)
        grad_normed = scatter_rows(trans_dot(grad_three, mix_matrix).astype(bf16))
        mix_part = outer_dot(normed, grad_three).astype(bf16)
        mix_piece = jnp.sum(grad_normed * unit, axis=0)
        grad_x = grad_middle + norm_back(grad_normed * norm_mix[layer], unit, factor)

        down_shard = lax.psum_scatter(down_part, "seq", scatter_dimension=1, tiled=True)
        up_shard = lax.psum_scatter(up_part, "seq", scatter_dimension=0, tiled=True)
        out_shard = lax.psum_scatter(out_part, "seq", scatter_dimension=1, tiled=True)
        mix_shard = lax.psum_scatter(mix_part, "seq", scatter_dimension=0, tiled=True)
        shards[layer] = (
            mix_shard[:, :channels],
            mix_shard[:, channels : 2 * channels],
            mix_shard[:, 2 * channels :],
            out_shard,
            up_shard[:, :hidden_units],
            up_shard[:, hidden_units:],
            down_shard,
        )
        smalls[layer] = total_small(
            jnp.stack([mix_piece, ffn_piece]),
            jnp.concatenate([bound_piece, gain_piece], axis=0),
            first_channel,
            channels,
        )
    stacked = tuple(
        jnp.stack([shards[layer][member].astype(f32) for layer in range(LAYERS)])
        for member in range(7)
    )
    small = jnp.stack(smalls)
    return (hidden_out, grad_x, *stacked, small[:, 2], small[:, 0], small[:, 1], small[:, 3])


def solution(mesh):
    rows = P(("seq", "fsdp"), None)
    wide = P(None, "seq", "fsdp")
    tall = P(None, "fsdp", "seq")
    weights = (wide, wide, wide, tall, wide, wide, tall)
    return jax.shard_map(
        local,
        mesh=mesh,
        in_specs=(rows, *weights, P(), P(), P(), P(), P(), rows),
        out_specs=(rows, rows, *weights, P(), P(), P(), P()),
        check_vma=False,
    )
```

```python
import functools

import jax
import jax.numpy as jnp
from jax import lax
from jax.experimental import pallas as pl
from jax.experimental.pallas import tpu as pltpu
from jax.sharding import Mesh
from jax.sharding import PartitionSpec as P

LAYERS = 2
epsilon = 1e-06
STEP = 32
LANES = 256
VMEM = 52 * 1024 * 1024
f32 = jnp.float32
bf16 = jnp.bfloat16
SEQ = ("chip", "core")
NT = (((1,), (1,)), ((), ()))


def exchange(values, step):
    size = lax.axis_size("fsdp")
    return lax.ppermute(values, "fsdp", [(i, i ^ step) for i in range(size)])


def swap(values, axis):
    return lax.ppermute(values, axis, [(0, 1), (1, 0)])


def seq_length():
    return lax.axis_size("chip") * lax.axis_size("core")


def after(value, *others):
    return lax.optimization_barrier((value, *others))[0]


def all_after(values, *others):
    return list(lax.optimization_barrier((*values, *others)))[: len(values)]


def gather_rows(own, *meanwhile):
    arrived = [exchange(own, step) for step in range(1, lax.axis_size("fsdp"))]
    return [own] + all_after(arrived, *meanwhile)


def scatter_rows(pieces, between=None, *meanwhile):
    arrived = [exchange(pieces[step], step) for step in range(1, len(pieces))]
    made = None
    if between is not None:
        made, result = between()
        arrived = all_after(arrived, *made, *meanwhile)
    total = pieces[0].astype(f32)
    for piece in arrived:
        total = total + piece.astype(f32)
    return total if made is None else (total, result)


def total_rows(part):
    size = lax.axis_size("fsdp")
    pieces = part.reshape(size, -1)
    total = pieces
    for step in range(1, size):
        other = exchange(pieces, step)
        total = total + jnp.stack([other[k ^ step] for k in range(size)])
    return total.reshape(-1)


def rms_parts(values):
    factor = lax.rsqrt(jnp.mean(values * values, axis=-1, keepdims=True) + epsilon)
    return (values * factor, factor)


def norm_back(grad_unit, unit_rows, factor):
    return factor * (
        grad_unit - unit_rows * jnp.mean(grad_unit * unit_rows, axis=-1, keepdims=True)
    )


def dsilu(values, sigma):
    return sigma * (1.0 + values * (1.0 - sigma))


def sigmoid(values):
    return 1.0 / (1.0 + jnp.exp(-values))


def dot(left, right):
    return jnp.dot(left, right, preferred_element_type=f32)


def trans_dot(left, right):
    return lax.dot_general(left, right, NT, preferred_element_type=f32)


def whole(array):
    return pl.BlockSpec(array.shape, lambda j, *_: (0, 0))


def call(kernel, grid, in_specs, out_specs, out_shape, scratch, operands, cost, prefetch=()):
    return pl.pallas_call(
        kernel,
        grid_spec=pltpu.PrefetchScalarGridSpec(
            num_scalar_prefetch=len(prefetch),
            grid=grid,
            in_specs=in_specs,
            out_specs=out_specs,
            scratch_shapes=scratch,
        ),
        out_shape=out_shape,
        compiler_params=pltpu.CompilerParams(vmem_limit_bytes=VMEM),
        cost_estimate=pl.CostEstimate(flops=cost, bytes_accessed=cost // 512, transcendentals=0),
    )(*prefetch, *operands)


def assemble(pieces, rows_ref):
    rows = pieces[0].shape[0]

    @pl.when(pl.program_id(0) == 0)
    def _():
        for k, piece in enumerate(pieces):
            rows_ref[k * rows : (k + 1) * rows, :] = piece[...]


def outer(terms):
    lefts = [left for left, _ in terms]
    groups, which = [], []
    for _, pieces in terms:
        found = [k for k, group in enumerate(groups) if group is pieces]
        which.append(found[0] if found else len(groups))
        if not found:
            groups.append(pieces)
    rows, width = lefts[0].shape[0], groups[0][0].shape[1] // seq_length()
    heights = [left.shape[1] for left in lefts]
    total, count, chips = sum(heights), len(groups[0]), lax.axis_size("chip")

    def kernel(core_ref, *refs):
        left_refs, refs = refs[: len(lefts)], refs[len(lefts) :]
        piece_refs, (own, other, turned) = refs[: 2 * count * len(groups)], refs[2 * count * len(groups) :]

        @pl.when(pl.program_id(0) == 0)
        def _():
            top = 0
            for left, height in zip(left_refs, heights, strict=True):
                turned[top : top + height, :] = left[...].T
                top += height

        rights = []
        for g in range(len(groups)):
            halves = [
                jnp.concatenate([ref[...] for ref in piece_refs[k * count : (k + 1) * count]], axis=0)
                for k in (2 * g, 2 * g + 1)
            ]
            rights.append(jnp.concatenate(halves, axis=1))
        top = 0
        for height, group in zip(heights, which, strict=True):
            both = dot(turned[top : top + height, :], rights[group]).astype(bf16)
            own[top : top + height, :] = both[:, :width]
            other[top : top + height, :] = both[:, width:]
            top += height

    def columns(pieces, flip):
        return [
            pl.BlockSpec((p.shape[0], width), lambda j, core: (0, 2 * j + (1 - core[0] if flip else core[0])))
            for p in pieces
        ]

    out = jax.ShapeDtypeStruct((total, width * chips), bf16)
    return call(
        kernel,
        (chips,),
        [whole(left) for left in lefts]
        + [spec for group in groups for flip in (False, True) for spec in columns(group, flip)],
        [pl.BlockSpec((total, width), lambda j, core: (0, j))] * 2,
        [out, out],
        [pltpu.VMEM((total, rows), bf16)],
        [*lefts, *(piece for group in groups for _ in range(2) for piece in group)],
        6 * rows * total * width * 2 * chips,
        prefetch=(jnp.reshape(lax.axis_index("core"), (1,)).astype(jnp.int32),),
    )


def scatter_columns(halves):
    own, other = halves
    half = (own.astype(f32) + swap(other, "core").astype(f32)).astype(bf16)
    return lax.psum_scatter(half, "chip", scatter_dimension=1, tiled=True)


def cut(values, count):
    rows = values.shape[0] // count
    return [values[k * rows : (k + 1) * rows] for k in range(count)]


def rows_at(matrix, at, rows, tile):
    return (matrix, at // tile) if at % tile == 0 else (matrix[at : at + rows], 0)


def tile_of(units):
    return (128, units // 128) if units % 128 == 0 else (units, 1)


def up_and_gate(pieces, both, units):
    rows, depth = sum(p.shape[0] for p in pieces), pieces[0].shape[1]
    tile, steps = tile_of(units)
    chunk = rows if steps > 1 else rows // 4

    def kernel(*refs):
        piece_refs, (up_ref, gate_ref, upward_ref, gating_ref, hidden_ref, x_ref) = (
            refs[: len(pieces)], refs[len(pieces) :],
        )
        assemble(piece_refs, x_ref)
        for start in range(0, rows, chunk):
            here = slice(start, start + chunk)
            x = x_ref[here, :]
            if steps > 1:
                joined = trans_dot(x, jnp.concatenate([up_ref[...], gate_ref[...]], axis=0))
                upward, gating = joined[:, :tile], joined[:, tile:]
            else:
                upward, gating = trans_dot(x, up_ref[...]), trans_dot(x, gate_ref[...])
            upward_ref[here, :] = upward.astype(bf16)
            gating_ref[here, :] = gating.astype(bf16)
            hidden_ref[here, :] = (gating * sigmoid(gating) * upward).astype(bf16)

    out = jax.ShapeDtypeStruct((rows, units), bf16)
    return call(
        kernel,
        (steps,),
        [whole(p) for p in pieces]
        + [
            pl.BlockSpec((tile, depth), lambda j: (j, 0)),
            pl.BlockSpec((tile, depth), lambda j: (steps + j, 0)),
        ],
        [pl.BlockSpec((rows, tile), lambda j: (0, j))] * 3,
        [out] * 3,
        [pltpu.VMEM((rows, depth), bf16)],
        [*pieces, both, both],
        4 * rows * depth * units,
    )


def up_and_gate_back(pieces, down, at, upward, gating):
    rows, depth = sum(p.shape[0] for p in pieces), pieces[0].shape[1]
    units = upward.shape[1]
    tile, steps = (256, -(-units // 256)) if units % 128 == 0 else (units, 1)
    down, first = rows_at(down, at, units, tile)
    chunk = rows if steps > 1 else rows // 4

    def kernel(*refs):
        piece_refs, (down_ref, upward_ref, gating_ref, grad_up_ref, grad_gate_ref, x_ref) = (
            refs[: len(pieces)], refs[len(pieces) :],
        )
        assemble(piece_refs, x_ref)
        for start in range(0, rows, chunk):
            here = slice(start, start + chunk)
            grad = trans_dot(x_ref[here, :], down_ref[...])
            gating = gating_ref[here, :].astype(f32)
            sigma = sigmoid(gating)
            grad_up_ref[here, :] = (grad * gating * sigma).astype(bf16)
            grad_gate_ref[here, :] = (
                grad * upward_ref[here, :].astype(f32) * dsilu(gating, sigma)
            ).astype(bf16)

    block = pl.BlockSpec((rows, tile), lambda j: (0, j))
    out = jax.ShapeDtypeStruct((rows, units), bf16)
    return call(
        kernel,
        (steps,),
        [whole(p) for p in pieces]
        + [pl.BlockSpec((tile, depth), lambda j: (first + j, 0)), block, block],
        [block] * 2,
        [out] * 2,
        [pltpu.VMEM((rows, depth), bf16)],
        [*pieces, down, upward, gating],
        2 * rows * depth * units,
    )


def tile_base(place, index, size, per_piece):
    piece = lax.bitwise_xor(index // per_piece, place)
    return pl.multiple_of((piece * per_piece + lax.rem(index, per_piece)) * STEP, STEP)


def scan_kernel(count, product, place_ref, *refs):
    piece_refs, refs = refs[:count], refs[count:]
    (input_ref, forget_ref, gate_ref, keep_ref, bound_ref,
     pi_ref, pf_ref, pg_ref, state_ref, decay_ref, x_ref) = refs
    assemble(piece_refs, x_ref)
    x = x_ref[...]
    pi_ref[...] = product(x, input_ref[...])
    pf_ref[...] = product(x, forget_ref[...])
    pg_ref[...] = product(x, gate_ref[...])
    rows, lanes = pi_ref.shape
    per_piece = rows // count // STEP
    place = place_ref[0]
    bound = bound_ref[...]
    row = lax.broadcasted_iota(jnp.int32, (8, lanes), 0)

    def step(index, carry):
        carry_decay, carry_state = carry
        base = tile_base(place, index, count, per_piece)
        here = pl.ds(base, STEP)
        forget = bound + (1.0 - bound) * sigmoid(pf_ref[here, :])
        inp = pi_ref[here, :]
        source = inp * sigmoid(inp) * (1.0 - forget)
        decay = forget * keep_ref[here, :]
        for part in range(STEP // 8):
            a = decay[part * 8 : part * 8 + 8]
            b = source[part * 8 : part * 8 + 8]
            for shift in (1, 2, 4):
                a_before = jnp.where(row >= shift, pltpu.roll(a, shift, 0), 1.0)
                b_before = jnp.where(row >= shift, pltpu.roll(b, shift, 0), 0.0)
                b = a * b_before + b
                a = a * a_before
            b = a * carry_state + b
            a = a * carry_decay
            state_ref[pl.ds(base + part * 8, 8), :] = b
            decay_ref[pl.ds(base + part * 8, 8), :] = a
            carry_decay, carry_state = a[7:8], b[7:8]
        return carry_decay, carry_state

    lax.fori_loop(
        0, rows // STEP, step, (jnp.ones((1, lanes), f32), jnp.zeros((1, lanes), f32))
    )


def back_kernel(count, width, product, place_ref, *refs):
    piece_refs, refs = refs[:count], refs[count:]
    (out_ref, state_ref, gate_ref, pf_ref, inverse_ref, inner_ref, keep_ref, bound_ref, gain_ref,
     adjoint_ref, reach_ref, grad_gate_ref, mix_ref, gain_out_ref, x_ref, mixed_ref) = refs
    assemble(piece_refs, x_ref)
    mixed_ref[...] = product(x_ref[...], out_ref[...])
    rows, lanes = mixed_ref.shape
    per_piece = rows // count // STEP
    place = place_ref[0]
    bound = bound_ref[...]
    gain = gain_ref[...]
    row = lax.broadcasted_iota(jnp.int32, (8, lanes), 0)
    tiles = rows // STEP

    def step(number, carry):
        carry_reach, carry_adjoint, later, gain_sum = carry
        base = tile_base(place, tiles - 1 - number, count, per_piece)
        here = pl.ds(base, STEP)
        grad_mixed = mixed_ref[here, :]
        inverse = inverse_ref[here, :]
        scaled = state_ref[here, :] * inverse
        gate = gate_ref[here, :]
        sigma = sigmoid(gate)
        silu_gate = gate * sigma
        piece = grad_mixed * scaled
        contribution = piece * silu_gate
        grad_gate_ref[here, :] = (piece * gain * dsilu(gate, sigma)).astype(bf16)
        mix_ref[here, :] = (scaled * gain * silu_gate).astype(bf16)
        grad_state = inverse * (
            grad_mixed * gain * silu_gate - scaled * (inner_ref[here, :] * (1.0 / width))
        )
        decay = (bound + (1.0 - bound) * sigmoid(pf_ref[here, :])) * keep_ref[here, :]
        for part in reversed(range(STEP // 8)):
            now = decay[part * 8 : part * 8 + 8]
            gain_sum = gain_sum + contribution[part * 8 : part * 8 + 8]
            a = jnp.where(row == 7, later, pltpu.roll(now, 7, 0))
            b = grad_state[part * 8 : part * 8 + 8]
            for shift in (1, 2, 4):
                a_after = jnp.where(row < 8 - shift, pltpu.roll(a, 8 - shift, 0), 1.0)
                b_after = jnp.where(row < 8 - shift, pltpu.roll(b, 8 - shift, 0), 0.0)
                b = a * b_after + b
                a = a * a_after
            b = a * carry_adjoint + b
            a = a * carry_reach
            adjoint_ref[pl.ds(base + part * 8, 8), :] = b
            reach_ref[pl.ds(base + part * 8, 8), :] = a
            carry_reach, carry_adjoint, later = a[0:1], b[0:1], now[0:1]
        return carry_reach, carry_adjoint, later, gain_sum

    one, zero = jnp.ones((1, lanes), f32), jnp.zeros((1, lanes), f32)
    last = lax.fori_loop(0, tiles, step, (one, zero, one, jnp.zeros((8, lanes), f32)))
    gain_out_ref[...] = jnp.sum(last[3], axis=0, keepdims=True)


def gates_kernel(
    count, place_ref, adjoint_ref, reach_ref, state_ref, pi_ref, pf_ref, keep_ref, bound_ref,
    coming_ref, entering_ref, grad_input_ref, grad_forget_ref, bound_out_ref,
):
    rows, lanes = adjoint_ref.shape
    per_piece = rows // count // STEP
    place = place_ref[0]
    bound = bound_ref[...]
    coming = coming_ref[...]
    row = lax.broadcasted_iota(jnp.int32, (STEP, lanes), 0)

    def step(index, carry):
        before, bound_sum = carry
        base = tile_base(place, index, count, per_piece)
        here = pl.ds(base, STEP)
        adjoint = adjoint_ref[here, :] + reach_ref[here, :] * coming
        state = state_ref[here, :]
        previous = jnp.where(row == 0, before, pltpu.roll(state, 1, 0))
        inp = pi_ref[here, :]
        sigma_input = sigmoid(inp)
        sigma_forget = sigmoid(pf_ref[here, :])
        forget = bound + (1.0 - bound) * sigma_forget
        grad_forget = adjoint * (keep_ref[here, :] * previous - inp * sigma_input)
        piece = grad_forget * (1.0 - sigma_forget)
        grad_input_ref[here, :] = (adjoint * (1.0 - forget) * dsilu(inp, sigma_input)).astype(bf16)
        grad_forget_ref[here, :] = (piece * (1.0 - bound) * sigma_forget).astype(bf16)
        for part in range(STEP // 8):
            bound_sum = bound_sum + piece[part * 8 : part * 8 + 8]
        return state[STEP - 1 : STEP], bound_sum

    last = lax.fori_loop(
        0, rows // STEP, step, (entering_ref[...], jnp.zeros((8, lanes), f32))
    )
    bound_out_ref[...] = jnp.sum(last[1], axis=0, keepdims=True)


def over_channels(kernel, place, pieces, matrices, operands, outs, scratch, channels, cost):
    lanes = min(LANES, channels)

    def part(matrix, at, columns):
        if columns:
            return pl.BlockSpec((matrix.shape[0], lanes), lambda c, p: (0, at // lanes + c))
        return pl.BlockSpec((lanes, matrix.shape[1]), lambda c, p: (at // lanes + c, 0))

    def spec(rows, narrow):
        if narrow:
            return pl.BlockSpec((rows, 1), lambda c, p: (0, 0))
        return pl.BlockSpec((rows, lanes), lambda c, p: (0, c))

    return call(
        kernel,
        (channels // lanes,),
        [whole(p) for p in pieces]
        + [part(*m) for m in matrices]
        + [spec(o.shape[0], o.shape[1] == 1) for o in operands],
        [spec(rows, False) for rows, _ in outs],
        [jax.ShapeDtypeStruct((rows, channels), kind) for rows, kind in outs],
        scratch,
        [*pieces, *(m[0] for m in matrices), *operands],
        cost,
        prefetch=(place,),
    )


def entering_of(decay, state, reverse):
    length = seq_length()
    chips, core = length // 2, lax.axis_index("core")
    own = jnp.concatenate([decay, state], axis=0)
    other = swap(own, "core")
    is_first = core == (1 if reverse else 0)
    first, second = jnp.where(is_first, own, other), jnp.where(is_first, other, own)
    pair = jnp.concatenate(
        [first[0:1] * second[0:1], second[0:1] * first[1:2] + second[1:2]], axis=0
    )
    sign = -1 if reverse else 1
    arrived = [
        lax.ppermute(
            pair,
            SEQ,
            [(i, i + sign * 2 * hop) for i in range(length) if 0 <= i + sign * 2 * hop < length],
        )
        for hop in range(1, chips)
    ]
    total = jnp.zeros_like(state)
    for hop in range(chips - 1, 0, -1):
        total = arrived[hop - 1][0:1] * total + arrived[hop - 1][1:2]
    return jnp.where(is_first, total, other[0:1] * total + other[1:2])


def total_small(rows_of_width, rows_of_channels, first_channel, channels):
    size = lax.axis_size("fsdp")
    place = lax.axis_index("fsdp")

    def columns(step):
        return lax.dynamic_slice_in_dim(
            rows_of_width, lax.bitwise_xor(place, step) * channels, channels, 1
        )

    mine = columns(0)
    for step in range(1, size):
        mine = mine + exchange(columns(step), step)
    mine = jnp.sum(lax.all_gather(jnp.concatenate([mine, rows_of_channels], axis=0), SEQ), axis=0)
    total = jnp.zeros((mine.shape[0], channels * size), f32)
    total = lax.dynamic_update_slice_in_dim(total, mine, first_channel, 1)
    for step in range(1, size):
        total = lax.dynamic_update_slice_in_dim(
            total, exchange(mine, step), lax.bitwise_xor(place, step) * channels, 1
        )
    return total


def local(
    hidden_in, w_input, w_forget, w_gate, w_out, w_up, w_glu, w_down,
    lower_bound, norm_mix, norm_ffn, out_gain, lengths, cotangent,
):
    row_count, model_width = hidden_in.shape
    channels = w_input.shape[2]
    hidden_units = w_up.shape[2]
    size = lax.axis_size("fsdp")
    place = lax.axis_index("fsdp")
    block_rows = row_count * size
    first_channel = place * channels
    place_array = jnp.reshape(place, (1,)).astype(jnp.int32)
    last_layer = LAYERS - 1

    starts = jnp.cumsum(lengths) - lengths
    owners = lax.bitwise_xor(jnp.arange(size, dtype=jnp.int32), place.astype(jnp.int32))
    positions = (
        lax.axis_index(SEQ) * block_rows
        + (owners[:, None] * row_count + jnp.arange(row_count, dtype=jnp.int32)[None, :])
    ).reshape(-1)
    keep = (1.0 - jnp.any(positions[:, None] == starts[None, :], axis=1).astype(f32))[:, None]
    bounds = lax.dynamic_slice_in_dim(lower_bound, first_channel, channels, 1)
    gains = lax.dynamic_slice_in_dim(out_gain, first_channel, channels, 1)

    def side(*shards):
        return lax.all_gather(jnp.concatenate(shards, axis=1), SEQ, axis=0, tiled=True)

    def tall(*shards):
        return lax.all_gather(jnp.concatenate(shards, axis=0), SEQ, axis=1, tiled=True)

    mix_rows = [0] + [3 * channels] * last_layer
    mixes = [side(w_input[0], w_forget[0], w_gate[0])]
    lows, boths = [tall(w_out[0], w_down[0])], []
    for layer in range(LAYERS):
        if layer > 0:
            turned = (w_input[layer].T, w_forget[layer].T, w_gate[layer].T)
            lows.append(tall(*turned, w_out[layer], w_down[layer]))
            mixes.append(lows[layer])
        boths.append(tall(w_up[layer].T, w_glu[layer].T))

    stream = hidden_in.astype(f32)
    saved = []
    for layer in range(LAYERS):
        mix, low, at_out = mixes[layer], lows[layer], mix_rows[layer]
        at_down, first_layer = at_out + channels, layer == 0
        bound, gain = bounds[layer][None, :], gains[layer][None, :]
        unit, factor = rms_parts(stream)
        normed = gather_rows((unit * norm_mix[layer]).astype(bf16))
        if layer == 0:
            grad_y = gather_rows(after(cotangent, *normed))
            normed = all_after(normed, *grad_y)
        proj_input, proj_forget, proj_gate, local_state, local_decay = over_channels(
            functools.partial(scan_kernel, size, dot if first_layer else trans_dot),
            place_array,
            normed,
            [(mix, k * channels, first_layer) for k in range(3)],
            (keep, bound),
            ((block_rows, f32),) * 5,
            [pltpu.VMEM((block_rows, model_width), bf16)],
            channels,
            6 * block_rows * model_width * channels,
        )
        last_row = lax.bitwise_xor(size - 1, place) * row_count + row_count - 1
        entering = entering_of(
            lax.dynamic_slice_in_dim(local_decay, last_row, 1, 0),
            lax.dynamic_slice_in_dim(local_state, last_row, 1, 0),
            False,
        )
        state = local_state + local_decay * entering
        squares = total_rows(jnp.sum(state * state, axis=1))
        inverse = lax.rsqrt(squares / model_width + epsilon)[:, None]
        loose = (state * gain * jax.nn.silu(proj_gate)).astype(bf16)
        parts = cut(dot(loose, low[at_out:at_down]).astype(bf16), size)
        branch = scatter_rows(parts) * inverse[:row_count]
        middle = stream + branch
        unit_two, _ = rms_parts(middle)
        normed_two = (unit_two * norm_ffn[layer]).astype(bf16)
        normed_two = gather_rows(normed_two)
        upward, gating, hidden = up_and_gate(normed_two, boths[layer], hidden_units)
        if layer < last_layer:
            stream = middle + scatter_rows(cut(dot(hidden, low[at_down:]).astype(bf16), size))
        saved.append(
            (factor, normed, proj_input, proj_forget, proj_gate, entering,
             state, inverse, branch, middle, normed_two, upward, gating, hidden, unit)
        )

    grad_x = cotangent.astype(f32)
    shards = [None] * LAYERS
    smalls = [None] * LAYERS
    scattered = {}

    def arrived(*names):
        return tuple(scattered[name] for name in names if name in scattered)

    for layer in reversed(range(LAYERS)):
        mix, low, at_out, both = mixes[layer], lows[layer], mix_rows[layer], boths[layer]
        at_down, first_layer = at_out + channels, layer == 0
        bound, gain = bounds[layer][None, :], gains[layer][None, :]
        (factor, normed, proj_input, proj_forget, proj_gate, entering, state, inverse,
         branch, middle, normed_two, upward, gating, hidden, unit) = saved[layer]
        unit_two, factor_two = rms_parts(middle)

        if layer < last_layer:
            grad_y = gather_rows(grad_x.astype(bf16), *arrived(("ffn", layer + 1)))
        down_part = outer([(hidden, grad_y)])
        down_shard = scatter_columns(down_part)
        grad_up, grad_glu = up_and_gate_back(
            all_after(grad_y, *down_part), low, at_down, upward, gating
        )
        part = dot(jnp.concatenate([grad_up, grad_glu], axis=1), both).astype(bf16)

        def ffn_gradients():
            made = outer([(after(grad_up, part), normed_two), (grad_glu, normed_two)])
            return made, scatter_columns(made)

        grad_normed_two, ffn_shard = scatter_rows(
            cut(part, size), ffn_gradients, *arrived(("low", layer + 1))
        )
        ffn_piece = jnp.sum(grad_normed_two * unit_two, axis=0)
        grad_middle = grad_x + norm_back(grad_normed_two * norm_ffn[layer], unit_two, factor_two)

        grad_m_own = grad_middle.astype(bf16)
        grad_m = gather_rows(grad_m_own, down_shard)
        inner = jnp.concatenate(
            gather_rows(jnp.sum(grad_m_own.astype(f32) * branch, axis=1)), axis=0
        )[:, None]
        adjoint, reach, grad_gate, mixed, gain_piece = over_channels(
            functools.partial(back_kernel, size, model_width, trans_dot),
            place_array,
            grad_m,
            [(low, at_out, False)],
            (state, proj_gate, proj_forget, inverse, inner, keep, bound, gain),
            ((block_rows, f32), (block_rows, f32), (block_rows, bf16), (block_rows, bf16), (1, f32)),
            [pltpu.VMEM((block_rows, model_width), bf16), pltpu.VMEM((block_rows, min(LANES, channels)), f32)],
            channels,
            100 * block_rows * channels,
        )
        first_row = place * row_count
        first_decay = (
            bound
            + (1.0 - bound)
            * jax.nn.sigmoid(lax.dynamic_slice_in_dim(proj_forget, first_row, 1, 0))
        ) * lax.dynamic_slice_in_dim(keep, first_row, 1, 0)
        coming = entering_of(
            first_decay * lax.dynamic_slice_in_dim(reach, first_row, 1, 0),
            first_decay * lax.dynamic_slice_in_dim(adjoint, first_row, 1, 0),
            True,
        )
        grad_input, grad_forget, bound_piece = over_channels(
            functools.partial(gates_kernel, size),
            place_array,
            [],
            [],
            (adjoint, reach, state, proj_input, proj_forget, keep, bound, coming, entering),
            ((block_rows, bf16), (block_rows, bf16), (1, f32)),
            [],
            channels,
            100 * block_rows * channels,
        )
        grad_three = (grad_input, grad_forget, grad_gate)
        joined = jnp.concatenate([grad_input, grad_forget, grad_gate], axis=1)
        part = trans_dot(joined, mix) if first_layer else dot(joined, mix[: 3 * channels])
        part = part.astype(bf16)

        def low_gradients():
            made = outer([(after(joined, part), normed), (mixed, grad_m)])
            return made, scatter_columns(made)

        grad_normed, low_shard = scatter_rows(
            cut(part, size), low_gradients, *((ffn_shard,) if first_layer else ())
        )
        scattered.update({("ffn", layer): ffn_shard, ("low", layer): low_shard})
        mix_piece = jnp.sum(grad_normed * unit, axis=0)
        grad_x = grad_middle + norm_back(grad_normed * norm_mix[layer], unit, factor)

        scattered[layer] = (ffn_shard, down_shard, low_shard)
        smalls[layer] = (mix_piece, ffn_piece, bound_piece, gain_piece)
    middle, hidden = saved[last_layer][9], saved[last_layer][13]
    part = dot(after(hidden, grad_x), lows[-1][mix_rows[-1] + channels :]).astype(bf16)
    hidden_out = (middle + scatter_rows(cut(part, size))).astype(bf16)
    wide_rows = jnp.stack([row for pieces in smalls for row in pieces[:2]])
    own_rows = jnp.concatenate([row for pieces in smalls for row in pieces[2:]], axis=0)
    small = total_small(after(wide_rows, grad_x), own_rows, first_channel, channels)
    for layer in range(LAYERS):
        ffn_shard, down_shard, low_shard = scattered[layer]
        if layer == 0:
            low_shard = after(low_shard, hidden_out)
        shards[layer] = (
            *(low_shard[k * channels : (k + 1) * channels].T for k in range(3)),
            low_shard[3 * channels :],
            ffn_shard[:hidden_units].T,
            ffn_shard[hidden_units:].T,
            down_shard,
        )
    stacked = tuple(
        jnp.stack([shards[layer][member].astype(f32) for layer in range(LAYERS)])
        for member in range(7)
    )
    wide_rows, own_rows = small[: 2 * LAYERS], small[2 * LAYERS :]
    return (
        hidden_out, grad_x, *stacked, own_rows[0::2], wide_rows[0::2], wide_rows[1::2], own_rows[1::2]
    )


def solution(mesh):
    length, size = mesh.devices.shape
    split = Mesh(mesh.devices.reshape(length // 2, 2, size), (*SEQ, "fsdp"))
    rows = P((*SEQ, "fsdp"), None)
    wide = P(None, SEQ, "fsdp")
    tall = P(None, "fsdp", SEQ)
    weights = (wide, wide, wide, tall, wide, wide, tall)
    return jax.shard_map(
        local,
        mesh=split,
        in_specs=(rows, *weights, P(), P(), P(), P(), P(), rows),
        out_specs=(rows, rows, *weights, P(), P(), P(), P()),
        check_vma=False,
    )
```

```python
import functools

import jax
import jax.numpy as jnp
from jax import lax
from jax.experimental import pallas as pl
from jax.experimental.pallas import tpu as pltpu
from jax.sharding import Mesh
from jax.sharding import PartitionSpec as P

LAYERS = 2
epsilon = 1e-06
STEP = 32
LANES = 256
VMEM = 52 * 1024 * 1024
OUTER = 4
SCALE = 5.5
DUE = {
    ("down", 1): (1, "sum"), ("ffn", 1): (0, "gather"), ("low", 1): (0, "part"),
    ("down", 0): (0, "middle"), ("ffn", 0): (0, "last"),
}
f32 = jnp.float32
bf16 = jnp.bfloat16
SEQ = ("chip", "core")
NT = (((1,), (1,)), ((), ()))


def exchange(values, step):
    size = lax.axis_size("fsdp")
    return lax.ppermute(values, "fsdp", [(i, i ^ step) for i in range(size)])


def swap(values, axis):
    return lax.ppermute(values, axis, [(0, 1), (1, 0)])


def seq_length():
    return lax.axis_size("chip") * lax.axis_size("core")


def after(value, *others):
    return lax.optimization_barrier((value, *others))[0]


def all_after(values, *others):
    return list(lax.optimization_barrier((*values, *others)))[: len(values)]


def gather_rows(own, *meanwhile):
    arrived = [exchange(own, step) for step in range(1, lax.axis_size("fsdp"))]
    return [own] + all_after(arrived, *meanwhile)


def scatter_rows(pieces, *meanwhile):
    arrived = [exchange(pieces[step], step) for step in range(1, len(pieces))]
    if meanwhile:
        arrived = all_after(arrived, *meanwhile)
    total = pieces[0].astype(f32)
    for piece in arrived:
        total = total + piece.astype(f32)
    return total


def total_rows(part):
    size = lax.axis_size("fsdp")
    pieces = part.reshape(size, -1)
    total = pieces
    for step in range(1, size):
        other = exchange(pieces, step)
        total = total + jnp.stack([other[k ^ step] for k in range(size)])
    return total.reshape(-1)


def rms_parts(values):
    factor = lax.rsqrt(jnp.mean(values * values, axis=-1, keepdims=True) + epsilon)
    return (values * factor, factor)


def norm_back(grad_unit, unit_rows, factor):
    return factor * (
        grad_unit - unit_rows * jnp.mean(grad_unit * unit_rows, axis=-1, keepdims=True)
    )


def dsilu(values, sigma):
    return sigma * (1.0 + values * (1.0 - sigma))


def sigmoid(values):
    return 1.0 / (1.0 + jnp.exp(-values))


def dot(left, right):
    return jnp.dot(left, right, preferred_element_type=f32)


def trans_dot(left, right):
    return lax.dot_general(left, right, NT, preferred_element_type=f32)


def whole(array):
    return pl.BlockSpec(array.shape, lambda j, *_: (0, 0))


def call(kernel, grid, in_specs, out_specs, out_shape, scratch, operands, cost, prefetch=()):
    return pl.pallas_call(
        kernel,
        grid_spec=pltpu.PrefetchScalarGridSpec(
            num_scalar_prefetch=len(prefetch),
            grid=grid,
            in_specs=in_specs,
            out_specs=out_specs,
            scratch_shapes=scratch,
        ),
        out_shape=out_shape,
        compiler_params=pltpu.CompilerParams(vmem_limit_bytes=VMEM),
        cost_estimate=pl.CostEstimate(flops=int(SCALE * cost), bytes_accessed=cost // 512, transcendentals=0),
    )(*prefetch, *operands)


def assemble(pieces, rows_ref):
    rows = pieces[0].shape[0]

    @pl.when(pl.program_id(0) == 0)
    def _():
        for k, piece in enumerate(pieces):
            rows_ref[k * rows : (k + 1) * rows, :] = piece[...]


def twins(values):
    return [swap(v, "core") for v in values]


def outer(terms):
    lefts = [left for left, _ in terms]
    groups, which = [], []
    for _, pieces in terms:
        found = [k for k, group in enumerate(groups) if group is pieces]
        which.append(found[0] if found else len(groups))
        if not found:
            groups.append(pieces)
    rows, width = sum(p.shape[0] for p in groups[0]), groups[0][0].shape[1] // seq_length()
    heights = [left[0].shape[1] for left in lefts]
    flat = [piece for left in lefts for piece in left]
    total, count, chips = sum(heights), len(groups[0]), lax.axis_size("chip")

    def kernel(core_ref, *refs):
        left_refs, refs = refs[: len(flat)], refs[len(flat) :]
        piece_refs, (out, turned) = refs[: count * len(groups)], refs[count * len(groups) :]

        @pl.when(pl.program_id(0) == 0)
        def _():
            top, at = 0, 0
            for left, height in zip(lefts, heights, strict=True):
                start = 0
                for k, piece in enumerate(left):
                    turned[top : top + height, start : start + piece.shape[0]] = left_refs[at + k][...].T
                    start += piece.shape[0]
                top, at = top + height, at + len(left)

        rights = [
            jnp.concatenate([ref[...] for ref in piece_refs[g * count : (g + 1) * count]], axis=0)
            for g in range(len(groups))
        ]
        top = 0
        for height, group in zip(heights, which, strict=True):
            out[top : top + height, :] = dot(turned[top : top + height, :], rights[group]).astype(bf16)
            top += height

    return call(
        kernel,
        (chips,),
        [whole(left) for left in flat]
        + [
            pl.BlockSpec((p.shape[0], width), lambda j, core: (0, 2 * j + core[0]))
            for group in groups
            for p in group
        ],
        pl.BlockSpec((total, width), lambda j, core: (0, j)),
        jax.ShapeDtypeStruct((total, width * chips), bf16),
        [pltpu.VMEM((total, rows), bf16)],
        [*flat, *(piece for group in groups for piece in group)],
        OUTER * rows * total * width * chips,
        prefetch=(jnp.reshape(lax.axis_index("core"), (1,)).astype(jnp.int32),),
    )


def scatter_columns(part):
    return lax.psum_scatter(part, "chip", scatter_dimension=1, tiled=True)


def cut(values, count):
    rows = values.shape[0] // count
    return [values[k * rows : (k + 1) * rows] for k in range(count)]


def rows_at(matrix, at, rows, tile):
    return (matrix, at // tile) if at % tile == 0 else (matrix[at : at + rows], 0)


def tile_of(units):
    return (128, units // 128) if units % 128 == 0 else (units, 1)


def up_and_gate(pieces, both, units):
    rows, depth = sum(p.shape[0] for p in pieces), pieces[0].shape[1]
    tile, steps = tile_of(units)
    chunk = rows if steps > 1 else rows // 4

    def kernel(*refs):
        piece_refs, (up_ref, gate_ref, upward_ref, gating_ref, hidden_ref, x_ref) = (
            refs[: len(pieces)], refs[len(pieces) :],
        )
        assemble(piece_refs, x_ref)
        for start in range(0, rows, chunk):
            here = slice(start, start + chunk)
            x = x_ref[here, :]
            if steps > 1:
                joined = trans_dot(x, jnp.concatenate([up_ref[...], gate_ref[...]], axis=0))
                upward, gating = joined[:, :tile], joined[:, tile:]
            else:
                upward, gating = trans_dot(x, up_ref[...]), trans_dot(x, gate_ref[...])
            upward_ref[here, :] = upward.astype(bf16)
            gating_ref[here, :] = gating.astype(bf16)
            hidden_ref[here, :] = (gating * sigmoid(gating) * upward).astype(bf16)

    out = jax.ShapeDtypeStruct((rows, units), bf16)
    return call(
        kernel,
        (steps,),
        [whole(p) for p in pieces]
        + [
            pl.BlockSpec((tile, depth), lambda j: (j, 0)),
            pl.BlockSpec((tile, depth), lambda j: (steps + j, 0)),
        ],
        [pl.BlockSpec((rows, tile), lambda j: (0, j))] * 3,
        [out] * 3,
        [pltpu.VMEM((rows, depth), bf16)],
        [*pieces, both, both],
        4 * rows * depth * units,
    )


def up_and_gate_back(pieces, down, at, upward, gating):
    rows, depth = sum(p.shape[0] for p in pieces), pieces[0].shape[1]
    units = upward.shape[1]
    tile, steps = (256, -(-units // 256)) if units % 128 == 0 else (units, 1)
    down, first = rows_at(down, at, units, tile)
    chunk = rows if steps > 1 else rows // 4

    def kernel(*refs):
        piece_refs, (down_ref, upward_ref, gating_ref, grad_up_ref, grad_gate_ref, x_ref) = (
            refs[: len(pieces)], refs[len(pieces) :],
        )
        assemble(piece_refs, x_ref)
        for start in range(0, rows, chunk):
            here = slice(start, start + chunk)
            grad = trans_dot(x_ref[here, :], down_ref[...])
            gating = gating_ref[here, :].astype(f32)
            sigma = sigmoid(gating)
            grad_up_ref[here, :] = (grad * gating * sigma).astype(bf16)
            grad_gate_ref[here, :] = (
                grad * upward_ref[here, :].astype(f32) * dsilu(gating, sigma)
            ).astype(bf16)

    block = pl.BlockSpec((rows, tile), lambda j: (0, j))
    out = jax.ShapeDtypeStruct((rows, units), bf16)
    return call(
        kernel,
        (steps,),
        [whole(p) for p in pieces]
        + [pl.BlockSpec((tile, depth), lambda j: (first + j, 0)), block, block],
        [block] * 2,
        [out] * 2,
        [pltpu.VMEM((rows, depth), bf16)],
        [*pieces, down, upward, gating],
        2 * rows * depth * units,
    )


def tile_base(place, index, size, per_piece):
    piece = lax.bitwise_xor(index // per_piece, place)
    return pl.multiple_of((piece * per_piece + lax.rem(index, per_piece)) * STEP, STEP)


def scan_kernel(count, product, place_ref, *refs):
    piece_refs, refs = refs[:count], refs[count:]
    (input_ref, forget_ref, gate_ref, keep_ref, bound_ref,
     pi_ref, pf_ref, pg_ref, state_ref, decay_ref, x_ref) = refs
    assemble(piece_refs, x_ref)
    x = x_ref[...]
    pi_ref[...] = product(x, input_ref[...])
    pf_ref[...] = product(x, forget_ref[...])
    pg_ref[...] = product(x, gate_ref[...])
    rows, lanes = pi_ref.shape
    per_piece = rows // count // STEP
    place = place_ref[0]
    bound = bound_ref[...]
    row = lax.broadcasted_iota(jnp.int32, (8, lanes), 0)

    def step(index, carry):
        carry_decay, carry_state = carry
        base = tile_base(place, index, count, per_piece)
        here = pl.ds(base, STEP)
        forget = bound + (1.0 - bound) * sigmoid(pf_ref[here, :])
        inp = pi_ref[here, :]
        source = inp * sigmoid(inp) * (1.0 - forget)
        decay = forget * keep_ref[here, :]
        for part in range(STEP // 8):
            a = decay[part * 8 : part * 8 + 8]
            b = source[part * 8 : part * 8 + 8]
            for shift in (1, 2, 4):
                a_before = jnp.where(row >= shift, pltpu.roll(a, shift, 0), 1.0)
                b_before = jnp.where(row >= shift, pltpu.roll(b, shift, 0), 0.0)
                b = a * b_before + b
                a = a * a_before
            b = a * carry_state + b
            a = a * carry_decay
            state_ref[pl.ds(base + part * 8, 8), :] = b
            decay_ref[pl.ds(base + part * 8, 8), :] = a
            carry_decay, carry_state = a[7:8], b[7:8]
        return carry_decay, carry_state

    lax.fori_loop(
        0, rows // STEP, step, (jnp.ones((1, lanes), f32), jnp.zeros((1, lanes), f32))
    )


def back_kernel(count, width, product, place_ref, *refs):
    piece_refs, refs = refs[:count], refs[count:]
    (out_ref, state_ref, gate_ref, pf_ref, inverse_ref, inner_ref, keep_ref, bound_ref, gain_ref,
     adjoint_ref, reach_ref, grad_gate_ref, mix_ref, gain_out_ref, x_ref, mixed_ref) = refs
    assemble(piece_refs, x_ref)
    mixed_ref[...] = product(x_ref[...], out_ref[...])
    rows, lanes = mixed_ref.shape
    per_piece = rows // count // STEP
    place = place_ref[0]
    bound = bound_ref[...]
    gain = gain_ref[...]
    row = lax.broadcasted_iota(jnp.int32, (8, lanes), 0)
    tiles = rows // STEP

    def step(number, carry):
        carry_reach, carry_adjoint, later, gain_sum = carry
        base = tile_base(place, tiles - 1 - number, count, per_piece)
        here = pl.ds(base, STEP)
        grad_mixed = mixed_ref[here, :]
        inverse = inverse_ref[here, :]
        scaled = state_ref[here, :] * inverse
        gate = gate_ref[here, :]
        sigma = sigmoid(gate)
        silu_gate = gate * sigma
        piece = grad_mixed * scaled
        contribution = piece * silu_gate
        grad_gate_ref[here, :] = (piece * gain * dsilu(gate, sigma)).astype(bf16)
        mix_ref[here, :] = (scaled * gain * silu_gate).astype(bf16)
        grad_state = inverse * (
            grad_mixed * gain * silu_gate - scaled * (inner_ref[here, :] * (1.0 / width))
        )
        decay = (bound + (1.0 - bound) * sigmoid(pf_ref[here, :])) * keep_ref[here, :]
        for part in reversed(range(STEP // 8)):
            now = decay[part * 8 : part * 8 + 8]
            gain_sum = gain_sum + contribution[part * 8 : part * 8 + 8]
            a = jnp.where(row == 7, later, pltpu.roll(now, 7, 0))
            b = grad_state[part * 8 : part * 8 + 8]
            for shift in (1, 2, 4):
                a_after = jnp.where(row < 8 - shift, pltpu.roll(a, 8 - shift, 0), 1.0)
                b_after = jnp.where(row < 8 - shift, pltpu.roll(b, 8 - shift, 0), 0.0)
                b = a * b_after + b
                a = a * a_after
            b = a * carry_adjoint + b
            a = a * carry_reach
            adjoint_ref[pl.ds(base + part * 8, 8), :] = b
            reach_ref[pl.ds(base + part * 8, 8), :] = a
            carry_reach, carry_adjoint, later = a[0:1], b[0:1], now[0:1]
        return carry_reach, carry_adjoint, later, gain_sum

    one, zero = jnp.ones((1, lanes), f32), jnp.zeros((1, lanes), f32)
    last = lax.fori_loop(0, tiles, step, (one, zero, one, jnp.zeros((8, lanes), f32)))
    gain_out_ref[...] = jnp.sum(last[3], axis=0, keepdims=True)


def gates_kernel(
    count, place_ref, adjoint_ref, reach_ref, state_ref, pi_ref, pf_ref, keep_ref, bound_ref,
    coming_ref, entering_ref, grad_input_ref, grad_forget_ref, bound_out_ref,
):
    rows, lanes = adjoint_ref.shape
    per_piece = rows // count // STEP
    place = place_ref[0]
    bound = bound_ref[...]
    coming = coming_ref[...]
    row = lax.broadcasted_iota(jnp.int32, (STEP, lanes), 0)

    def step(index, carry):
        before, bound_sum = carry
        base = tile_base(place, index, count, per_piece)
        here = pl.ds(base, STEP)
        adjoint = adjoint_ref[here, :] + reach_ref[here, :] * coming
        state = state_ref[here, :]
        previous = jnp.where(row == 0, before, pltpu.roll(state, 1, 0))
        inp = pi_ref[here, :]
        sigma_input = sigmoid(inp)
        sigma_forget = sigmoid(pf_ref[here, :])
        forget = bound + (1.0 - bound) * sigma_forget
        grad_forget = adjoint * (keep_ref[here, :] * previous - inp * sigma_input)
        piece = grad_forget * (1.0 - sigma_forget)
        grad_input_ref[here, :] = (adjoint * (1.0 - forget) * dsilu(inp, sigma_input)).astype(bf16)
        grad_forget_ref[here, :] = (piece * (1.0 - bound) * sigma_forget).astype(bf16)
        for part in range(STEP // 8):
            bound_sum = bound_sum + piece[part * 8 : part * 8 + 8]
        return state[STEP - 1 : STEP], bound_sum

    last = lax.fori_loop(
        0, rows // STEP, step, (entering_ref[...], jnp.zeros((8, lanes), f32))
    )
    bound_out_ref[...] = jnp.sum(last[1], axis=0, keepdims=True)


def over_channels(kernel, place, pieces, matrices, operands, outs, scratch, channels, cost):
    lanes = min(LANES, channels)

    def part(matrix, at, columns):
        if columns:
            return pl.BlockSpec((matrix.shape[0], lanes), lambda c, p: (0, at // lanes + c))
        return pl.BlockSpec((lanes, matrix.shape[1]), lambda c, p: (at // lanes + c, 0))

    def spec(rows, narrow):
        if narrow:
            return pl.BlockSpec((rows, 1), lambda c, p: (0, 0))
        return pl.BlockSpec((rows, lanes), lambda c, p: (0, c))

    return call(
        kernel,
        (channels // lanes,),
        [whole(p) for p in pieces]
        + [part(*m) for m in matrices]
        + [spec(o.shape[0], o.shape[1] == 1) for o in operands],
        [spec(rows, False) for rows, _ in outs],
        [jax.ShapeDtypeStruct((rows, channels), kind) for rows, kind in outs],
        scratch,
        [*pieces, *(m[0] for m in matrices), *operands],
        cost,
        prefetch=(place,),
    )


def entering_of(decay, state, reverse):
    length = seq_length()
    chips, core = length // 2, lax.axis_index("core")
    own = jnp.concatenate([decay, state], axis=0)
    other = swap(own, "core")
    is_first = core == (1 if reverse else 0)
    first, second = jnp.where(is_first, own, other), jnp.where(is_first, other, own)
    pair = jnp.concatenate(
        [first[0:1] * second[0:1], second[0:1] * first[1:2] + second[1:2]], axis=0
    )
    sign = -1 if reverse else 1
    arrived = [
        lax.ppermute(
            pair,
            SEQ,
            [(i, i + sign * 2 * hop) for i in range(length) if 0 <= i + sign * 2 * hop < length],
        )
        for hop in range(1, chips)
    ]
    total = jnp.zeros_like(state)
    for hop in range(chips - 1, 0, -1):
        total = arrived[hop - 1][0:1] * total + arrived[hop - 1][1:2]
    return jnp.where(is_first, total, other[0:1] * total + other[1:2])


def total_small(rows_of_width, rows_of_channels, first_channel, channels):
    size = lax.axis_size("fsdp")
    place = lax.axis_index("fsdp")

    def columns(step):
        return lax.dynamic_slice_in_dim(
            rows_of_width, lax.bitwise_xor(place, step) * channels, channels, 1
        )

    mine = columns(0)
    for step in range(1, size):
        mine = mine + exchange(columns(step), step)
    mine = jnp.sum(lax.all_gather(jnp.concatenate([mine, rows_of_channels], axis=0), SEQ), axis=0)
    total = jnp.zeros((mine.shape[0], channels * size), f32)
    total = lax.dynamic_update_slice_in_dim(total, mine, first_channel, 1)
    for step in range(1, size):
        total = lax.dynamic_update_slice_in_dim(
            total, exchange(mine, step), lax.bitwise_xor(place, step) * channels, 1
        )
    return total


def local(
    hidden_in, w_input, w_forget, w_gate, w_out, w_up, w_glu, w_down,
    lower_bound, norm_mix, norm_ffn, out_gain, lengths, cotangent,
):
    row_count, model_width = hidden_in.shape
    channels = w_input.shape[2]
    hidden_units = w_up.shape[2]
    size = lax.axis_size("fsdp")
    place = lax.axis_index("fsdp")
    block_rows = row_count * size
    first_channel = place * channels
    place_array = jnp.reshape(place, (1,)).astype(jnp.int32)
    last_layer = LAYERS - 1

    starts = jnp.cumsum(lengths) - lengths
    owners = lax.bitwise_xor(jnp.arange(size, dtype=jnp.int32), place.astype(jnp.int32))
    positions = (
        lax.axis_index(SEQ) * block_rows
        + (owners[:, None] * row_count + jnp.arange(row_count, dtype=jnp.int32)[None, :])
    ).reshape(-1)
    keep = (1.0 - jnp.any(positions[:, None] == starts[None, :], axis=1).astype(f32))[:, None]
    bounds = lax.dynamic_slice_in_dim(lower_bound, first_channel, channels, 1)
    gains = lax.dynamic_slice_in_dim(out_gain, first_channel, channels, 1)

    def side(*shards):
        return lax.all_gather(jnp.concatenate(shards, axis=1), SEQ, axis=0, tiled=True)

    def tall(*shards):
        return lax.all_gather(jnp.concatenate(shards, axis=0), SEQ, axis=1, tiled=True)

    first_mix = side(w_input[0], w_forget[0], w_gate[0])
    joined = tall(w_out[0], w_down[0])
    mixes, outs, boths, downs = [first_mix], [(joined, 0)], [], [(joined, channels)]
    for layer in range(LAYERS):
        if layer > 0:
            joined = tall(w_input[layer].T, w_forget[layer].T, w_gate[layer].T, w_out[layer])
            mixes.append(joined)
            outs.append((joined, 3 * channels))
        boths.append(tall(w_up[layer].T, w_glu[layer].T))
        if layer > 0:
            downs.append((tall(w_down[layer]), 0))

    def rows_of(matrix_at, rows):
        matrix, at = matrix_at
        return matrix[at : at + rows]

    stream = hidden_in.astype(f32)
    saved = []
    for layer in range(LAYERS):
        mix, first_layer = mixes[layer], layer == 0
        bound, gain = bounds[layer][None, :], gains[layer][None, :]
        unit, factor = rms_parts(stream)
        normed = gather_rows((unit * norm_mix[layer]).astype(bf16))
        if layer == 0:
            grad_y = gather_rows(after(cotangent, *normed))
        proj_input, proj_forget, proj_gate, local_state, local_decay = over_channels(
            functools.partial(scan_kernel, size, dot if first_layer else trans_dot),
            place_array,
            normed,
            [(mix, k * channels, first_layer) for k in range(3)],
            (keep, bound),
            ((block_rows, f32),) * 5,
            [pltpu.VMEM((block_rows, model_width), bf16)],
            channels,
            6 * block_rows * model_width * channels,
        )
        if layer == 0:
            local_state, local_decay = all_after((local_state, local_decay), *grad_y)
        last_row = lax.bitwise_xor(size - 1, place) * row_count + row_count - 1
        entering = entering_of(
            lax.dynamic_slice_in_dim(local_decay, last_row, 1, 0),
            lax.dynamic_slice_in_dim(local_state, last_row, 1, 0),
            False,
        )
        state = local_state + local_decay * entering
        squares = total_rows(jnp.sum(state * state, axis=1))
        inverse = lax.rsqrt(squares / model_width + epsilon)[:, None]
        loose = (state * gain * jax.nn.silu(proj_gate)).astype(bf16)
        parts = cut(dot(loose, rows_of(outs[layer], channels)).astype(bf16), size)
        branch = scatter_rows(parts) * inverse[:row_count]
        middle = stream + branch
        unit_two, _ = rms_parts(middle)
        normed_two = (unit_two * norm_ffn[layer]).astype(bf16)
        normed_two = gather_rows(normed_two)
        upward, gating, hidden = up_and_gate(normed_two, boths[layer], hidden_units)
        if layer < last_layer:
            stream = middle + scatter_rows(cut(dot(hidden, rows_of(downs[layer], hidden_units)).astype(bf16), size))
        twin_rows = (twins(normed), twins(normed_two), twins([hidden]))
        saved.append(
            (factor, twin_rows, normed, proj_input, proj_forget, proj_gate, entering,
             state, inverse, branch, middle, normed_two, upward, gating, hidden, unit)
        )

    grad_x = cotangent.astype(f32)
    shards = [None] * LAYERS
    smalls = [None] * LAYERS
    scattered = {}

    def due(layer, place):
        names = [name for name, when in DUE.items() if when == (layer, place)]
        return tuple(scattered[name] for name in names if name in scattered)

    final_middle, final_hidden = saved[last_layer][10], saved[last_layer][14]
    for layer in reversed(range(LAYERS)):
        mix, both, first_layer = mixes[layer], boths[layer], layer == 0
        bound, gain = bounds[layer][None, :], gains[layer][None, :]
        (factor, twin_rows, normed, proj_input, proj_forget, proj_gate, entering, state, inverse,
         branch, middle, normed_two, upward, gating, hidden, unit) = saved[layer]
        unit_two, factor_two = rms_parts(middle)
        all_normed, all_two = normed + twin_rows[0], normed_two + twin_rows[1]

        if layer < last_layer:
            grad_y = gather_rows(grad_x.astype(bf16), *due(layer, "gather"))
        down_part = outer([([hidden, *twin_rows[2]], grad_y + twins(grad_y))])
        down_shard = scattered["down", layer] = scatter_columns(down_part)
        grad_up, grad_glu = up_and_gate_back(
            all_after(grad_y, down_part), *downs[layer], upward, gating
        )
        twin_up, twin_glu = twins((grad_up, grad_glu))
        grad_up, grad_glu = all_after((grad_up, grad_glu), *due(layer, "part"))
        part = dot(jnp.concatenate([grad_up, grad_glu], axis=1), both).astype(bf16)
        *parts, ready = all_after((*cut(part, size), grad_up))
        ffn_part = outer([([ready, twin_up], all_two), ([grad_glu, twin_glu], all_two)])
        ffn_shard = scattered["ffn", layer] = scatter_columns(ffn_part)
        grad_normed_two = scatter_rows(parts, ffn_part, *due(layer, "sum"))
        ffn_piece = jnp.sum(grad_normed_two * unit_two, axis=0)
        grad_middle = grad_x + norm_back(grad_normed_two * norm_ffn[layer], unit_two, factor_two)

        grad_m_own = grad_middle.astype(bf16)
        grad_m_own = after(grad_m_own, *due(layer, "norm"))
        grad_m = gather_rows(grad_m_own, *due(layer, "middle"))
        inner = jnp.concatenate(
            gather_rows(jnp.sum(grad_m_own.astype(f32) * branch, axis=1)), axis=0
        )[:, None]
        adjoint, reach, grad_gate, mixed, gain_piece = over_channels(
            functools.partial(back_kernel, size, model_width, trans_dot),
            place_array,
            grad_m,
            [(*outs[layer], False)],
            (state, proj_gate, proj_forget, inverse, inner, keep, bound, gain),
            ((block_rows, f32), (block_rows, f32), (block_rows, bf16), (block_rows, bf16), (1, f32)),
            [pltpu.VMEM((block_rows, model_width), bf16), pltpu.VMEM((block_rows, min(LANES, channels)), f32)],
            channels,
            100 * block_rows * channels,
        )
        all_m, twin_mixed = grad_m + twins(grad_m), twins([mixed])
        first_row = place * row_count
        first_decay = (
            bound
            + (1.0 - bound)
            * jax.nn.sigmoid(lax.dynamic_slice_in_dim(proj_forget, first_row, 1, 0))
        ) * lax.dynamic_slice_in_dim(keep, first_row, 1, 0)
        coming = entering_of(
            first_decay * lax.dynamic_slice_in_dim(reach, first_row, 1, 0),
            first_decay * lax.dynamic_slice_in_dim(adjoint, first_row, 1, 0),
            True,
        )
        ready = [*all_m, *twin_mixed, *due(layer, "coming")]
        if first_layer:
            output = dot(after(final_hidden, adjoint), rows_of(downs[last_layer], hidden_units)).astype(bf16)
            hidden_out = (final_middle + scatter_rows(cut(output, size))).astype(bf16)
            ready.append(output)
        coming = after(coming, *ready)
        grad_input, grad_forget, bound_piece = over_channels(
            functools.partial(gates_kernel, size),
            place_array,
            [],
            [],
            (adjoint, reach, state, proj_input, proj_forget, keep, bound, coming, entering),
            ((block_rows, bf16), (block_rows, bf16), (1, f32)),
            [],
            channels,
            100 * block_rows * channels,
        )
        grad_three = (grad_input, grad_forget, grad_gate)
        joined = jnp.concatenate([grad_input, grad_forget, grad_gate], axis=1)
        (twin_joined,) = twins((joined,))
        if first_layer:
            low_part = outer([([joined, twin_joined], all_normed), ([mixed, *twin_mixed], all_m)])
            part = trans_dot(after(joined, low_part), mix)
        else:
            part = dot(joined, mix[: 3 * channels])
        part = part.astype(bf16)

        if first_layer:
            parts = cut(part, size)
        else:
            *parts, ready = all_after((*cut(part, size), joined))
            low_part = outer([([ready, twin_joined], all_normed), ([mixed, *twin_mixed], all_m)])
        low_shard = scattered["low", layer] = scatter_columns(low_part)
        grad_normed = scatter_rows(parts, low_part, *due(layer, "last"))
        mix_piece = jnp.sum(grad_normed * unit, axis=0)
        grad_x = grad_middle + norm_back(grad_normed * norm_mix[layer], unit, factor)

        smalls[layer] = (mix_piece, ffn_piece, bound_piece, gain_piece)
    wide_rows = jnp.stack([row for pieces in smalls for row in pieces[:2]])
    own_rows = jnp.concatenate([row for pieces in smalls for row in pieces[2:]], axis=0)
    small = total_small(after(wide_rows, grad_x, *due(0, "after")), own_rows, first_channel, channels)
    for layer in range(LAYERS):
        ffn_shard, down_shard, low_shard = (scattered[name, layer] for name in ("ffn", "down", "low"))
        if layer == 0:
            low_shard = after(low_shard, small)
        shards[layer] = (
            *(low_shard[k * channels : (k + 1) * channels].T for k in range(3)),
            low_shard[3 * channels :],
            ffn_shard[:hidden_units].T,
            ffn_shard[hidden_units:].T,
            down_shard,
        )
    stacked = tuple(
        jnp.stack([shards[layer][member].astype(f32) for layer in range(LAYERS)])
        for member in range(7)
    )
    wide_rows, own_rows = small[: 2 * LAYERS], small[2 * LAYERS :]
    return (
        hidden_out, grad_x, *stacked, own_rows[0::2], wide_rows[0::2], wide_rows[1::2], own_rows[1::2]
    )


def solution(mesh):
    length, size = mesh.devices.shape
    split = Mesh(mesh.devices.reshape(length // 2, 2, size), (*SEQ, "fsdp"))
    rows = P((*SEQ, "fsdp"), None)
    wide = P(None, SEQ, "fsdp")
    tall = P(None, "fsdp", SEQ)
    weights = (wide, wide, wide, tall, wide, wide, tall)
    return jax.shard_map(
        local,
        mesh=split,
        in_specs=(rows, *weights, P(), P(), P(), P(), P(), rows),
        out_specs=(rows, rows, *weights, P(), P(), P(), P()),
        check_vma=False,
    )
```

```python
import functools

import jax
import jax.numpy as jnp
from jax import lax
from jax.experimental import pallas as pl
from jax.experimental.pallas import tpu as pltpu
from jax.sharding import Mesh
from jax.sharding import PartitionSpec as P

LAYERS = 2
epsilon = 1e-06
STEP = 32
LANES = 256
VMEM = 52 * 1024 * 1024
OUTER = 4
SCALE = 5.5
DUE = {
    ("down", 1): (1, "sum"), ("ffn", 1): (0, "gather"), ("low", 1): (0, "part"),
    ("down", 0): (0, "middle"), ("ffn", 0): (0, "last"),
}
f32 = jnp.float32
bf16 = jnp.bfloat16
SEQ = ("chip", "core")
NT = (((1,), (1,)), ((), ()))


def exchange(values, step):
    size = lax.axis_size("fsdp")
    return lax.ppermute(values, "fsdp", [(i, i ^ step) for i in range(size)])


def swap(values, axis):
    return lax.ppermute(values, axis, [(0, 1), (1, 0)])


def seq_length():
    return lax.axis_size("chip") * lax.axis_size("core")


def after(value, *others):
    return lax.optimization_barrier((value, *others))[0]


def all_after(values, *others):
    return list(lax.optimization_barrier((*values, *others)))[: len(values)]


def gather_rows(own, *meanwhile):
    arrived = [exchange(own, step) for step in range(1, lax.axis_size("fsdp"))]
    return [own] + all_after(arrived, *meanwhile)


def scatter_rows(pieces, *meanwhile):
    arrived = [exchange(pieces[step], step) for step in range(1, len(pieces))]
    if meanwhile:
        arrived = all_after(arrived, *meanwhile)
    total = pieces[0].astype(f32)
    for piece in arrived:
        total = total + piece.astype(f32)
    return total


def total_rows(part):
    size = lax.axis_size("fsdp")
    pieces = part.reshape(size, -1)
    total = pieces
    for step in range(1, size):
        other = exchange(pieces, step)
        total = total + jnp.stack([other[k ^ step] for k in range(size)])
    return total.reshape(-1)


def rms_parts(values):
    factor = lax.rsqrt(jnp.mean(values * values, axis=-1, keepdims=True) + epsilon)
    return (values * factor, factor)


def norm_back(grad_unit, unit_rows, factor):
    return factor * (
        grad_unit - unit_rows * jnp.mean(grad_unit * unit_rows, axis=-1, keepdims=True)
    )


def dsilu(values, sigma):
    return sigma * (1.0 + values * (1.0 - sigma))


def sigmoid(values):
    return 1.0 / (1.0 + jnp.exp(-values))


def dot(left, right):
    return jnp.dot(left, right, preferred_element_type=f32)


def trans_dot(left, right):
    return lax.dot_general(left, right, NT, preferred_element_type=f32)


def whole(array):
    return pl.BlockSpec(array.shape, lambda j, *_: (0, 0))


def call(kernel, grid, in_specs, out_specs, out_shape, scratch, operands, cost, prefetch=()):
    return pl.pallas_call(
        kernel,
        grid_spec=pltpu.PrefetchScalarGridSpec(
            num_scalar_prefetch=len(prefetch),
            grid=grid,
            in_specs=in_specs,
            out_specs=out_specs,
            scratch_shapes=scratch,
        ),
        out_shape=out_shape,
        compiler_params=pltpu.CompilerParams(vmem_limit_bytes=VMEM),
        cost_estimate=pl.CostEstimate(flops=int(SCALE * cost), bytes_accessed=cost // 512, transcendentals=0),
    )(*prefetch, *operands)


def assemble(pieces, rows_ref):
    rows = pieces[0].shape[0]

    @pl.when(pl.program_id(0) == 0)
    def _():
        for k, piece in enumerate(pieces):
            rows_ref[k * rows : (k + 1) * rows, :] = piece[...]


def twins(values):
    return [swap(v, "core") for v in values]


def outer(terms):
    lefts = [left for left, _ in terms]
    groups, which = [], []
    for _, pieces in terms:
        found = [k for k, group in enumerate(groups) if group is pieces]
        which.append(found[0] if found else len(groups))
        if not found:
            groups.append(pieces)
    rows, width = sum(p.shape[0] for p in groups[0]), groups[0][0].shape[1] // seq_length()
    heights = [left[0].shape[1] for left in lefts]
    flat = [piece for left in lefts for piece in left]
    total, count, chips = sum(heights), len(groups[0]), lax.axis_size("chip")

    def kernel(core_ref, *refs):
        left_refs, refs = refs[: len(flat)], refs[len(flat) :]
        piece_refs, (out, turned) = refs[: count * len(groups)], refs[count * len(groups) :]

        @pl.when(pl.program_id(0) == 0)
        def _():
            top, at = 0, 0
            for left, height in zip(lefts, heights, strict=True):
                start = 0
                for k, piece in enumerate(left):
                    turned[top : top + height, start : start + piece.shape[0]] = left_refs[at + k][...].T
                    start += piece.shape[0]
                top, at = top + height, at + len(left)

        rights = [
            jnp.concatenate([ref[...] for ref in piece_refs[g * count : (g + 1) * count]], axis=0)
            for g in range(len(groups))
        ]
        top = 0
        for height, group in zip(heights, which, strict=True):
            out[top : top + height, :] = dot(turned[top : top + height, :], rights[group]).astype(bf16)
            top += height

    return call(
        kernel,
        (chips,),
        [whole(left) for left in flat]
        + [
            pl.BlockSpec((p.shape[0], width), lambda j, core: (0, 2 * j + core[0]))
            for group in groups
            for p in group
        ],
        pl.BlockSpec((total, width), lambda j, core: (0, j)),
        jax.ShapeDtypeStruct((total, width * chips), bf16),
        [pltpu.VMEM((total, rows), bf16)],
        [*flat, *(piece for group in groups for piece in group)],
        OUTER * rows * total * width * chips,
        prefetch=(jnp.reshape(lax.axis_index("core"), (1,)).astype(jnp.int32),),
    )


def scatter_columns(part):
    return lax.psum_scatter(part, "chip", scatter_dimension=1, tiled=True)


def cut(values, count):
    rows = values.shape[0] // count
    return [values[k * rows : (k + 1) * rows] for k in range(count)]


def rows_at(matrix, at, rows, tile):
    return (matrix, at // tile) if at % tile == 0 else (matrix[at : at + rows], 0)


def tile_of(units):
    return (128, units // 128) if units % 128 == 0 else (units, 1)


def up_and_gate(pieces, both, units):
    rows, depth = sum(p.shape[0] for p in pieces), pieces[0].shape[1]
    tile, steps = tile_of(units)
    chunk = rows if steps > 1 else rows // 4

    def kernel(*refs):
        piece_refs, (up_ref, gate_ref, upward_ref, gating_ref, hidden_ref, x_ref) = (
            refs[: len(pieces)], refs[len(pieces) :],
        )
        assemble(piece_refs, x_ref)
        for start in range(0, rows, chunk):
            here = slice(start, start + chunk)
            x = x_ref[here, :]
            if steps > 1:
                joined = trans_dot(x, jnp.concatenate([up_ref[...], gate_ref[...]], axis=0))
                upward, gating = joined[:, :tile], joined[:, tile:]
            else:
                upward, gating = trans_dot(x, up_ref[...]), trans_dot(x, gate_ref[...])
            upward_ref[here, :] = upward.astype(bf16)
            gating_ref[here, :] = gating.astype(bf16)
            hidden_ref[here, :] = (gating * sigmoid(gating) * upward).astype(bf16)

    out = jax.ShapeDtypeStruct((rows, units), bf16)
    return call(
        kernel,
        (steps,),
        [whole(p) for p in pieces]
        + [
            pl.BlockSpec((tile, depth), lambda j: (j, 0)),
            pl.BlockSpec((tile, depth), lambda j: (steps + j, 0)),
        ],
        [pl.BlockSpec((rows, tile), lambda j: (0, j))] * 3,
        [out] * 3,
        [pltpu.VMEM((rows, depth), bf16)],
        [*pieces, both, both],
        4 * rows * depth * units,
    )


def up_and_gate_back(pieces, down, at, upward, gating):
    rows, depth = sum(p.shape[0] for p in pieces), pieces[0].shape[1]
    units = upward.shape[1]
    tile, steps = (256, -(-units // 256)) if units % 128 == 0 else (units, 1)
    down, first = rows_at(down, at, units, tile)
    chunk = rows if steps > 1 else rows // 4

    def kernel(*refs):
        piece_refs, (down_ref, upward_ref, gating_ref, grad_up_ref, grad_gate_ref, x_ref) = (
            refs[: len(pieces)], refs[len(pieces) :],
        )
        assemble(piece_refs, x_ref)
        for start in range(0, rows, chunk):
            here = slice(start, start + chunk)
            grad = trans_dot(x_ref[here, :], down_ref[...])
            gating = gating_ref[here, :].astype(f32)
            sigma = sigmoid(gating)
            grad_up_ref[here, :] = (grad * gating * sigma).astype(bf16)
            grad_gate_ref[here, :] = (
                grad * upward_ref[here, :].astype(f32) * dsilu(gating, sigma)
            ).astype(bf16)

    block = pl.BlockSpec((rows, tile), lambda j: (0, j))
    out = jax.ShapeDtypeStruct((rows, units), bf16)
    return call(
        kernel,
        (steps,),
        [whole(p) for p in pieces]
        + [pl.BlockSpec((tile, depth), lambda j: (first + j, 0)), block, block],
        [block] * 2,
        [out] * 2,
        [pltpu.VMEM((rows, depth), bf16)],
        [*pieces, down, upward, gating],
        2 * rows * depth * units,
    )


def tile_base(place, index, size, per_piece):
    piece = lax.bitwise_xor(index // per_piece, place)
    return pl.multiple_of((piece * per_piece + lax.rem(index, per_piece)) * STEP, STEP)


def scan_kernel(count, product, place_ref, *refs):
    piece_refs, refs = refs[:count], refs[count:]
    (input_ref, forget_ref, gate_ref, keep_ref, bound_ref,
     pi_ref, pf_ref, pg_ref, state_ref, decay_ref, x_ref) = refs
    assemble(piece_refs, x_ref)
    x = x_ref[...]
    pi_ref[...] = product(x, input_ref[...])
    pf_ref[...] = product(x, forget_ref[...])
    pg_ref[...] = product(x, gate_ref[...])
    rows, lanes = pi_ref.shape
    per_piece = rows // count // STEP
    place = place_ref[0]
    bound = bound_ref[...]
    row = lax.broadcasted_iota(jnp.int32, (8, lanes), 0)

    def step(index, carry):
        carry_decay, carry_state = carry
        base = tile_base(place, index, count, per_piece)
        here = pl.ds(base, STEP)
        forget = bound + (1.0 - bound) * sigmoid(pf_ref[here, :])
        inp = pi_ref[here, :]
        source = inp * sigmoid(inp) * (1.0 - forget)
        decay = forget * keep_ref[here, :]
        for part in range(STEP // 8):
            a = decay[part * 8 : part * 8 + 8]
            b = source[part * 8 : part * 8 + 8]
            for shift in (1, 2, 4):
                a_before = jnp.where(row >= shift, pltpu.roll(a, shift, 0), 1.0)
                b_before = jnp.where(row >= shift, pltpu.roll(b, shift, 0), 0.0)
                b = a * b_before + b
                a = a * a_before
            b = a * carry_state + b
            a = a * carry_decay
            state_ref[pl.ds(base + part * 8, 8), :] = b
            decay_ref[pl.ds(base + part * 8, 8), :] = a
            carry_decay, carry_state = a[7:8], b[7:8]
        return carry_decay, carry_state

    lax.fori_loop(
        0, rows // STEP, step, (jnp.ones((1, lanes), f32), jnp.zeros((1, lanes), f32))
    )


def back_kernel(count, width, product, place_ref, *refs):
    piece_refs, refs = refs[:count], refs[count:]
    (out_ref, state_ref, gate_ref, pf_ref, inverse_ref, inner_ref, keep_ref, bound_ref, gain_ref,
     adjoint_ref, reach_ref, grad_gate_ref, mix_ref, gain_out_ref, x_ref, mixed_ref) = refs
    assemble(piece_refs, x_ref)
    mixed_ref[...] = product(x_ref[...], out_ref[...])
    rows, lanes = mixed_ref.shape
    per_piece = rows // count // STEP
    place = place_ref[0]
    bound = bound_ref[...]
    gain = gain_ref[...]
    row = lax.broadcasted_iota(jnp.int32, (8, lanes), 0)
    tiles = rows // STEP

    def step(number, carry):
        carry_reach, carry_adjoint, later, gain_sum = carry
        base = tile_base(place, tiles - 1 - number, count, per_piece)
        here = pl.ds(base, STEP)
        grad_mixed = mixed_ref[here, :]
        inverse = inverse_ref[here, :]
        scaled = state_ref[here, :] * inverse
        gate = gate_ref[here, :]
        sigma = sigmoid(gate)
        silu_gate = gate * sigma
        piece = grad_mixed * scaled
        contribution = piece * silu_gate
        grad_gate_ref[here, :] = (piece * gain * dsilu(gate, sigma)).astype(bf16)
        mix_ref[here, :] = (scaled * gain * silu_gate).astype(bf16)
        grad_state = inverse * (
            grad_mixed * gain * silu_gate - scaled * (inner_ref[here, :] * (1.0 / width))
        )
        decay = (bound + (1.0 - bound) * sigmoid(pf_ref[here, :])) * keep_ref[here, :]
        for part in reversed(range(STEP // 8)):
            now = decay[part * 8 : part * 8 + 8]
            gain_sum = gain_sum + contribution[part * 8 : part * 8 + 8]
            a = jnp.where(row == 7, later, pltpu.roll(now, 7, 0))
            b = grad_state[part * 8 : part * 8 + 8]
            for shift in (1, 2, 4):
                a_after = jnp.where(row < 8 - shift, pltpu.roll(a, 8 - shift, 0), 1.0)
                b_after = jnp.where(row < 8 - shift, pltpu.roll(b, 8 - shift, 0), 0.0)
                b = a * b_after + b
                a = a * a_after
            b = a * carry_adjoint + b
            a = a * carry_reach
            adjoint_ref[pl.ds(base + part * 8, 8), :] = b
            reach_ref[pl.ds(base + part * 8, 8), :] = a
            carry_reach, carry_adjoint, later = a[0:1], b[0:1], now[0:1]
        return carry_reach, carry_adjoint, later, gain_sum

    one, zero = jnp.ones((1, lanes), f32), jnp.zeros((1, lanes), f32)
    last = lax.fori_loop(0, tiles, step, (one, zero, one, jnp.zeros((8, lanes), f32)))
    gain_out_ref[...] = jnp.sum(last[3], axis=0, keepdims=True)


def gates_kernel(
    count, place_ref, adjoint_ref, reach_ref, state_ref, pi_ref, pf_ref, keep_ref, bound_ref,
    coming_ref, entering_ref, grad_input_ref, grad_forget_ref, bound_out_ref,
):
    rows, lanes = adjoint_ref.shape
    per_piece = rows // count // STEP
    place = place_ref[0]
    bound = bound_ref[...]
    coming = coming_ref[...]
    row = lax.broadcasted_iota(jnp.int32, (STEP, lanes), 0)

    def step(index, carry):
        before, bound_sum = carry
        base = tile_base(place, index, count, per_piece)
        here = pl.ds(base, STEP)
        adjoint = adjoint_ref[here, :] + reach_ref[here, :] * coming
        state = state_ref[here, :]
        previous = jnp.where(row == 0, before, pltpu.roll(state, 1, 0))
        inp = pi_ref[here, :]
        sigma_input = sigmoid(inp)
        sigma_forget = sigmoid(pf_ref[here, :])
        forget = bound + (1.0 - bound) * sigma_forget
        grad_forget = adjoint * (keep_ref[here, :] * previous - inp * sigma_input)
        piece = grad_forget * (1.0 - sigma_forget)
        grad_input_ref[here, :] = (adjoint * (1.0 - forget) * dsilu(inp, sigma_input)).astype(bf16)
        grad_forget_ref[here, :] = (piece * (1.0 - bound) * sigma_forget).astype(bf16)
        for part in range(STEP // 8):
            bound_sum = bound_sum + piece[part * 8 : part * 8 + 8]
        return state[STEP - 1 : STEP], bound_sum

    last = lax.fori_loop(
        0, rows // STEP, step, (entering_ref[...], jnp.zeros((8, lanes), f32))
    )
    bound_out_ref[...] = jnp.sum(last[1], axis=0, keepdims=True)


def over_channels(kernel, place, pieces, matrices, operands, outs, scratch, channels, cost):
    lanes = min(LANES, channels)

    def part(matrix, at, columns):
        if columns:
            return pl.BlockSpec((matrix.shape[0], lanes), lambda c, p: (0, at // lanes + c))
        return pl.BlockSpec((lanes, matrix.shape[1]), lambda c, p: (at // lanes + c, 0))

    def spec(rows, narrow):
        if narrow:
            return pl.BlockSpec((rows, 1), lambda c, p: (0, 0))
        return pl.BlockSpec((rows, lanes), lambda c, p: (0, c))

    return call(
        kernel,
        (channels // lanes,),
        [whole(p) for p in pieces]
        + [part(*m) for m in matrices]
        + [spec(o.shape[0], o.shape[1] == 1) for o in operands],
        [spec(rows, False) for rows, _ in outs],
        [jax.ShapeDtypeStruct((rows, channels), kind) for rows, kind in outs],
        scratch,
        [*pieces, *(m[0] for m in matrices), *operands],
        cost,
        prefetch=(place,),
    )


def entering_of(decay, state, reverse):
    length = seq_length()
    chips, core = length // 2, lax.axis_index("core")
    own = jnp.concatenate([decay, state], axis=0)
    other = swap(own, "core")
    is_first = core == (1 if reverse else 0)
    first, second = jnp.where(is_first, own, other), jnp.where(is_first, other, own)
    pair = jnp.concatenate(
        [first[0:1] * second[0:1], second[0:1] * first[1:2] + second[1:2]], axis=0
    )
    sign = -1 if reverse else 1
    arrived = [
        lax.ppermute(
            pair,
            SEQ,
            [(i, i + sign * 2 * hop) for i in range(length) if 0 <= i + sign * 2 * hop < length],
        )
        for hop in range(1, chips)
    ]
    total = jnp.zeros_like(state)
    for hop in range(chips - 1, 0, -1):
        total = arrived[hop - 1][0:1] * total + arrived[hop - 1][1:2]
    return jnp.where(is_first, total, other[0:1] * total + other[1:2])


def total_small(rows_of_width, rows_of_channels, first_channel, channels):
    size = lax.axis_size("fsdp")
    place = lax.axis_index("fsdp")

    def columns(step):
        return lax.dynamic_slice_in_dim(
            rows_of_width, lax.bitwise_xor(place, step) * channels, channels, 1
        )

    mine = columns(0)
    for step in range(1, size):
        mine = mine + exchange(columns(step), step)
    mine = jnp.sum(lax.all_gather(jnp.concatenate([mine, rows_of_channels], axis=0), SEQ), axis=0)
    total = jnp.zeros((mine.shape[0], channels * size), f32)
    total = lax.dynamic_update_slice_in_dim(total, mine, first_channel, 1)
    for step in range(1, size):
        total = lax.dynamic_update_slice_in_dim(
            total, exchange(mine, step), lax.bitwise_xor(place, step) * channels, 1
        )
    return total


def local(
    hidden_in, w_input, w_forget, w_gate, w_out, w_up, w_glu, w_down,
    lower_bound, norm_mix, norm_ffn, out_gain, lengths, cotangent,
):
    row_count, model_width = hidden_in.shape
    channels = w_input.shape[2]
    hidden_units = w_up.shape[2]
    size = lax.axis_size("fsdp")
    place = lax.axis_index("fsdp")
    block_rows = row_count * size
    first_channel = place * channels
    place_array = jnp.reshape(place, (1,)).astype(jnp.int32)
    last_layer = LAYERS - 1

    starts = jnp.cumsum(lengths) - lengths
    owners = lax.bitwise_xor(jnp.arange(size, dtype=jnp.int32), place.astype(jnp.int32))
    positions = (
        lax.axis_index(SEQ) * block_rows
        + (owners[:, None] * row_count + jnp.arange(row_count, dtype=jnp.int32)[None, :])
    ).reshape(-1)
    keep = (1.0 - jnp.any(positions[:, None] == starts[None, :], axis=1).astype(f32))[:, None]
    bounds = lax.dynamic_slice_in_dim(lower_bound, first_channel, channels, 1)
    gains = lax.dynamic_slice_in_dim(out_gain, first_channel, channels, 1)

    def side(*shards):
        return lax.all_gather(jnp.concatenate(shards, axis=1), SEQ, axis=0, tiled=True)

    def tall(*shards):
        return lax.all_gather(jnp.concatenate(shards, axis=0), SEQ, axis=1, tiled=True)

    mixes, boths, downs = [side(w_input[0], w_forget[0], w_gate[0], w_out[0].T)], [], []
    for layer in range(LAYERS):
        if layer > 0:
            mixes.append(tall(w_input[layer].T, w_forget[layer].T, w_gate[layer].T, w_out[layer]))
        if layer < last_layer:
            joined = tall(w_up[layer].T, w_glu[layer].T, w_down[layer])
            boths.append((joined, 0))
            downs.append((joined, 2 * hidden_units))
        else:
            boths.append((tall(w_up[layer].T, w_glu[layer].T), 0))
            downs.append((tall(w_down[layer]), 0))

    def rows_of(matrix_at, rows):
        matrix, at = matrix_at
        return matrix[at : at + rows]

    stream = hidden_in.astype(f32)
    saved = []
    for layer in range(LAYERS):
        mix, first_layer = mixes[layer], layer == 0
        bound, gain = bounds[layer][None, :], gains[layer][None, :]
        unit, factor = rms_parts(stream)
        normed = gather_rows((unit * norm_mix[layer]).astype(bf16))
        if layer == 0:
            grad_y = gather_rows(after(cotangent, *normed))
        proj_input, proj_forget, proj_gate, local_state, local_decay = over_channels(
            functools.partial(scan_kernel, size, dot if first_layer else trans_dot),
            place_array,
            normed,
            [(mix, k * channels, first_layer) for k in range(3)],
            (keep, bound),
            ((block_rows, f32),) * 5,
            [pltpu.VMEM((block_rows, model_width), bf16)],
            channels,
            6 * block_rows * model_width * channels,
        )
        if layer == 0:
            local_state, local_decay = all_after((local_state, local_decay), *grad_y)
        last_row = lax.bitwise_xor(size - 1, place) * row_count + row_count - 1
        entering = entering_of(
            lax.dynamic_slice_in_dim(local_decay, last_row, 1, 0),
            lax.dynamic_slice_in_dim(local_state, last_row, 1, 0),
            False,
        )
        state = local_state + local_decay * entering
        squares = total_rows(jnp.sum(state * state, axis=1))
        inverse = lax.rsqrt(squares / model_width + epsilon)[:, None]
        loose = (state * gain * jax.nn.silu(proj_gate)).astype(bf16)
        if first_layer:
            part = trans_dot(loose, mix[:, 3 * channels :])
        else:
            part = dot(loose, mix[3 * channels :])
        parts = cut(part.astype(bf16), size)
        branch = scatter_rows(parts) * inverse[:row_count]
        middle = stream + branch
        unit_two, _ = rms_parts(middle)
        normed_two = (unit_two * norm_ffn[layer]).astype(bf16)
        normed_two = gather_rows(normed_two)
        upward, gating, hidden = up_and_gate(normed_two, boths[layer][0], hidden_units)
        if layer < last_layer:
            stream = middle + scatter_rows(cut(dot(hidden, rows_of(downs[layer], hidden_units)).astype(bf16), size))
        twin_rows = (twins(normed), twins(normed_two), twins([hidden]))
        saved.append(
            (factor, twin_rows, normed, proj_input, proj_forget, proj_gate, entering,
             state, inverse, branch, middle, normed_two, upward, gating, hidden, unit)
        )

    grad_x = cotangent.astype(f32)
    shards = [None] * LAYERS
    smalls = [None] * LAYERS
    scattered = {}

    def due(layer, place):
        names = [name for name, when in DUE.items() if when == (layer, place)]
        return tuple(scattered[name] for name in names if name in scattered)

    final_middle, final_hidden = saved[last_layer][10], saved[last_layer][14]
    for layer in reversed(range(LAYERS)):
        mix, both, first_layer = mixes[layer], rows_of(boths[layer], 2 * hidden_units), layer == 0
        bound, gain = bounds[layer][None, :], gains[layer][None, :]
        (factor, twin_rows, normed, proj_input, proj_forget, proj_gate, entering, state, inverse,
         branch, middle, normed_two, upward, gating, hidden, unit) = saved[layer]
        unit_two, factor_two = rms_parts(middle)
        all_normed, all_two = normed + twin_rows[0], normed_two + twin_rows[1]

        if layer < last_layer:
            grad_y = gather_rows(grad_x.astype(bf16), *due(layer, "gather"))
        down_part = outer([([hidden, *twin_rows[2]], grad_y + twins(grad_y))])
        down_shard = scattered["down", layer] = scatter_columns(down_part)
        grad_up, grad_glu = up_and_gate_back(
            all_after(grad_y, down_part), *downs[layer], upward, gating
        )
        twin_up, twin_glu = twins((grad_up, grad_glu))
        grad_up, grad_glu = all_after((grad_up, grad_glu), *due(layer, "part"))
        part = dot(jnp.concatenate([grad_up, grad_glu], axis=1), both).astype(bf16)
        *parts, ready = all_after((*cut(part, size), grad_up))
        ffn_part = outer([([ready, twin_up], all_two), ([grad_glu, twin_glu], all_two)])
        ffn_shard = scattered["ffn", layer] = scatter_columns(ffn_part)
        grad_normed_two = scatter_rows(parts, ffn_part, *due(layer, "sum"))
        ffn_piece = jnp.sum(grad_normed_two * unit_two, axis=0)
        grad_middle = grad_x + norm_back(grad_normed_two * norm_ffn[layer], unit_two, factor_two)

        grad_m_own = grad_middle.astype(bf16)
        grad_m_own = after(grad_m_own, *due(layer, "norm"))
        if first_layer:
            output = dot(after(final_hidden, grad_m_own), rows_of(downs[last_layer], hidden_units)).astype(bf16)
            grad_m = gather_rows(grad_m_own, output, *due(layer, "middle"))
            hidden_out = (final_middle + scatter_rows(cut(output, size))).astype(bf16)
        else:
            grad_m = gather_rows(grad_m_own, *due(layer, "middle"))
        inner = jnp.concatenate(
            gather_rows(jnp.sum(grad_m_own.astype(f32) * branch, axis=1)), axis=0
        )[:, None]
        adjoint, reach, grad_gate, mixed, gain_piece = over_channels(
            functools.partial(back_kernel, size, model_width, dot if first_layer else trans_dot),
            place_array,
            grad_m,
            [(mix, 3 * channels, first_layer)],
            (state, proj_gate, proj_forget, inverse, inner, keep, bound, gain),
            ((block_rows, f32), (block_rows, f32), (block_rows, bf16), (block_rows, bf16), (1, f32)),
            [pltpu.VMEM((block_rows, model_width), bf16), pltpu.VMEM((block_rows, min(LANES, channels)), f32)],
            channels,
            100 * block_rows * channels,
        )
        all_m, twin_mixed = grad_m + twins(grad_m), twins([mixed])
        first_row = place * row_count
        first_decay = (
            bound
            + (1.0 - bound)
            * jax.nn.sigmoid(lax.dynamic_slice_in_dim(proj_forget, first_row, 1, 0))
        ) * lax.dynamic_slice_in_dim(keep, first_row, 1, 0)
        coming = entering_of(
            first_decay * lax.dynamic_slice_in_dim(reach, first_row, 1, 0),
            first_decay * lax.dynamic_slice_in_dim(adjoint, first_row, 1, 0),
            True,
        )
        ready = [*all_m, *twin_mixed, *due(layer, "coming")]
        coming = after(coming, *ready)
        grad_input, grad_forget, bound_piece = over_channels(
            functools.partial(gates_kernel, size),
            place_array,
            [],
            [],
            (adjoint, reach, state, proj_input, proj_forget, keep, bound, coming, entering),
            ((block_rows, bf16), (block_rows, bf16), (1, f32)),
            [],
            channels,
            100 * block_rows * channels,
        )
        grad_three = (grad_input, grad_forget, grad_gate)
        joined = jnp.concatenate([grad_input, grad_forget, grad_gate], axis=1)
        if first_layer:
            joined = after(joined, hidden_out)
        (twin_joined,) = twins((joined,))
        if first_layer:
            low_part = outer([([joined, twin_joined], all_normed), ([mixed, *twin_mixed], all_m)])
            part = trans_dot(after(joined, low_part), mix[:, : 3 * channels])
        else:
            part = dot(joined, mix[: 3 * channels])
        part = part.astype(bf16)

        if first_layer:
            parts = cut(part, size)
        else:
            *parts, ready = all_after((*cut(part, size), joined))
            low_part = outer([([ready, twin_joined], all_normed), ([mixed, *twin_mixed], all_m)])
        low_shard = scattered["low", layer] = scatter_columns(low_part)
        grad_normed = scatter_rows(parts, low_part, *due(layer, "last"))
        mix_piece = jnp.sum(grad_normed * unit, axis=0)
        grad_x = grad_middle + norm_back(grad_normed * norm_mix[layer], unit, factor)

        smalls[layer] = (mix_piece, ffn_piece, bound_piece, gain_piece)
    wide_rows = jnp.stack([row for pieces in smalls for row in pieces[:2]])
    own_rows = jnp.concatenate([row for pieces in smalls for row in pieces[2:]], axis=0)
    small = total_small(after(wide_rows, grad_x, *due(0, "after")), own_rows, first_channel, channels)
    for layer in range(LAYERS):
        ffn_shard, down_shard, low_shard = (scattered[name, layer] for name in ("ffn", "down", "low"))
        if layer == 0:
            low_shard = after(low_shard, small)
        shards[layer] = (
            *(low_shard[k * channels : (k + 1) * channels].T for k in range(3)),
            low_shard[3 * channels :],
            ffn_shard[:hidden_units].T,
            ffn_shard[hidden_units:].T,
            down_shard,
        )
    stacked = tuple(
        jnp.stack([shards[layer][member].astype(f32) for layer in range(LAYERS)])
        for member in range(7)
    )
    wide_rows, own_rows = small[: 2 * LAYERS], small[2 * LAYERS :]
    return (
        hidden_out, grad_x, *stacked, own_rows[0::2], wide_rows[0::2], wide_rows[1::2], own_rows[1::2]
    )


def solution(mesh):
    length, size = mesh.devices.shape
    split = Mesh(mesh.devices.reshape(length // 2, 2, size), (*SEQ, "fsdp"))
    rows = P((*SEQ, "fsdp"), None)
    wide = P(None, SEQ, "fsdp")
    tall = P(None, "fsdp", SEQ)
    weights = (wide, wide, wide, tall, wide, wide, tall)
    return jax.shard_map(
        local,
        mesh=split,
        in_specs=(rows, *weights, P(), P(), P(), P(), P(), rows),
        out_specs=(rows, rows, *weights, P(), P(), P(), P()),
        check_vma=False,
    )
```

```python
import functools

import jax
import jax.numpy as jnp
from jax import lax
from jax.experimental import pallas as pl
from jax.experimental.pallas import tpu as pltpu
from jax.sharding import Mesh
from jax.sharding import PartitionSpec as P

LAYERS = 2
epsilon = 1e-06
STEP = 32
LANES = 256
VMEM = 52 * 1024 * 1024
OUTER = 4
SCALE = 5.5
DUE = {
    ("down", 1): (1, "sum"), ("ffn", 1): (0, "gather"), ("low", 1): (0, "part"),
    ("down", 0): (0, "middle"), ("ffn", 0): (0, "last"),
}
f32 = jnp.float32
bf16 = jnp.bfloat16
SEQ = ("chip", "core")
NT = (((1,), (1,)), ((), ()))


def exchange(values, step):
    size = lax.axis_size("fsdp")
    return lax.ppermute(values, "fsdp", [(i, i ^ step) for i in range(size)])


def swap(values, axis):
    return lax.ppermute(values, axis, [(0, 1), (1, 0)])


def seq_length():
    return lax.axis_size("chip") * lax.axis_size("core")


def after(value, *others):
    return lax.optimization_barrier((value, *others))[0]


def all_after(values, *others):
    return list(lax.optimization_barrier((*values, *others)))[: len(values)]


def gather_rows(own, *meanwhile):
    arrived = [exchange(own, step) for step in range(1, lax.axis_size("fsdp"))]
    return [own] + all_after(arrived, *meanwhile)


def scatter_rows(pieces, *meanwhile):
    arrived = [exchange(pieces[step], step) for step in range(1, len(pieces))]
    if meanwhile:
        arrived = all_after(arrived, *meanwhile)
    total = pieces[0].astype(f32)
    for piece in arrived:
        total = total + piece.astype(f32)
    return total


def total_rows(part):
    size = lax.axis_size("fsdp")
    pieces = part.reshape(size, -1)
    total = pieces
    for step in range(1, size):
        other = exchange(pieces, step)
        total = total + jnp.stack([other[k ^ step] for k in range(size)])
    return total.reshape(-1)


def rms_parts(values):
    factor = lax.rsqrt(jnp.mean(values * values, axis=-1, keepdims=True) + epsilon)
    return (values * factor, factor)


def norm_back(grad_unit, unit_rows, factor):
    return factor * (
        grad_unit - unit_rows * jnp.mean(grad_unit * unit_rows, axis=-1, keepdims=True)
    )


def dsilu(values, sigma):
    return sigma * (1.0 + values * (1.0 - sigma))


def sigmoid(values):
    return 1.0 / (1.0 + jnp.exp(-values))


def dot(left, right):
    return jnp.dot(left, right, preferred_element_type=f32)


def trans_dot(left, right):
    return lax.dot_general(left, right, NT, preferred_element_type=f32)


def whole(array):
    return pl.BlockSpec(array.shape, lambda j, *_: (0, 0))


def call(kernel, grid, in_specs, out_specs, out_shape, scratch, operands, cost, prefetch=()):
    return pl.pallas_call(
        kernel,
        grid_spec=pltpu.PrefetchScalarGridSpec(
            num_scalar_prefetch=len(prefetch),
            grid=grid,
            in_specs=in_specs,
            out_specs=out_specs,
            scratch_shapes=scratch,
        ),
        out_shape=out_shape,
        compiler_params=pltpu.CompilerParams(vmem_limit_bytes=VMEM),
        cost_estimate=pl.CostEstimate(flops=int(SCALE * cost), bytes_accessed=cost // 512, transcendentals=0),
    )(*prefetch, *operands)


def assemble(pieces, rows_ref):
    rows = pieces[0].shape[0]

    @pl.when(pl.program_id(0) == 0)
    def _():
        for k, piece in enumerate(pieces):
            rows_ref[k * rows : (k + 1) * rows, :] = piece[...]


def twins(values):
    return [swap(v, "core") for v in values]


def outer(terms):
    lefts = [left for left, _ in terms]
    groups, which = [], []
    for _, pieces in terms:
        found = [k for k, group in enumerate(groups) if group is pieces]
        which.append(found[0] if found else len(groups))
        if not found:
            groups.append(pieces)
    rows, width = sum(p.shape[0] for p in groups[0]), groups[0][0].shape[1] // seq_length()
    heights = [left[0].shape[1] for left in lefts]
    flat = [piece for left in lefts for piece in left]
    total, count, chips = sum(heights), len(groups[0]), lax.axis_size("chip")

    def kernel(core_ref, *refs):
        left_refs, refs = refs[: len(flat)], refs[len(flat) :]
        piece_refs, (out, turned) = refs[: count * len(groups)], refs[count * len(groups) :]

        @pl.when(pl.program_id(0) == 0)
        def _():
            top, at = 0, 0
            for left, height in zip(lefts, heights, strict=True):
                start = 0
                for k, piece in enumerate(left):
                    turned[top : top + height, start : start + piece.shape[0]] = left_refs[at + k][...].T
                    start += piece.shape[0]
                top, at = top + height, at + len(left)

        rights = [
            jnp.concatenate([ref[...] for ref in piece_refs[g * count : (g + 1) * count]], axis=0)
            for g in range(len(groups))
        ]
        top = 0
        for height, group in zip(heights, which, strict=True):
            out[top : top + height, :] = dot(turned[top : top + height, :], rights[group]).astype(bf16)
            top += height

    return call(
        kernel,
        (chips,),
        [whole(left) for left in flat]
        + [
            pl.BlockSpec((p.shape[0], width), lambda j, core: (0, 2 * j + core[0]))
            for group in groups
            for p in group
        ],
        pl.BlockSpec((total, width), lambda j, core: (0, j)),
        jax.ShapeDtypeStruct((total, width * chips), bf16),
        [pltpu.VMEM((total, rows), bf16)],
        [*flat, *(piece for group in groups for piece in group)],
        OUTER * rows * total * width * chips,
        prefetch=(jnp.reshape(lax.axis_index("core"), (1,)).astype(jnp.int32),),
    )


def scatter_columns(part):
    return lax.psum_scatter(part, "chip", scatter_dimension=1, tiled=True)


def cut(values, count):
    rows = values.shape[0] // count
    return [values[k * rows : (k + 1) * rows] for k in range(count)]


def unfold(shards):
    height, width = shards[0].shape
    units, layers = height // 4, len(shards)

    def kernel(*refs):
        for layer, ref in enumerate(refs[:layers]):
            for k, out in enumerate(refs[layers:]):
                part = ref[k * units : (k + 1) * units, :].astype(f32)
                out[layer] = part if k == 3 else part.T

    shapes = [(layers, width, units)] * 3 + [(layers, units, width)]
    return call(
        kernel,
        (1,),
        [whole(shard) for shard in shards],
        [pl.BlockSpec(shape, lambda j: (0, 0, 0)) for shape in shapes],
        [jax.ShapeDtypeStruct(shape, f32) for shape in shapes],
        [],
        shards,
        0,
    )


def rows_at(matrix, at, rows, tile):
    return (matrix, at // tile) if at % tile == 0 else (matrix[at : at + rows], 0)


def tile_of(units):
    return (128, units // 128) if units % 128 == 0 else (units, 1)


def up_and_gate(pieces, both, units):
    rows, depth = sum(p.shape[0] for p in pieces), pieces[0].shape[1]
    tile, steps = tile_of(units)
    chunk = rows if steps > 1 else rows // 4

    def kernel(*refs):
        piece_refs, (up_ref, gate_ref, upward_ref, gating_ref, hidden_ref, x_ref) = (
            refs[: len(pieces)], refs[len(pieces) :],
        )
        assemble(piece_refs, x_ref)
        for start in range(0, rows, chunk):
            here = slice(start, start + chunk)
            x = x_ref[here, :]
            if steps > 1:
                joined = trans_dot(x, jnp.concatenate([up_ref[...], gate_ref[...]], axis=0))
                upward, gating = joined[:, :tile], joined[:, tile:]
            else:
                upward, gating = trans_dot(x, up_ref[...]), trans_dot(x, gate_ref[...])
            upward_ref[here, :] = upward.astype(bf16)
            gating_ref[here, :] = gating.astype(bf16)
            hidden_ref[here, :] = (gating * sigmoid(gating) * upward).astype(bf16)

    out = jax.ShapeDtypeStruct((rows, units), bf16)
    return call(
        kernel,
        (steps,),
        [whole(p) for p in pieces]
        + [
            pl.BlockSpec((tile, depth), lambda j: (j, 0)),
            pl.BlockSpec((tile, depth), lambda j: (steps + j, 0)),
        ],
        [pl.BlockSpec((rows, tile), lambda j: (0, j))] * 3,
        [out] * 3,
        [pltpu.VMEM((rows, depth), bf16)],
        [*pieces, both, both],
        4 * rows * depth * units,
    )


def up_and_gate_back(pieces, down, at, upward, gating):
    rows, depth = sum(p.shape[0] for p in pieces), pieces[0].shape[1]
    units = upward.shape[1]
    tile, steps = (256, -(-units // 256)) if units % 128 == 0 else (units, 1)
    down, first = rows_at(down, at, units, tile)
    chunk = rows if steps > 1 else rows // 4

    def kernel(*refs):
        piece_refs, (down_ref, upward_ref, gating_ref, grad_up_ref, grad_gate_ref, x_ref) = (
            refs[: len(pieces)], refs[len(pieces) :],
        )
        assemble(piece_refs, x_ref)
        for start in range(0, rows, chunk):
            here = slice(start, start + chunk)
            grad = trans_dot(x_ref[here, :], down_ref[...])
            gating = gating_ref[here, :].astype(f32)
            sigma = sigmoid(gating)
            grad_up_ref[here, :] = (grad * gating * sigma).astype(bf16)
            grad_gate_ref[here, :] = (
                grad * upward_ref[here, :].astype(f32) * dsilu(gating, sigma)
            ).astype(bf16)

    block = pl.BlockSpec((rows, tile), lambda j: (0, j))
    out = jax.ShapeDtypeStruct((rows, units), bf16)
    return call(
        kernel,
        (steps,),
        [whole(p) for p in pieces]
        + [pl.BlockSpec((tile, depth), lambda j: (first + j, 0)), block, block],
        [block] * 2,
        [out] * 2,
        [pltpu.VMEM((rows, depth), bf16)],
        [*pieces, down, upward, gating],
        2 * rows * depth * units,
    )


def tile_base(place, index, size, per_piece):
    piece = lax.bitwise_xor(index // per_piece, place)
    return pl.multiple_of((piece * per_piece + lax.rem(index, per_piece)) * STEP, STEP)


def scan_kernel(count, product, place_ref, *refs):
    piece_refs, refs = refs[:count], refs[count:]
    (input_ref, forget_ref, gate_ref, keep_ref, bound_ref,
     pi_ref, pf_ref, pg_ref, state_ref, decay_ref, x_ref) = refs
    assemble(piece_refs, x_ref)
    x = x_ref[...]
    pi_ref[...] = product(x, input_ref[...])
    pf_ref[...] = product(x, forget_ref[...])
    pg_ref[...] = product(x, gate_ref[...])
    rows, lanes = pi_ref.shape
    per_piece = rows // count // STEP
    place = place_ref[0]
    bound = bound_ref[...]
    row = lax.broadcasted_iota(jnp.int32, (8, lanes), 0)

    def step(index, carry):
        carry_decay, carry_state = carry
        base = tile_base(place, index, count, per_piece)
        here = pl.ds(base, STEP)
        forget = bound + (1.0 - bound) * sigmoid(pf_ref[here, :])
        inp = pi_ref[here, :]
        source = inp * sigmoid(inp) * (1.0 - forget)
        decay = forget * keep_ref[here, :]
        for part in range(STEP // 8):
            a = decay[part * 8 : part * 8 + 8]
            b = source[part * 8 : part * 8 + 8]
            for shift in (1, 2, 4):
                a_before = jnp.where(row >= shift, pltpu.roll(a, shift, 0), 1.0)
                b_before = jnp.where(row >= shift, pltpu.roll(b, shift, 0), 0.0)
                b = a * b_before + b
                a = a * a_before
            b = a * carry_state + b
            a = a * carry_decay
            state_ref[pl.ds(base + part * 8, 8), :] = b
            decay_ref[pl.ds(base + part * 8, 8), :] = a
            carry_decay, carry_state = a[7:8], b[7:8]
        return carry_decay, carry_state

    lax.fori_loop(
        0, rows // STEP, step, (jnp.ones((1, lanes), f32), jnp.zeros((1, lanes), f32))
    )


def back_kernel(count, width, product, place_ref, *refs):
    piece_refs, refs = refs[:count], refs[count:]
    (out_ref, state_ref, gate_ref, pf_ref, inverse_ref, inner_ref, keep_ref, bound_ref, gain_ref,
     adjoint_ref, reach_ref, grad_gate_ref, mix_ref, gain_out_ref, x_ref, mixed_ref) = refs
    assemble(piece_refs, x_ref)
    mixed_ref[...] = product(x_ref[...], out_ref[...])
    rows, lanes = mixed_ref.shape
    per_piece = rows // count // STEP
    place = place_ref[0]
    bound = bound_ref[...]
    gain = gain_ref[...]
    row = lax.broadcasted_iota(jnp.int32, (8, lanes), 0)
    tiles = rows // STEP

    def step(number, carry):
        carry_reach, carry_adjoint, later, gain_sum = carry
        base = tile_base(place, tiles - 1 - number, count, per_piece)
        here = pl.ds(base, STEP)
        grad_mixed = mixed_ref[here, :]
        inverse = inverse_ref[here, :]
        scaled = state_ref[here, :] * inverse
        gate = gate_ref[here, :]
        sigma = sigmoid(gate)
        silu_gate = gate * sigma
        piece = grad_mixed * scaled
        contribution = piece * silu_gate
        grad_gate_ref[here, :] = (piece * gain * dsilu(gate, sigma)).astype(bf16)
        mix_ref[here, :] = (scaled * gain * silu_gate).astype(bf16)
        grad_state = inverse * (
            grad_mixed * gain * silu_gate - scaled * (inner_ref[here, :] * (1.0 / width))
        )
        decay = (bound + (1.0 - bound) * sigmoid(pf_ref[here, :])) * keep_ref[here, :]
        for part in reversed(range(STEP // 8)):
            now = decay[part * 8 : part * 8 + 8]
            gain_sum = gain_sum + contribution[part * 8 : part * 8 + 8]
            a = jnp.where(row == 7, later, pltpu.roll(now, 7, 0))
            b = grad_state[part * 8 : part * 8 + 8]
            for shift in (1, 2, 4):
                a_after = jnp.where(row < 8 - shift, pltpu.roll(a, 8 - shift, 0), 1.0)
                b_after = jnp.where(row < 8 - shift, pltpu.roll(b, 8 - shift, 0), 0.0)
                b = a * b_after + b
                a = a * a_after
            b = a * carry_adjoint + b
            a = a * carry_reach
            adjoint_ref[pl.ds(base + part * 8, 8), :] = b
            reach_ref[pl.ds(base + part * 8, 8), :] = a
            carry_reach, carry_adjoint, later = a[0:1], b[0:1], now[0:1]
        return carry_reach, carry_adjoint, later, gain_sum

    one, zero = jnp.ones((1, lanes), f32), jnp.zeros((1, lanes), f32)
    last = lax.fori_loop(0, tiles, step, (one, zero, one, jnp.zeros((8, lanes), f32)))
    gain_out_ref[...] = jnp.sum(last[3], axis=0, keepdims=True)


def gates_kernel(
    count, place_ref, adjoint_ref, reach_ref, state_ref, pi_ref, pf_ref, keep_ref, bound_ref,
    coming_ref, entering_ref, grad_input_ref, grad_forget_ref, bound_out_ref,
):
    rows, lanes = adjoint_ref.shape
    per_piece = rows // count // STEP
    place = place_ref[0]
    bound = bound_ref[...]
    coming = coming_ref[...]
    row = lax.broadcasted_iota(jnp.int32, (STEP, lanes), 0)

    def step(index, carry):
        before, bound_sum = carry
        base = tile_base(place, index, count, per_piece)
        here = pl.ds(base, STEP)
        adjoint = adjoint_ref[here, :] + reach_ref[here, :] * coming
        state = state_ref[here, :]
        previous = jnp.where(row == 0, before, pltpu.roll(state, 1, 0))
        inp = pi_ref[here, :]
        sigma_input = sigmoid(inp)
        sigma_forget = sigmoid(pf_ref[here, :])
        forget = bound + (1.0 - bound) * sigma_forget
        grad_forget = adjoint * (keep_ref[here, :] * previous - inp * sigma_input)
        piece = grad_forget * (1.0 - sigma_forget)
        grad_input_ref[here, :] = (adjoint * (1.0 - forget) * dsilu(inp, sigma_input)).astype(bf16)
        grad_forget_ref[here, :] = (piece * (1.0 - bound) * sigma_forget).astype(bf16)
        for part in range(STEP // 8):
            bound_sum = bound_sum + piece[part * 8 : part * 8 + 8]
        return state[STEP - 1 : STEP], bound_sum

    last = lax.fori_loop(
        0, rows // STEP, step, (entering_ref[...], jnp.zeros((8, lanes), f32))
    )
    bound_out_ref[...] = jnp.sum(last[1], axis=0, keepdims=True)


def over_channels(kernel, place, pieces, matrices, operands, outs, scratch, channels, cost):
    lanes = min(LANES, channels)

    def part(matrix, at, columns):
        if columns:
            return pl.BlockSpec((matrix.shape[0], lanes), lambda c, p: (0, at // lanes + c))
        return pl.BlockSpec((lanes, matrix.shape[1]), lambda c, p: (at // lanes + c, 0))

    def spec(rows, narrow):
        if narrow:
            return pl.BlockSpec((rows, 1), lambda c, p: (0, 0))
        return pl.BlockSpec((rows, lanes), lambda c, p: (0, c))

    return call(
        kernel,
        (channels // lanes,),
        [whole(p) for p in pieces]
        + [part(*m) for m in matrices]
        + [spec(o.shape[0], o.shape[1] == 1) for o in operands],
        [spec(rows, False) for rows, _ in outs],
        [jax.ShapeDtypeStruct((rows, channels), kind) for rows, kind in outs],
        scratch,
        [*pieces, *(m[0] for m in matrices), *operands],
        cost,
        prefetch=(place,),
    )


def entering_of(decay, state, reverse):
    length = seq_length()
    chips, core = length // 2, lax.axis_index("core")
    own = jnp.concatenate([decay, state], axis=0)
    other = swap(own, "core")
    is_first = core == (1 if reverse else 0)
    first, second = jnp.where(is_first, own, other), jnp.where(is_first, other, own)
    pair = jnp.concatenate(
        [first[0:1] * second[0:1], second[0:1] * first[1:2] + second[1:2]], axis=0
    )
    sign = -1 if reverse else 1
    arrived = [
        lax.ppermute(
            pair,
            SEQ,
            [(i, i + sign * 2 * hop) for i in range(length) if 0 <= i + sign * 2 * hop < length],
        )
        for hop in range(1, chips)
    ]
    total = jnp.zeros_like(state)
    for hop in range(chips - 1, 0, -1):
        total = arrived[hop - 1][0:1] * total + arrived[hop - 1][1:2]
    return jnp.where(is_first, total, other[0:1] * total + other[1:2])


def total_small(rows_of_width, rows_of_channels, first_channel, channels):
    size = lax.axis_size("fsdp")
    place = lax.axis_index("fsdp")

    def columns(step):
        return lax.dynamic_slice_in_dim(
            rows_of_width, lax.bitwise_xor(place, step) * channels, channels, 1
        )

    mine = columns(0)
    for step in range(1, size):
        mine = mine + exchange(columns(step), step)
    mine = jnp.concatenate([mine, rows_of_channels], axis=0)
    mine = mine + swap(mine, "core")
    chips, step = lax.axis_size("chip"), 1
    while step < chips:
        mine = mine + lax.ppermute(mine, "chip", [(i, i ^ step) for i in range(chips)])
        step *= 2
    total = jnp.zeros((mine.shape[0], channels * size), f32)
    total = lax.dynamic_update_slice_in_dim(total, mine, first_channel, 1)
    for step in range(1, size):
        total = lax.dynamic_update_slice_in_dim(
            total, exchange(mine, step), lax.bitwise_xor(place, step) * channels, 1
        )
    return total


def local(
    hidden_in, w_input, w_forget, w_gate, w_out, w_up, w_glu, w_down,
    lower_bound, norm_mix, norm_ffn, out_gain, lengths, cotangent,
):
    row_count, model_width = hidden_in.shape
    channels = w_input.shape[2]
    hidden_units = w_up.shape[2]
    size = lax.axis_size("fsdp")
    place = lax.axis_index("fsdp")
    block_rows = row_count * size
    first_channel = place * channels
    place_array = jnp.reshape(place, (1,)).astype(jnp.int32)
    last_layer = LAYERS - 1

    starts = jnp.cumsum(lengths) - lengths
    owners = lax.bitwise_xor(jnp.arange(size, dtype=jnp.int32), place.astype(jnp.int32))
    positions = (
        lax.axis_index(SEQ) * block_rows
        + (owners[:, None] * row_count + jnp.arange(row_count, dtype=jnp.int32)[None, :])
    ).reshape(-1)
    keep = (1.0 - jnp.any(positions[:, None] == starts[None, :], axis=1).astype(f32))[:, None]
    bounds = lax.dynamic_slice_in_dim(lower_bound, first_channel, channels, 1)
    gains = lax.dynamic_slice_in_dim(out_gain, first_channel, channels, 1)

    def side(*shards):
        return lax.all_gather(jnp.concatenate(shards, axis=1), SEQ, axis=0, tiled=True)

    def tall(*shards):
        return lax.all_gather(jnp.concatenate(shards, axis=0), SEQ, axis=1, tiled=True)

    mixes, boths, downs = [side(w_input[0], w_forget[0], w_gate[0], w_out[0].T)], [], []
    for layer in range(LAYERS):
        if layer > 0:
            mixes.append(tall(w_input[layer].T, w_forget[layer].T, w_gate[layer].T, w_out[layer]))
        if layer < last_layer:
            joined = tall(w_up[layer].T, w_glu[layer].T, w_down[layer])
            boths.append((joined, 0))
            downs.append((joined, 2 * hidden_units))
        else:
            boths.append((tall(w_up[layer].T, w_glu[layer].T), 0))
            downs.append((tall(w_down[layer]), 0))

    def rows_of(matrix_at, rows):
        matrix, at = matrix_at
        return matrix[at : at + rows]

    stream = hidden_in.astype(f32)
    saved = []
    for layer in range(LAYERS):
        mix, first_layer = mixes[layer], layer == 0
        bound, gain = bounds[layer][None, :], gains[layer][None, :]
        unit, factor = rms_parts(stream)
        normed = gather_rows((unit * norm_mix[layer]).astype(bf16))
        if layer == 0:
            grad_y = gather_rows(after(cotangent, *normed))
        proj_input, proj_forget, proj_gate, local_state, local_decay = over_channels(
            functools.partial(scan_kernel, size, dot if first_layer else trans_dot),
            place_array,
            normed,
            [(mix, k * channels, first_layer) for k in range(3)],
            (keep, bound),
            ((block_rows, f32),) * 5,
            [pltpu.VMEM((block_rows, model_width), bf16)],
            channels,
            6 * block_rows * model_width * channels,
        )
        if layer == 0:
            local_state, local_decay = all_after((local_state, local_decay), *grad_y)
        last_row = lax.bitwise_xor(size - 1, place) * row_count + row_count - 1
        entering = entering_of(
            lax.dynamic_slice_in_dim(local_decay, last_row, 1, 0),
            lax.dynamic_slice_in_dim(local_state, last_row, 1, 0),
            False,
        )
        state = local_state + local_decay * entering
        squares = total_rows(jnp.sum(state * state, axis=1))
        inverse = lax.rsqrt(squares / model_width + epsilon)[:, None]
        loose = (state * gain * jax.nn.silu(proj_gate)).astype(bf16)
        if first_layer:
            part = trans_dot(loose, mix[:, 3 * channels :])
        else:
            part = dot(loose, mix[3 * channels :])
        parts = cut(part.astype(bf16), size)
        branch = scatter_rows(parts) * inverse[:row_count]
        middle = stream + branch
        unit_two, _ = rms_parts(middle)
        normed_two = (unit_two * norm_ffn[layer]).astype(bf16)
        normed_two = gather_rows(normed_two)
        upward, gating, hidden = up_and_gate(normed_two, boths[layer][0], hidden_units)
        if layer < last_layer:
            stream = middle + scatter_rows(cut(dot(hidden, rows_of(downs[layer], hidden_units)).astype(bf16), size))
        twin_rows = (twins(normed), twins(normed_two), twins([hidden]))
        saved.append(
            (factor, twin_rows, normed, proj_input, proj_forget, proj_gate, entering,
             state, inverse, branch, middle, normed_two, upward, gating, hidden, unit)
        )

    grad_x = cotangent.astype(f32)
    shards = [None] * LAYERS
    smalls = [None] * LAYERS
    scattered = {}

    def due(layer, place):
        names = [name for name, when in DUE.items() if when == (layer, place)]
        return tuple(scattered[name] for name in names if name in scattered)

    final_middle, final_hidden = saved[last_layer][10], saved[last_layer][14]
    for layer in reversed(range(LAYERS)):
        mix, both, first_layer = mixes[layer], rows_of(boths[layer], 2 * hidden_units), layer == 0
        bound, gain = bounds[layer][None, :], gains[layer][None, :]
        (factor, twin_rows, normed, proj_input, proj_forget, proj_gate, entering, state, inverse,
         branch, middle, normed_two, upward, gating, hidden, unit) = saved[layer]
        unit_two, factor_two = rms_parts(middle)
        all_normed, all_two = normed + twin_rows[0], normed_two + twin_rows[1]

        if layer < last_layer:
            grad_y = gather_rows(grad_x.astype(bf16), *due(layer, "gather"))
        down_part = outer([([hidden, *twin_rows[2]], grad_y + twins(grad_y))])
        down_shard = scattered["down", layer] = scatter_columns(down_part)
        grad_up, grad_glu = up_and_gate_back(
            all_after(grad_y, down_part), *downs[layer], upward, gating
        )
        twin_up, twin_glu = twins((grad_up, grad_glu))
        grad_up, grad_glu = all_after((grad_up, grad_glu), *due(layer, "part"))
        part = dot(jnp.concatenate([grad_up, grad_glu], axis=1), both).astype(bf16)
        *parts, ready = all_after((*cut(part, size), grad_up))
        ffn_part = outer([([ready, twin_up], all_two), ([grad_glu, twin_glu], all_two)])
        ffn_shard = scattered["ffn", layer] = scatter_columns(ffn_part)
        grad_normed_two = scatter_rows(parts, ffn_part, *due(layer, "sum"))
        ffn_piece = jnp.sum(grad_normed_two * unit_two, axis=0)
        grad_middle = grad_x + norm_back(grad_normed_two * norm_ffn[layer], unit_two, factor_two)

        grad_m_own = grad_middle.astype(bf16)
        grad_m_own = after(grad_m_own, *due(layer, "norm"))
        if first_layer:
            output = dot(after(final_hidden, grad_m_own), rows_of(downs[last_layer], hidden_units)).astype(bf16)
            grad_m = gather_rows(grad_m_own, output, *due(layer, "middle"))
            hidden_out = (final_middle + scatter_rows(cut(output, size))).astype(bf16)
        else:
            grad_m = gather_rows(grad_m_own, *due(layer, "middle"))
        inner = jnp.concatenate(
            gather_rows(jnp.sum(grad_m_own.astype(f32) * branch, axis=1)), axis=0
        )[:, None]
        adjoint, reach, grad_gate, mixed, gain_piece = over_channels(
            functools.partial(back_kernel, size, model_width, dot if first_layer else trans_dot),
            place_array,
            grad_m,
            [(mix, 3 * channels, first_layer)],
            (state, proj_gate, proj_forget, inverse, inner, keep, bound, gain),
            ((block_rows, f32), (block_rows, f32), (block_rows, bf16), (block_rows, bf16), (1, f32)),
            [pltpu.VMEM((block_rows, model_width), bf16), pltpu.VMEM((block_rows, min(LANES, channels)), f32)],
            channels,
            100 * block_rows * channels,
        )
        all_m, twin_mixed = grad_m + twins(grad_m), twins([mixed])
        first_row = place * row_count
        first_decay = (
            bound
            + (1.0 - bound)
            * jax.nn.sigmoid(lax.dynamic_slice_in_dim(proj_forget, first_row, 1, 0))
        ) * lax.dynamic_slice_in_dim(keep, first_row, 1, 0)
        coming = entering_of(
            first_decay * lax.dynamic_slice_in_dim(reach, first_row, 1, 0),
            first_decay * lax.dynamic_slice_in_dim(adjoint, first_row, 1, 0),
            True,
        )
        ready = [*all_m, *twin_mixed, *due(layer, "coming")]
        coming = after(coming, *ready)
        grad_input, grad_forget, bound_piece = over_channels(
            functools.partial(gates_kernel, size),
            place_array,
            [],
            [],
            (adjoint, reach, state, proj_input, proj_forget, keep, bound, coming, entering),
            ((block_rows, bf16), (block_rows, bf16), (1, f32)),
            [],
            channels,
            100 * block_rows * channels,
        )
        grad_three = (grad_input, grad_forget, grad_gate)
        joined = jnp.concatenate([grad_input, grad_forget, grad_gate], axis=1)
        if first_layer:
            joined = after(joined, hidden_out)
        (twin_joined,) = twins((joined,))
        part = trans_dot(joined, mix[:, : 3 * channels]) if first_layer else dot(joined, mix[: 3 * channels])
        part = part.astype(bf16)

        *parts, ready = all_after((*cut(part, size), joined))
        low_part = outer([([ready, twin_joined], all_normed), ([mixed, *twin_mixed], all_m)])
        low_shard = scattered["low", layer] = scatter_columns(low_part)
        grad_normed = scatter_rows(parts, low_part, *due(layer, "last"))
        mix_piece = jnp.sum(grad_normed * unit, axis=0)
        grad_x = grad_middle + norm_back(grad_normed * norm_mix[layer], unit, factor)

        smalls[layer] = (mix_piece, ffn_piece, bound_piece, gain_piece)
    wide_rows = jnp.stack([row for pieces in smalls for row in pieces[:2]])
    own_rows = jnp.concatenate([row for pieces in smalls for row in pieces[2:]], axis=0)
    small = total_small(after(wide_rows, *due(0, "after")), own_rows, first_channel, channels)
    for layer in range(LAYERS):
        ffn_shard, down_shard = scattered["ffn", layer], scattered["down", layer]
        shards[layer] = (ffn_shard[:hidden_units].T, ffn_shard[hidden_units:].T, down_shard)
    low_shards = [after(scattered["low", 0], grad_x)] + [scattered["low", k] for k in range(1, LAYERS)]
    stacked = [*unfold(low_shards)] + [
        jnp.stack([shards[layer][member].astype(f32) for layer in range(LAYERS)]) for member in range(3)
    ]
    wide_rows, own_rows = small[: 2 * LAYERS], small[2 * LAYERS :]
    return (
        hidden_out, grad_x, *stacked, own_rows[0::2], wide_rows[0::2], wide_rows[1::2], own_rows[1::2]
    )


def solution(mesh):
    length, size = mesh.devices.shape
    split = Mesh(mesh.devices.reshape(length // 2, 2, size), (*SEQ, "fsdp"))
    rows = P((*SEQ, "fsdp"), None)
    wide = P(None, SEQ, "fsdp")
    tall = P(None, "fsdp", SEQ)
    weights = (wide, wide, wide, tall, wide, wide, tall)
    return jax.shard_map(
        local,
        mesh=split,
        in_specs=(rows, *weights, P(), P(), P(), P(), P(), rows),
        out_specs=(rows, rows, *weights, P(), P(), P(), P()),
        check_vma=False,
    )
```

```python
import functools

import jax
import jax.numpy as jnp
from jax import lax
from jax.experimental import pallas as pl
from jax.experimental.pallas import tpu as pltpu
from jax.sharding import Mesh
from jax.sharding import PartitionSpec as P

LAYERS = 2
epsilon = 1e-06
STEP = 32
LANES = 256
VMEM = 52 * 1024 * 1024
OUTER = 4
SCALE = 5.5
DUE = {
    ("down", 1): (1, "sum"), ("ffn", 1): (0, "gather"), ("low", 1): (0, "part"),
    ("down", 0): (0, "middle"), ("ffn", 0): (0, "last"),
}
f32 = jnp.float32
bf16 = jnp.bfloat16
SEQ = ("chip", "core")
NT = (((1,), (1,)), ((), ()))


def exchange(values, step):
    size = lax.axis_size("fsdp")
    return lax.ppermute(values, "fsdp", [(i, i ^ step) for i in range(size)])


def swap(values, axis):
    return lax.ppermute(values, axis, [(0, 1), (1, 0)])


def seq_length():
    return lax.axis_size("chip") * lax.axis_size("core")


def after(value, *others):
    return lax.optimization_barrier((value, *others))[0]


def all_after(values, *others):
    return list(lax.optimization_barrier((*values, *others)))[: len(values)]


def gather_rows(own, *meanwhile):
    arrived = [exchange(own, step) for step in range(1, lax.axis_size("fsdp"))]
    return [own] + all_after(arrived, *meanwhile)


def scatter_rows(pieces, *meanwhile):
    arrived = [exchange(pieces[step], step) for step in range(1, len(pieces))]
    if meanwhile:
        arrived = all_after(arrived, *meanwhile)
    total = pieces[0].astype(f32)
    for piece in arrived:
        total = total + piece.astype(f32)
    return total


def total_rows(part):
    size = lax.axis_size("fsdp")
    pieces = part.reshape(size, -1)
    total = pieces
    for step in range(1, size):
        other = exchange(pieces, step)
        total = total + jnp.stack([other[k ^ step] for k in range(size)])
    return total.reshape(-1)


def rms_parts(values):
    factor = lax.rsqrt(jnp.mean(values * values, axis=-1, keepdims=True) + epsilon)
    return (values * factor, factor)


def norm_back(grad_unit, unit_rows, factor):
    return factor * (
        grad_unit - unit_rows * jnp.mean(grad_unit * unit_rows, axis=-1, keepdims=True)
    )


def dsilu(values, sigma):
    return sigma * (1.0 + values * (1.0 - sigma))


def sigmoid(values):
    return 1.0 / (1.0 + jnp.exp(-values))


def dot(left, right):
    return jnp.dot(left, right, preferred_element_type=f32)


def trans_dot(left, right):
    return lax.dot_general(left, right, NT, preferred_element_type=f32)


def whole(array):
    return pl.BlockSpec(array.shape, lambda j, *_: (0, 0))


def call(kernel, grid, in_specs, out_specs, out_shape, scratch, operands, cost, prefetch=()):
    return pl.pallas_call(
        kernel,
        grid_spec=pltpu.PrefetchScalarGridSpec(
            num_scalar_prefetch=len(prefetch),
            grid=grid,
            in_specs=in_specs,
            out_specs=out_specs,
            scratch_shapes=scratch,
        ),
        out_shape=out_shape,
        compiler_params=pltpu.CompilerParams(vmem_limit_bytes=VMEM),
        cost_estimate=pl.CostEstimate(flops=int(SCALE * cost), bytes_accessed=cost // 512, transcendentals=0),
    )(*prefetch, *operands)


def assemble(pieces, rows_ref):
    rows = pieces[0].shape[0]

    @pl.when(pl.program_id(0) == 0)
    def _():
        for k, piece in enumerate(pieces):
            rows_ref[k * rows : (k + 1) * rows, :] = piece[...]


def twins(values):
    return [swap(v, "core") for v in values]


def outer(terms):
    lefts = [left for left, _ in terms]
    groups, which = [], []
    for _, pieces in terms:
        found = [k for k, group in enumerate(groups) if group is pieces]
        which.append(found[0] if found else len(groups))
        if not found:
            groups.append(pieces)
    rows, width = sum(p.shape[0] for p in groups[0]), groups[0][0].shape[1] // seq_length()
    heights = [left[0].shape[1] for left in lefts]
    flat = [piece for left in lefts for piece in left]
    total, count, chips = sum(heights), len(groups[0]), lax.axis_size("chip")

    def kernel(core_ref, *refs):
        left_refs, refs = refs[: len(flat)], refs[len(flat) :]
        piece_refs, (out, turned) = refs[: count * len(groups)], refs[count * len(groups) :]

        @pl.when(pl.program_id(0) == 0)
        def _():
            top, at = 0, 0
            for left, height in zip(lefts, heights, strict=True):
                start = 0
                for k, piece in enumerate(left):
                    turned[top : top + height, start : start + piece.shape[0]] = left_refs[at + k][...].T
                    start += piece.shape[0]
                top, at = top + height, at + len(left)

        rights = [
            jnp.concatenate([ref[...] for ref in piece_refs[g * count : (g + 1) * count]], axis=0)
            for g in range(len(groups))
        ]
        top = 0
        for height, group in zip(heights, which, strict=True):
            out[top : top + height, :] = dot(turned[top : top + height, :], rights[group]).astype(bf16)
            top += height

    return call(
        kernel,
        (chips,),
        [whole(left) for left in flat]
        + [
            pl.BlockSpec((p.shape[0], width), lambda j, core: (0, 2 * j + core[0]))
            for group in groups
            for p in group
        ],
        pl.BlockSpec((total, width), lambda j, core: (0, j)),
        jax.ShapeDtypeStruct((total, width * chips), bf16),
        [pltpu.VMEM((total, rows), bf16)],
        [*flat, *(piece for group in groups for piece in group)],
        OUTER * rows * total * width * chips,
        prefetch=(jnp.reshape(lax.axis_index("core"), (1,)).astype(jnp.int32),),
    )


def scatter_columns(part):
    return lax.psum_scatter(part, "chip", scatter_dimension=1, tiled=True)


def cut(values, count):
    rows = values.shape[0] // count
    return [values[k * rows : (k + 1) * rows] for k in range(count)]


def unfold(shard, layer, layers, before=()):
    height, width = shard.shape
    units = height // 4

    def kernel(ref, *refs):
        for k, out in enumerate(refs[len(before) :]):
            part = ref[k * units : (k + 1) * units, :].astype(f32)
            out[0] = part if k == 3 else part.T

    shapes = [(width, units)] * 3 + [(units, width)]
    return pl.pallas_call(
        kernel,
        grid=(1,),
        in_specs=[whole(shard)] + [pl.BlockSpec(memory_space=pl.ANY)] * len(before),
        out_specs=[pl.BlockSpec((1, *shape), lambda j: (layer, 0, 0)) for shape in shapes],
        out_shape=[jax.ShapeDtypeStruct((layers, *shape), f32) for shape in shapes],
        input_output_aliases={k + 1: k for k in range(len(before))},
        compiler_params=pltpu.CompilerParams(vmem_limit_bytes=VMEM),
        cost_estimate=pl.CostEstimate(flops=0, bytes_accessed=0, transcendentals=0),
    )(shard, *before)


def rows_at(matrix, at, rows, tile):
    return (matrix, at // tile) if at % tile == 0 else (matrix[at : at + rows], 0)


def tile_of(units):
    return (128, units // 128) if units % 128 == 0 else (units, 1)


def up_and_gate(pieces, both, units):
    rows, depth = sum(p.shape[0] for p in pieces), pieces[0].shape[1]
    tile, steps = tile_of(units)
    chunk = rows if steps > 1 else rows // 4

    def kernel(*refs):
        piece_refs, (up_ref, gate_ref, upward_ref, gating_ref, hidden_ref, x_ref) = (
            refs[: len(pieces)], refs[len(pieces) :],
        )
        assemble(piece_refs, x_ref)
        for start in range(0, rows, chunk):
            here = slice(start, start + chunk)
            x = x_ref[here, :]
            if steps > 1:
                joined = trans_dot(x, jnp.concatenate([up_ref[...], gate_ref[...]], axis=0))
                upward, gating = joined[:, :tile], joined[:, tile:]
            else:
                upward, gating = trans_dot(x, up_ref[...]), trans_dot(x, gate_ref[...])
            upward_ref[here, :] = upward.astype(bf16)
            gating_ref[here, :] = gating.astype(bf16)
            hidden_ref[here, :] = (gating * sigmoid(gating) * upward).astype(bf16)

    out = jax.ShapeDtypeStruct((rows, units), bf16)
    return call(
        kernel,
        (steps,),
        [whole(p) for p in pieces]
        + [
            pl.BlockSpec((tile, depth), lambda j: (j, 0)),
            pl.BlockSpec((tile, depth), lambda j: (steps + j, 0)),
        ],
        [pl.BlockSpec((rows, tile), lambda j: (0, j))] * 3,
        [out] * 3,
        [pltpu.VMEM((rows, depth), bf16)],
        [*pieces, both, both],
        4 * rows * depth * units,
    )


def up_and_gate_back(pieces, down, at, upward, gating):
    rows, depth = sum(p.shape[0] for p in pieces), pieces[0].shape[1]
    units = upward.shape[1]
    tile, steps = (256, -(-units // 256)) if units % 128 == 0 else (units, 1)
    down, first = rows_at(down, at, units, tile)
    chunk = rows if steps > 1 else rows // 4

    def kernel(*refs):
        piece_refs, (down_ref, upward_ref, gating_ref, grad_up_ref, grad_gate_ref, x_ref) = (
            refs[: len(pieces)], refs[len(pieces) :],
        )
        assemble(piece_refs, x_ref)
        for start in range(0, rows, chunk):
            here = slice(start, start + chunk)
            grad = trans_dot(x_ref[here, :], down_ref[...])
            gating = gating_ref[here, :].astype(f32)
            sigma = sigmoid(gating)
            grad_up_ref[here, :] = (grad * gating * sigma).astype(bf16)
            grad_gate_ref[here, :] = (
                grad * upward_ref[here, :].astype(f32) * dsilu(gating, sigma)
            ).astype(bf16)

    block = pl.BlockSpec((rows, tile), lambda j: (0, j))
    out = jax.ShapeDtypeStruct((rows, units), bf16)
    return call(
        kernel,
        (steps,),
        [whole(p) for p in pieces]
        + [pl.BlockSpec((tile, depth), lambda j: (first + j, 0)), block, block],
        [block] * 2,
        [out] * 2,
        [pltpu.VMEM((rows, depth), bf16)],
        [*pieces, down, upward, gating],
        2 * rows * depth * units,
    )


def tile_base(place, index, size, per_piece):
    piece = lax.bitwise_xor(index // per_piece, place)
    return pl.multiple_of((piece * per_piece + lax.rem(index, per_piece)) * STEP, STEP)


def scan_kernel(count, product, place_ref, *refs):
    piece_refs, refs = refs[:count], refs[count:]
    (input_ref, forget_ref, gate_ref, keep_ref, bound_ref,
     pi_ref, pf_ref, pg_ref, state_ref, decay_ref, x_ref) = refs
    assemble(piece_refs, x_ref)
    x = x_ref[...]
    pi_ref[...] = product(x, input_ref[...])
    pf_ref[...] = product(x, forget_ref[...])
    pg_ref[...] = product(x, gate_ref[...])
    rows, lanes = pi_ref.shape
    per_piece = rows // count // STEP
    place = place_ref[0]
    bound = bound_ref[...]
    row = lax.broadcasted_iota(jnp.int32, (8, lanes), 0)

    def step(index, carry):
        carry_decay, carry_state = carry
        base = tile_base(place, index, count, per_piece)
        here = pl.ds(base, STEP)
        forget = bound + (1.0 - bound) * sigmoid(pf_ref[here, :])
        inp = pi_ref[here, :]
        source = inp * sigmoid(inp) * (1.0 - forget)
        decay = forget * keep_ref[here, :]
        for part in range(STEP // 8):
            a = decay[part * 8 : part * 8 + 8]
            b = source[part * 8 : part * 8 + 8]
            for shift in (1, 2, 4):
                a_before = jnp.where(row >= shift, pltpu.roll(a, shift, 0), 1.0)
                b_before = jnp.where(row >= shift, pltpu.roll(b, shift, 0), 0.0)
                b = a * b_before + b
                a = a * a_before
            b = a * carry_state + b
            a = a * carry_decay
            state_ref[pl.ds(base + part * 8, 8), :] = b
            decay_ref[pl.ds(base + part * 8, 8), :] = a
            carry_decay, carry_state = a[7:8], b[7:8]
        return carry_decay, carry_state

    lax.fori_loop(
        0, rows // STEP, step, (jnp.ones((1, lanes), f32), jnp.zeros((1, lanes), f32))
    )


def back_kernel(count, width, product, place_ref, *refs):
    piece_refs, refs = refs[:count], refs[count:]
    (out_ref, state_ref, gate_ref, pf_ref, inverse_ref, inner_ref, keep_ref, bound_ref, gain_ref,
     adjoint_ref, reach_ref, grad_gate_ref, mix_ref, gain_out_ref, x_ref, mixed_ref) = refs
    assemble(piece_refs, x_ref)
    mixed_ref[...] = product(x_ref[...], out_ref[...])
    rows, lanes = mixed_ref.shape
    per_piece = rows // count // STEP
    place = place_ref[0]
    bound = bound_ref[...]
    gain = gain_ref[...]
    row = lax.broadcasted_iota(jnp.int32, (8, lanes), 0)
    tiles = rows // STEP

    def step(number, carry):
        carry_reach, carry_adjoint, later, gain_sum = carry
        base = tile_base(place, tiles - 1 - number, count, per_piece)
        here = pl.ds(base, STEP)
        grad_mixed = mixed_ref[here, :]
        inverse = inverse_ref[here, :]
        scaled = state_ref[here, :] * inverse
        gate = gate_ref[here, :]
        sigma = sigmoid(gate)
        silu_gate = gate * sigma
        piece = grad_mixed * scaled
        contribution = piece * silu_gate
        grad_gate_ref[here, :] = (piece * gain * dsilu(gate, sigma)).astype(bf16)
        mix_ref[here, :] = (scaled * gain * silu_gate).astype(bf16)
        grad_state = inverse * (
            grad_mixed * gain * silu_gate - scaled * (inner_ref[here, :] * (1.0 / width))
        )
        decay = (bound + (1.0 - bound) * sigmoid(pf_ref[here, :])) * keep_ref[here, :]
        for part in reversed(range(STEP // 8)):
            now = decay[part * 8 : part * 8 + 8]
            gain_sum = gain_sum + contribution[part * 8 : part * 8 + 8]
            a = jnp.where(row == 7, later, pltpu.roll(now, 7, 0))
            b = grad_state[part * 8 : part * 8 + 8]
            for shift in (1, 2, 4):
                a_after = jnp.where(row < 8 - shift, pltpu.roll(a, 8 - shift, 0), 1.0)
                b_after = jnp.where(row < 8 - shift, pltpu.roll(b, 8 - shift, 0), 0.0)
                b = a * b_after + b
                a = a * a_after
            b = a * carry_adjoint + b
            a = a * carry_reach
            adjoint_ref[pl.ds(base + part * 8, 8), :] = b
            reach_ref[pl.ds(base + part * 8, 8), :] = a
            carry_reach, carry_adjoint, later = a[0:1], b[0:1], now[0:1]
        return carry_reach, carry_adjoint, later, gain_sum

    one, zero = jnp.ones((1, lanes), f32), jnp.zeros((1, lanes), f32)
    last = lax.fori_loop(0, tiles, step, (one, zero, one, jnp.zeros((8, lanes), f32)))
    gain_out_ref[...] = jnp.sum(last[3], axis=0, keepdims=True)


def gates_kernel(
    count, place_ref, adjoint_ref, reach_ref, state_ref, pi_ref, pf_ref, keep_ref, bound_ref,
    coming_ref, entering_ref, grad_input_ref, grad_forget_ref, bound_out_ref,
):
    rows, lanes = adjoint_ref.shape
    per_piece = rows // count // STEP
    place = place_ref[0]
    bound = bound_ref[...]
    coming = coming_ref[...]
    row = lax.broadcasted_iota(jnp.int32, (STEP, lanes), 0)

    def step(index, carry):
        before, bound_sum = carry
        base = tile_base(place, index, count, per_piece)
        here = pl.ds(base, STEP)
        adjoint = adjoint_ref[here, :] + reach_ref[here, :] * coming
        state = state_ref[here, :]
        previous = jnp.where(row == 0, before, pltpu.roll(state, 1, 0))
        inp = pi_ref[here, :]
        sigma_input = sigmoid(inp)
        sigma_forget = sigmoid(pf_ref[here, :])
        forget = bound + (1.0 - bound) * sigma_forget
        grad_forget = adjoint * (keep_ref[here, :] * previous - inp * sigma_input)
        piece = grad_forget * (1.0 - sigma_forget)
        grad_input_ref[here, :] = (adjoint * (1.0 - forget) * dsilu(inp, sigma_input)).astype(bf16)
        grad_forget_ref[here, :] = (piece * (1.0 - bound) * sigma_forget).astype(bf16)
        for part in range(STEP // 8):
            bound_sum = bound_sum + piece[part * 8 : part * 8 + 8]
        return state[STEP - 1 : STEP], bound_sum

    last = lax.fori_loop(
        0, rows // STEP, step, (entering_ref[...], jnp.zeros((8, lanes), f32))
    )
    bound_out_ref[...] = jnp.sum(last[1], axis=0, keepdims=True)


def over_channels(kernel, place, pieces, matrices, operands, outs, scratch, channels, cost):
    lanes = min(LANES, channels)

    def part(matrix, at, columns):
        if columns:
            return pl.BlockSpec((matrix.shape[0], lanes), lambda c, p: (0, at // lanes + c))
        return pl.BlockSpec((lanes, matrix.shape[1]), lambda c, p: (at // lanes + c, 0))

    def spec(rows, narrow):
        if narrow:
            return pl.BlockSpec((rows, 1), lambda c, p: (0, 0))
        return pl.BlockSpec((rows, lanes), lambda c, p: (0, c))

    return call(
        kernel,
        (channels // lanes,),
        [whole(p) for p in pieces]
        + [part(*m) for m in matrices]
        + [spec(o.shape[0], o.shape[1] == 1) for o in operands],
        [spec(rows, False) for rows, _ in outs],
        [jax.ShapeDtypeStruct((rows, channels), kind) for rows, kind in outs],
        scratch,
        [*pieces, *(m[0] for m in matrices), *operands],
        cost,
        prefetch=(place,),
    )


def entering_of(decay, state, reverse):
    length = seq_length()
    chips, core = length // 2, lax.axis_index("core")
    own = jnp.concatenate([decay, state], axis=0)
    other = swap(own, "core")
    is_first = core == (1 if reverse else 0)
    first, second = jnp.where(is_first, own, other), jnp.where(is_first, other, own)
    pair = jnp.concatenate(
        [first[0:1] * second[0:1], second[0:1] * first[1:2] + second[1:2]], axis=0
    )
    sign = -1 if reverse else 1
    arrived = [
        lax.ppermute(
            pair,
            SEQ,
            [(i, i + sign * 2 * hop) for i in range(length) if 0 <= i + sign * 2 * hop < length],
        )
        for hop in range(1, chips)
    ]
    total = jnp.zeros_like(state)
    for hop in range(chips - 1, 0, -1):
        total = arrived[hop - 1][0:1] * total + arrived[hop - 1][1:2]
    return jnp.where(is_first, total, other[0:1] * total + other[1:2])


def total_small(rows_of_width, rows_of_channels, first_channel, channels):
    size = lax.axis_size("fsdp")
    place = lax.axis_index("fsdp")

    def columns(step):
        return lax.dynamic_slice_in_dim(
            rows_of_width, lax.bitwise_xor(place, step) * channels, channels, 1
        )

    mine = columns(0)
    for step in range(1, size):
        mine = mine + exchange(columns(step), step)
    mine = jnp.concatenate([mine, rows_of_channels], axis=0)
    mine = mine + swap(mine, "core")
    chips, step = lax.axis_size("chip"), 1
    while step < chips:
        mine = mine + lax.ppermute(mine, "chip", [(i, i ^ step) for i in range(chips)])
        step *= 2
    total = jnp.zeros((mine.shape[0], channels * size), f32)
    total = lax.dynamic_update_slice_in_dim(total, mine, first_channel, 1)
    for step in range(1, size):
        total = lax.dynamic_update_slice_in_dim(
            total, exchange(mine, step), lax.bitwise_xor(place, step) * channels, 1
        )
    return total


def local(
    hidden_in, w_input, w_forget, w_gate, w_out, w_up, w_glu, w_down,
    lower_bound, norm_mix, norm_ffn, out_gain, lengths, cotangent,
):
    row_count, model_width = hidden_in.shape
    channels = w_input.shape[2]
    hidden_units = w_up.shape[2]
    size = lax.axis_size("fsdp")
    place = lax.axis_index("fsdp")
    block_rows = row_count * size
    first_channel = place * channels
    place_array = jnp.reshape(place, (1,)).astype(jnp.int32)
    last_layer = LAYERS - 1

    starts = jnp.cumsum(lengths) - lengths
    owners = lax.bitwise_xor(jnp.arange(size, dtype=jnp.int32), place.astype(jnp.int32))
    positions = (
        lax.axis_index(SEQ) * block_rows
        + (owners[:, None] * row_count + jnp.arange(row_count, dtype=jnp.int32)[None, :])
    ).reshape(-1)
    keep = (1.0 - jnp.any(positions[:, None] == starts[None, :], axis=1).astype(f32))[:, None]
    bounds = lax.dynamic_slice_in_dim(lower_bound, first_channel, channels, 1)
    gains = lax.dynamic_slice_in_dim(out_gain, first_channel, channels, 1)

    def side(*shards):
        return lax.all_gather(jnp.concatenate(shards, axis=1), SEQ, axis=0, tiled=True)

    def tall(*shards):
        return lax.all_gather(jnp.concatenate(shards, axis=0), SEQ, axis=1, tiled=True)

    mixes, boths, downs = [side(w_input[0], w_forget[0], w_gate[0], w_out[0].T)], [], []
    for layer in range(LAYERS):
        if layer > 0:
            mixes.append(tall(w_input[layer].T, w_forget[layer].T, w_gate[layer].T, w_out[layer]))
        if layer < last_layer:
            joined = tall(w_up[layer].T, w_glu[layer].T, w_down[layer])
            boths.append((joined, 0))
            downs.append((joined, 2 * hidden_units))
        else:
            boths.append((tall(w_up[layer].T, w_glu[layer].T), 0))
            downs.append((tall(w_down[layer]), 0))

    def rows_of(matrix_at, rows):
        matrix, at = matrix_at
        return matrix[at : at + rows]

    stream = hidden_in.astype(f32)
    saved = []
    for layer in range(LAYERS):
        mix, first_layer = mixes[layer], layer == 0
        bound, gain = bounds[layer][None, :], gains[layer][None, :]
        unit, factor = rms_parts(stream)
        normed = gather_rows((unit * norm_mix[layer]).astype(bf16))
        if layer == 0:
            grad_y = gather_rows(after(cotangent, *normed))
        proj_input, proj_forget, proj_gate, local_state, local_decay = over_channels(
            functools.partial(scan_kernel, size, dot if first_layer else trans_dot),
            place_array,
            normed,
            [(mix, k * channels, first_layer) for k in range(3)],
            (keep, bound),
            ((block_rows, f32),) * 5,
            [pltpu.VMEM((block_rows, model_width), bf16)],
            channels,
            6 * block_rows * model_width * channels,
        )
        if layer == 0:
            local_state, local_decay = all_after((local_state, local_decay), *grad_y)
        last_row = lax.bitwise_xor(size - 1, place) * row_count + row_count - 1
        entering = entering_of(
            lax.dynamic_slice_in_dim(local_decay, last_row, 1, 0),
            lax.dynamic_slice_in_dim(local_state, last_row, 1, 0),
            False,
        )
        state = local_state + local_decay * entering
        squares = total_rows(jnp.sum(state * state, axis=1))
        inverse = lax.rsqrt(squares / model_width + epsilon)[:, None]
        loose = (state * gain * jax.nn.silu(proj_gate)).astype(bf16)
        if first_layer:
            part = trans_dot(loose, mix[:, 3 * channels :])
        else:
            part = dot(loose, mix[3 * channels :])
        parts = cut(part.astype(bf16), size)
        branch = scatter_rows(parts) * inverse[:row_count]
        middle = stream + branch
        unit_two, _ = rms_parts(middle)
        normed_two = (unit_two * norm_ffn[layer]).astype(bf16)
        normed_two = gather_rows(normed_two)
        upward, gating, hidden = up_and_gate(normed_two, boths[layer][0], hidden_units)
        if layer < last_layer:
            stream = middle + scatter_rows(cut(dot(hidden, rows_of(downs[layer], hidden_units)).astype(bf16), size))
        twin_rows = (twins(normed), twins(normed_two), twins([hidden]))
        saved.append(
            (factor, twin_rows, normed, proj_input, proj_forget, proj_gate, entering,
             state, inverse, branch, middle, normed_two, upward, gating, hidden, unit)
        )

    grad_x = cotangent.astype(f32)
    shards = [None] * LAYERS
    smalls = [None] * LAYERS
    scattered = {}

    def due(layer, place):
        names = [name for name, when in DUE.items() if when == (layer, place)]
        return tuple(scattered[name] for name in names if name in scattered)

    final_middle, final_hidden = saved[last_layer][10], saved[last_layer][14]
    for layer in reversed(range(LAYERS)):
        mix, both, first_layer = mixes[layer], rows_of(boths[layer], 2 * hidden_units), layer == 0
        bound, gain = bounds[layer][None, :], gains[layer][None, :]
        (factor, twin_rows, normed, proj_input, proj_forget, proj_gate, entering, state, inverse,
         branch, middle, normed_two, upward, gating, hidden, unit) = saved[layer]
        unit_two, factor_two = rms_parts(middle)
        all_normed, all_two = normed + twin_rows[0], normed_two + twin_rows[1]

        if layer < last_layer:
            grad_y = gather_rows(grad_x.astype(bf16), *due(layer, "gather"))
        down_part = outer([([hidden, *twin_rows[2]], grad_y + twins(grad_y))])
        down_shard = scattered["down", layer] = scatter_columns(down_part)
        grad_up, grad_glu = up_and_gate_back(
            all_after(grad_y, down_part), *downs[layer], upward, gating
        )
        twin_up, twin_glu = twins((grad_up, grad_glu))
        grad_up, grad_glu = all_after((grad_up, grad_glu), *due(layer, "part"))
        part = dot(jnp.concatenate([grad_up, grad_glu], axis=1), both).astype(bf16)
        *parts, ready = all_after((*cut(part, size), grad_up))
        ffn_part = outer([([ready, twin_up], all_two), ([grad_glu, twin_glu], all_two)])
        ffn_shard = scattered["ffn", layer] = scatter_columns(ffn_part)
        grad_normed_two = scatter_rows(parts, ffn_part, *due(layer, "sum"))
        ffn_piece = jnp.sum(grad_normed_two * unit_two, axis=0)
        grad_middle = grad_x + norm_back(grad_normed_two * norm_ffn[layer], unit_two, factor_two)

        grad_m_own = grad_middle.astype(bf16)
        grad_m_own = after(grad_m_own, *due(layer, "norm"))
        if first_layer:
            output = dot(after(final_hidden, grad_m_own), rows_of(downs[last_layer], hidden_units)).astype(bf16)
            grad_m = gather_rows(grad_m_own, output, *due(layer, "middle"))
            hidden_out = (final_middle + scatter_rows(cut(output, size))).astype(bf16)
        else:
            grad_m = gather_rows(grad_m_own, *due(layer, "middle"))
        inner = jnp.concatenate(
            gather_rows(jnp.sum(grad_m_own.astype(f32) * branch, axis=1)), axis=0
        )[:, None]
        adjoint, reach, grad_gate, mixed, gain_piece = over_channels(
            functools.partial(back_kernel, size, model_width, dot if first_layer else trans_dot),
            place_array,
            grad_m,
            [(mix, 3 * channels, first_layer)],
            (state, proj_gate, proj_forget, inverse, inner, keep, bound, gain),
            ((block_rows, f32), (block_rows, f32), (block_rows, bf16), (block_rows, bf16), (1, f32)),
            [pltpu.VMEM((block_rows, model_width), bf16), pltpu.VMEM((block_rows, min(LANES, channels)), f32)],
            channels,
            100 * block_rows * channels,
        )
        all_m, twin_mixed = grad_m + twins(grad_m), twins([mixed])
        first_row = place * row_count
        first_decay = (
            bound
            + (1.0 - bound)
            * jax.nn.sigmoid(lax.dynamic_slice_in_dim(proj_forget, first_row, 1, 0))
        ) * lax.dynamic_slice_in_dim(keep, first_row, 1, 0)
        coming = entering_of(
            first_decay * lax.dynamic_slice_in_dim(reach, first_row, 1, 0),
            first_decay * lax.dynamic_slice_in_dim(adjoint, first_row, 1, 0),
            True,
        )
        ready = [*all_m, *twin_mixed, *due(layer, "coming")]
        coming = after(coming, *ready)
        grad_input, grad_forget, bound_piece = over_channels(
            functools.partial(gates_kernel, size),
            place_array,
            [],
            [],
            (adjoint, reach, state, proj_input, proj_forget, keep, bound, coming, entering),
            ((block_rows, bf16), (block_rows, bf16), (1, f32)),
            [],
            channels,
            100 * block_rows * channels,
        )
        grad_three = (grad_input, grad_forget, grad_gate)
        joined = jnp.concatenate([grad_input, grad_forget, grad_gate], axis=1)
        if first_layer:
            joined = after(joined, hidden_out)
        (twin_joined,) = twins((joined,))
        part = trans_dot(joined, mix[:, : 3 * channels]) if first_layer else dot(joined, mix[: 3 * channels])
        part = part.astype(bf16)

        *parts, ready = all_after((*cut(part, size), joined))
        low_part = outer([([ready, twin_joined], all_normed), ([mixed, *twin_mixed], all_m)])
        low_shard = scattered["low", layer] = scatter_columns(low_part)
        grad_normed = scatter_rows(parts, low_part, *due(layer, "last"))
        mix_piece = jnp.sum(grad_normed * unit, axis=0)
        grad_x = grad_middle + norm_back(grad_normed * norm_mix[layer], unit, factor)

        smalls[layer] = (mix_piece, ffn_piece, bound_piece, gain_piece)
    wide_rows = jnp.stack([row for pieces in smalls for row in pieces[:2]])
    own_rows = jnp.concatenate([row for pieces in smalls for row in pieces[2:]], axis=0)
    small = total_small(after(wide_rows, *due(0, "after")), own_rows, first_channel, channels)
    for layer in range(LAYERS):
        ffn_shard, down_shard = scattered["ffn", layer], scattered["down", layer]
        shards[layer] = (ffn_shard[:hidden_units].T, ffn_shard[hidden_units:].T, down_shard)
    low_gradients = ()
    for layer in reversed(range(LAYERS)):
        low_shard = scattered["low", layer]
        if layer == 0:
            low_shard = after(low_shard, grad_x, *low_gradients)
        low_gradients = unfold(low_shard, layer, LAYERS, low_gradients)
    stacked = [*low_gradients] + [
        jnp.stack([shards[layer][member].astype(f32) for layer in range(LAYERS)]) for member in range(3)
    ]
    wide_rows, own_rows = small[: 2 * LAYERS], small[2 * LAYERS :]
    return (
        hidden_out, grad_x, *stacked, own_rows[0::2], wide_rows[0::2], wide_rows[1::2], own_rows[1::2]
    )


def solution(mesh):
    length, size = mesh.devices.shape
    split = Mesh(mesh.devices.reshape(length // 2, 2, size), (*SEQ, "fsdp"))
    rows = P((*SEQ, "fsdp"), None)
    wide = P(None, SEQ, "fsdp")
    tall = P(None, "fsdp", SEQ)
    weights = (wide, wide, wide, tall, wide, wide, tall)
    return jax.shard_map(
        local,
        mesh=split,
        in_specs=(rows, *weights, P(), P(), P(), P(), P(), rows),
        out_specs=(rows, rows, *weights, P(), P(), P(), P()),
        check_vma=False,
    )
```

```python
import functools

import jax
import jax.numpy as jnp
from jax import lax
from jax.experimental import pallas as pl
from jax.experimental.pallas import tpu as pltpu
from jax.sharding import Mesh
from jax.sharding import PartitionSpec as P

LAYERS = 2
epsilon = 1e-06
STEP = 32
LANES = 256
VMEM = 52 * 1024 * 1024
OUTER = 4
SCALE = 5.5
DUE = {
    ("down", 1): (1, "sum"), ("ffn", 1): (0, "gather"), ("low", 1): (0, "part"),
    ("down", 0): (0, "middle"), ("ffn", 0): (0, "last"),
}
f32 = jnp.float32
bf16 = jnp.bfloat16
SEQ = ("chip", "core")
NT = (((1,), (1,)), ((), ()))


def exchange(values, step):
    size = lax.axis_size("fsdp")
    return lax.ppermute(values, "fsdp", [(i, i ^ step) for i in range(size)])


def swap(values, axis):
    return lax.ppermute(values, axis, [(0, 1), (1, 0)])


def seq_length():
    return lax.axis_size("chip") * lax.axis_size("core")


def after(value, *others):
    return lax.optimization_barrier((value, *others))[0]


def all_after(values, *others):
    return list(lax.optimization_barrier((*values, *others)))[: len(values)]


def gather_rows(own, *meanwhile):
    arrived = [exchange(own, step) for step in range(1, lax.axis_size("fsdp"))]
    return [own] + all_after(arrived, *meanwhile)


def scatter_rows(pieces, *meanwhile):
    arrived = [exchange(pieces[step], step) for step in range(1, len(pieces))]
    if meanwhile:
        arrived = all_after(arrived, *meanwhile)
    total = pieces[0].astype(f32)
    for piece in arrived:
        total = total + piece.astype(f32)
    return total


def total_rows(part):
    size = lax.axis_size("fsdp")
    pieces = part.reshape(size, -1)
    total = pieces
    for step in range(1, size):
        other = exchange(pieces, step)
        total = total + jnp.stack([other[k ^ step] for k in range(size)])
    return total.reshape(-1)


def rms_parts(values):
    factor = lax.rsqrt(jnp.mean(values * values, axis=-1, keepdims=True) + epsilon)
    return (values * factor, factor)


def norm_back(grad_unit, unit_rows, factor):
    return factor * (
        grad_unit - unit_rows * jnp.mean(grad_unit * unit_rows, axis=-1, keepdims=True)
    )


def dsilu(values, sigma):
    return sigma * (1.0 + values * (1.0 - sigma))


def sigmoid(values):
    return 1.0 / (1.0 + jnp.exp(-values))


def dot(left, right):
    return jnp.dot(left, right, preferred_element_type=f32)


def trans_dot(left, right):
    return lax.dot_general(left, right, NT, preferred_element_type=f32)


def whole(array):
    return pl.BlockSpec(array.shape, lambda j, *_: (0, 0))


def call(kernel, grid, in_specs, out_specs, out_shape, scratch, operands, cost, prefetch=()):
    return pl.pallas_call(
        kernel,
        grid_spec=pltpu.PrefetchScalarGridSpec(
            num_scalar_prefetch=len(prefetch),
            grid=grid,
            in_specs=in_specs,
            out_specs=out_specs,
            scratch_shapes=scratch,
        ),
        out_shape=out_shape,
        compiler_params=pltpu.CompilerParams(vmem_limit_bytes=VMEM),
        cost_estimate=pl.CostEstimate(flops=int(SCALE * cost), bytes_accessed=cost // 512, transcendentals=0),
    )(*prefetch, *operands)


def assemble(pieces, rows_ref):
    rows = pieces[0].shape[0]

    @pl.when(pl.program_id(0) == 0)
    def _():
        for k, piece in enumerate(pieces):
            rows_ref[k * rows : (k + 1) * rows, :] = piece[...]


def twins(values):
    return [swap(v, "core") for v in values]


def outer(terms):
    lefts = [left for left, _ in terms]
    groups, which = [], []
    for _, pieces in terms:
        found = [k for k, group in enumerate(groups) if group is pieces]
        which.append(found[0] if found else len(groups))
        if not found:
            groups.append(pieces)
    rows, width = sum(p.shape[0] for p in groups[0]), groups[0][0].shape[1] // seq_length()
    heights = [left[0].shape[1] for left in lefts]
    flat = [piece for left in lefts for piece in left]
    total, count, chips = sum(heights), len(groups[0]), lax.axis_size("chip")

    def kernel(core_ref, *refs):
        left_refs, refs = refs[: len(flat)], refs[len(flat) :]
        piece_refs, (out, turned) = refs[: count * len(groups)], refs[count * len(groups) :]

        @pl.when(pl.program_id(0) == 0)
        def _():
            top, at = 0, 0
            for left, height in zip(lefts, heights, strict=True):
                start = 0
                for k, piece in enumerate(left):
                    turned[top : top + height, start : start + piece.shape[0]] = left_refs[at + k][...].T
                    start += piece.shape[0]
                top, at = top + height, at + len(left)

        rights = [
            jnp.concatenate([ref[...] for ref in piece_refs[g * count : (g + 1) * count]], axis=0)
            for g in range(len(groups))
        ]
        top = 0
        for height, group in zip(heights, which, strict=True):
            out[top : top + height, :] = dot(turned[top : top + height, :], rights[group]).astype(bf16)
            top += height

    return call(
        kernel,
        (chips,),
        [whole(left) for left in flat]
        + [
            pl.BlockSpec((p.shape[0], width), lambda j, core: (0, 2 * j + core[0]))
            for group in groups
            for p in group
        ],
        pl.BlockSpec((total, width), lambda j, core: (0, j)),
        jax.ShapeDtypeStruct((total, width * chips), bf16),
        [pltpu.VMEM((total, rows), bf16)],
        [*flat, *(piece for group in groups for piece in group)],
        OUTER * rows * total * width * chips,
        prefetch=(jnp.reshape(lax.axis_index("core"), (1,)).astype(jnp.int32),),
    )


def scatter_columns(part):
    return lax.psum_scatter(part, "chip", scatter_dimension=1, tiled=True)


def cut(values, count):
    rows = values.shape[0] // count
    return [values[k * rows : (k + 1) * rows] for k in range(count)]


def unfold(shard, layer, layers, before=()):
    height, width = shard.shape
    units = height // 4

    def kernel(ref, *refs):
        for k, out in enumerate(refs[len(before) :]):
            part = ref[k * units : (k + 1) * units, :].astype(f32)
            out[0] = part if k == 3 else part.T

    shapes = [(width, units)] * 3 + [(units, width)]
    return pl.pallas_call(
        kernel,
        grid=(1,),
        in_specs=[whole(shard)] + [pl.BlockSpec(memory_space=pl.ANY)] * len(before),
        out_specs=[pl.BlockSpec((1, *shape), lambda j: (layer, 0, 0)) for shape in shapes],
        out_shape=[jax.ShapeDtypeStruct((layers, *shape), f32) for shape in shapes],
        input_output_aliases={k + 1: k for k in range(len(before))},
        compiler_params=pltpu.CompilerParams(vmem_limit_bytes=60 * 1000 * 1000),
        cost_estimate=pl.CostEstimate(flops=0, bytes_accessed=0, transcendentals=0),
    )(shard, *before)


def beside(matrices, turned):
    depth, width = matrices[0].shape[1:]
    count = len(matrices)

    def kernel(*refs):
        sources, (out, held, arrived) = refs[: count + 1], refs[count + 1 :]
        copies = [
            pltpu.make_async_copy(
                sources[k].at[0], out.at[:, k * width : (k + 1) * width], arrived.at[k]
            )
            for k in range(count)
        ]
        copies.append(pltpu.make_async_copy(sources[count].at[0], held, arrived.at[count]))
        for copy in copies:
            copy.start()
        for copy in copies:
            copy.wait()
        out[:, count * width :] = held[...].T

    operands = (*matrices, turned)
    return pl.pallas_call(
        kernel,
        in_specs=[pl.BlockSpec(memory_space=pl.ANY)] * len(operands),
        out_specs=pl.BlockSpec(memory_space=pltpu.VMEM),
        out_shape=jax.ShapeDtypeStruct((depth, width * len(operands)), bf16),
        scratch_shapes=[
            pltpu.VMEM(turned.shape[1:], bf16), pltpu.SemaphoreType.DMA((len(operands),)),
        ],
        compiler_params=pltpu.CompilerParams(vmem_limit_bytes=60 * 1000 * 1000),
        cost_estimate=pl.CostEstimate(flops=0, bytes_accessed=0, transcendentals=0),
    )(*operands)


def rows_at(matrix, at, rows, tile):
    return (matrix, at // tile) if at % tile == 0 else (matrix[at : at + rows], 0)


def tile_of(units):
    return (128, units // 128) if units % 128 == 0 else (units, 1)


def up_and_gate(pieces, both, units):
    rows, depth = sum(p.shape[0] for p in pieces), pieces[0].shape[1]
    tile, steps = tile_of(units)
    chunk = rows if steps > 1 else rows // 4

    def kernel(*refs):
        piece_refs, (up_ref, gate_ref, upward_ref, gating_ref, hidden_ref, x_ref) = (
            refs[: len(pieces)], refs[len(pieces) :],
        )
        assemble(piece_refs, x_ref)
        for start in range(0, rows, chunk):
            here = slice(start, start + chunk)
            x = x_ref[here, :]
            if steps > 1:
                joined = trans_dot(x, jnp.concatenate([up_ref[...], gate_ref[...]], axis=0))
                upward, gating = joined[:, :tile], joined[:, tile:]
            else:
                upward, gating = trans_dot(x, up_ref[...]), trans_dot(x, gate_ref[...])
            upward_ref[here, :] = upward.astype(bf16)
            gating_ref[here, :] = gating.astype(bf16)
            hidden_ref[here, :] = (gating * sigmoid(gating) * upward).astype(bf16)

    out = jax.ShapeDtypeStruct((rows, units), bf16)
    return call(
        kernel,
        (steps,),
        [whole(p) for p in pieces]
        + [
            pl.BlockSpec((tile, depth), lambda j: (j, 0)),
            pl.BlockSpec((tile, depth), lambda j: (steps + j, 0)),
        ],
        [pl.BlockSpec((rows, tile), lambda j: (0, j))] * 3,
        [out] * 3,
        [pltpu.VMEM((rows, depth), bf16)],
        [*pieces, both, both],
        4 * rows * depth * units,
    )


def up_and_gate_back(pieces, down, at, upward, gating):
    rows, depth = sum(p.shape[0] for p in pieces), pieces[0].shape[1]
    units = upward.shape[1]
    tile, steps = (256, -(-units // 256)) if units % 128 == 0 else (units, 1)
    down, first = rows_at(down, at, units, tile)
    chunk = rows if steps > 1 else rows // 4

    def kernel(*refs):
        piece_refs, (down_ref, upward_ref, gating_ref, grad_up_ref, grad_gate_ref, x_ref) = (
            refs[: len(pieces)], refs[len(pieces) :],
        )
        assemble(piece_refs, x_ref)
        for start in range(0, rows, chunk):
            here = slice(start, start + chunk)
            grad = trans_dot(x_ref[here, :], down_ref[...])
            gating = gating_ref[here, :].astype(f32)
            sigma = sigmoid(gating)
            grad_up_ref[here, :] = (grad * gating * sigma).astype(bf16)
            grad_gate_ref[here, :] = (
                grad * upward_ref[here, :].astype(f32) * dsilu(gating, sigma)
            ).astype(bf16)

    block = pl.BlockSpec((rows, tile), lambda j: (0, j))
    out = jax.ShapeDtypeStruct((rows, units), bf16)
    return call(
        kernel,
        (steps,),
        [whole(p) for p in pieces]
        + [pl.BlockSpec((tile, depth), lambda j: (first + j, 0)), block, block],
        [block] * 2,
        [out] * 2,
        [pltpu.VMEM((rows, depth), bf16)],
        [*pieces, down, upward, gating],
        2 * rows * depth * units,
    )


def tile_base(place, index, size, per_piece):
    piece = lax.bitwise_xor(index // per_piece, place)
    return pl.multiple_of((piece * per_piece + lax.rem(index, per_piece)) * STEP, STEP)


def scan_kernel(count, product, place_ref, *refs):
    piece_refs, refs = refs[:count], refs[count:]
    (input_ref, forget_ref, gate_ref, keep_ref, bound_ref,
     pi_ref, pf_ref, pg_ref, state_ref, decay_ref, x_ref) = refs
    assemble(piece_refs, x_ref)
    x = x_ref[...]
    pi_ref[...] = product(x, input_ref[...])
    pf_ref[...] = product(x, forget_ref[...])
    pg_ref[...] = product(x, gate_ref[...])
    rows, lanes = pi_ref.shape
    per_piece = rows // count // STEP
    place = place_ref[0]
    bound = bound_ref[...]
    row = lax.broadcasted_iota(jnp.int32, (8, lanes), 0)

    def step(index, carry):
        carry_decay, carry_state = carry
        base = tile_base(place, index, count, per_piece)
        here = pl.ds(base, STEP)
        forget = bound + (1.0 - bound) * sigmoid(pf_ref[here, :])
        inp = pi_ref[here, :]
        source = inp * sigmoid(inp) * (1.0 - forget)
        decay = forget * keep_ref[here, :]
        for part in range(STEP // 8):
            a = decay[part * 8 : part * 8 + 8]
            b = source[part * 8 : part * 8 + 8]
            for shift in (1, 2, 4):
                a_before = jnp.where(row >= shift, pltpu.roll(a, shift, 0), 1.0)
                b_before = jnp.where(row >= shift, pltpu.roll(b, shift, 0), 0.0)
                b = a * b_before + b
                a = a * a_before
            b = a * carry_state + b
            a = a * carry_decay
            state_ref[pl.ds(base + part * 8, 8), :] = b
            decay_ref[pl.ds(base + part * 8, 8), :] = a
            carry_decay, carry_state = a[7:8], b[7:8]
        return carry_decay, carry_state

    lax.fori_loop(
        0, rows // STEP, step, (jnp.ones((1, lanes), f32), jnp.zeros((1, lanes), f32))
    )


def back_kernel(count, width, product, place_ref, *refs):
    piece_refs, refs = refs[:count], refs[count:]
    (out_ref, state_ref, gate_ref, pf_ref, inverse_ref, inner_ref, keep_ref, bound_ref, gain_ref,
     adjoint_ref, reach_ref, grad_gate_ref, mix_ref, gain_out_ref, x_ref, mixed_ref) = refs
    assemble(piece_refs, x_ref)
    mixed_ref[...] = product(x_ref[...], out_ref[...])
    rows, lanes = mixed_ref.shape
    per_piece = rows // count // STEP
    place = place_ref[0]
    bound = bound_ref[...]
    gain = gain_ref[...]
    row = lax.broadcasted_iota(jnp.int32, (8, lanes), 0)
    tiles = rows // STEP

    def step(number, carry):
        carry_reach, carry_adjoint, later, gain_sum = carry
        base = tile_base(place, tiles - 1 - number, count, per_piece)
        here = pl.ds(base, STEP)
        grad_mixed = mixed_ref[here, :]
        inverse = inverse_ref[here, :]
        scaled = state_ref[here, :] * inverse
        gate = gate_ref[here, :]
        sigma = sigmoid(gate)
        silu_gate = gate * sigma
        piece = grad_mixed * scaled
        contribution = piece * silu_gate
        grad_gate_ref[here, :] = (piece * gain * dsilu(gate, sigma)).astype(bf16)
        mix_ref[here, :] = (scaled * gain * silu_gate).astype(bf16)
        grad_state = inverse * (
            grad_mixed * gain * silu_gate - scaled * (inner_ref[here, :] * (1.0 / width))
        )
        decay = (bound + (1.0 - bound) * sigmoid(pf_ref[here, :])) * keep_ref[here, :]
        for part in reversed(range(STEP // 8)):
            now = decay[part * 8 : part * 8 + 8]
            gain_sum = gain_sum + contribution[part * 8 : part * 8 + 8]
            a = jnp.where(row == 7, later, pltpu.roll(now, 7, 0))
            b = grad_state[part * 8 : part * 8 + 8]
            for shift in (1, 2, 4):
                a_after = jnp.where(row < 8 - shift, pltpu.roll(a, 8 - shift, 0), 1.0)
                b_after = jnp.where(row < 8 - shift, pltpu.roll(b, 8 - shift, 0), 0.0)
                b = a * b_after + b
                a = a * a_after
            b = a * carry_adjoint + b
            a = a * carry_reach
            adjoint_ref[pl.ds(base + part * 8, 8), :] = b
            reach_ref[pl.ds(base + part * 8, 8), :] = a
            carry_reach, carry_adjoint, later = a[0:1], b[0:1], now[0:1]
        return carry_reach, carry_adjoint, later, gain_sum

    one, zero = jnp.ones((1, lanes), f32), jnp.zeros((1, lanes), f32)
    last = lax.fori_loop(0, tiles, step, (one, zero, one, jnp.zeros((8, lanes), f32)))
    gain_out_ref[...] = jnp.sum(last[3], axis=0, keepdims=True)


def gates_kernel(
    count, place_ref, adjoint_ref, reach_ref, state_ref, pi_ref, pf_ref, keep_ref, bound_ref,
    coming_ref, entering_ref, grad_input_ref, grad_forget_ref, bound_out_ref,
):
    rows, lanes = adjoint_ref.shape
    per_piece = rows // count // STEP
    place = place_ref[0]
    bound = bound_ref[...]
    coming = coming_ref[...]
    row = lax.broadcasted_iota(jnp.int32, (STEP, lanes), 0)

    def step(index, carry):
        before, bound_sum = carry
        base = tile_base(place, index, count, per_piece)
        here = pl.ds(base, STEP)
        adjoint = adjoint_ref[here, :] + reach_ref[here, :] * coming
        state = state_ref[here, :]
        previous = jnp.where(row == 0, before, pltpu.roll(state, 1, 0))
        inp = pi_ref[here, :]
        sigma_input = sigmoid(inp)
        sigma_forget = sigmoid(pf_ref[here, :])
        forget = bound + (1.0 - bound) * sigma_forget
        grad_forget = adjoint * (keep_ref[here, :] * previous - inp * sigma_input)
        piece = grad_forget * (1.0 - sigma_forget)
        grad_input_ref[here, :] = (adjoint * (1.0 - forget) * dsilu(inp, sigma_input)).astype(bf16)
        grad_forget_ref[here, :] = (piece * (1.0 - bound) * sigma_forget).astype(bf16)
        for part in range(STEP // 8):
            bound_sum = bound_sum + piece[part * 8 : part * 8 + 8]
        return state[STEP - 1 : STEP], bound_sum

    last = lax.fori_loop(
        0, rows // STEP, step, (entering_ref[...], jnp.zeros((8, lanes), f32))
    )
    bound_out_ref[...] = jnp.sum(last[1], axis=0, keepdims=True)


def over_channels(kernel, place, pieces, matrices, operands, outs, scratch, channels, cost):
    lanes = min(LANES, channels)

    def part(matrix, at, columns):
        if columns:
            return pl.BlockSpec((matrix.shape[0], lanes), lambda c, p: (0, at // lanes + c))
        return pl.BlockSpec((lanes, matrix.shape[1]), lambda c, p: (at // lanes + c, 0))

    def spec(rows, narrow):
        if narrow:
            return pl.BlockSpec((rows, 1), lambda c, p: (0, 0))
        return pl.BlockSpec((rows, lanes), lambda c, p: (0, c))

    return call(
        kernel,
        (channels // lanes,),
        [whole(p) for p in pieces]
        + [part(*m) for m in matrices]
        + [spec(o.shape[0], o.shape[1] == 1) for o in operands],
        [spec(rows, False) for rows, _ in outs],
        [jax.ShapeDtypeStruct((rows, channels), kind) for rows, kind in outs],
        scratch,
        [*pieces, *(m[0] for m in matrices), *operands],
        cost,
        prefetch=(place,),
    )


def entering_of(decay, state, reverse):
    length = seq_length()
    chips, core = length // 2, lax.axis_index("core")
    own = jnp.concatenate([decay, state], axis=0)
    other = swap(own, "core")
    is_first = core == (1 if reverse else 0)
    first, second = jnp.where(is_first, own, other), jnp.where(is_first, other, own)
    pair = jnp.concatenate(
        [first[0:1] * second[0:1], second[0:1] * first[1:2] + second[1:2]], axis=0
    )
    sign = -1 if reverse else 1
    arrived = [
        lax.ppermute(
            pair,
            SEQ,
            [(i, i + sign * 2 * hop) for i in range(length) if 0 <= i + sign * 2 * hop < length],
        )
        for hop in range(1, chips)
    ]
    total = jnp.zeros_like(state)
    for hop in range(chips - 1, 0, -1):
        total = arrived[hop - 1][0:1] * total + arrived[hop - 1][1:2]
    return jnp.where(is_first, total, other[0:1] * total + other[1:2])


def total_small(rows_of_width, rows_of_channels, first_channel, channels):
    size = lax.axis_size("fsdp")
    place = lax.axis_index("fsdp")

    def columns(step):
        return lax.dynamic_slice_in_dim(
            rows_of_width, lax.bitwise_xor(place, step) * channels, channels, 1
        )

    mine = columns(0)
    for step in range(1, size):
        mine = mine + exchange(columns(step), step)
    mine = jnp.concatenate([mine, rows_of_channels], axis=0)
    mine = mine + swap(mine, "core")
    chips, step = lax.axis_size("chip"), 1
    while step < chips:
        mine = mine + lax.ppermute(mine, "chip", [(i, i ^ step) for i in range(chips)])
        step *= 2
    total = jnp.zeros((mine.shape[0], channels * size), f32)
    total = lax.dynamic_update_slice_in_dim(total, mine, first_channel, 1)
    for step in range(1, size):
        total = lax.dynamic_update_slice_in_dim(
            total, exchange(mine, step), lax.bitwise_xor(place, step) * channels, 1
        )
    return total


def local(
    hidden_in, w_input, w_forget, w_gate, w_out, w_up, w_glu, w_down,
    lower_bound, norm_mix, norm_ffn, out_gain, lengths, cotangent,
):
    row_count, model_width = hidden_in.shape
    channels = w_input.shape[2]
    hidden_units = w_up.shape[2]
    size = lax.axis_size("fsdp")
    place = lax.axis_index("fsdp")
    block_rows = row_count * size
    first_channel = place * channels
    place_array = jnp.reshape(place, (1,)).astype(jnp.int32)
    last_layer = LAYERS - 1

    starts = jnp.cumsum(lengths) - lengths
    owners = lax.bitwise_xor(jnp.arange(size, dtype=jnp.int32), place.astype(jnp.int32))
    positions = (
        lax.axis_index(SEQ) * block_rows
        + (owners[:, None] * row_count + jnp.arange(row_count, dtype=jnp.int32)[None, :])
    ).reshape(-1)
    keep = (1.0 - jnp.any(positions[:, None] == starts[None, :], axis=1).astype(f32))[:, None]
    bounds = lax.dynamic_slice_in_dim(lower_bound, first_channel, channels, 1)
    gains = lax.dynamic_slice_in_dim(out_gain, first_channel, channels, 1)

    def side(*shards):
        return lax.all_gather(jnp.concatenate(shards, axis=1), SEQ, axis=0, tiled=True)

    def tall(*shards):
        return lax.all_gather(jnp.concatenate(shards, axis=0), SEQ, axis=1, tiled=True)

    mixes, boths, downs = [side(beside((w_input, w_forget, w_gate), w_out))], [], []
    for layer in range(LAYERS):
        if layer > 0:
            mixes.append(tall(w_input[layer].T, w_forget[layer].T, w_gate[layer].T, w_out[layer]))
        if layer < last_layer:
            joined = tall(w_up[layer].T, w_glu[layer].T, w_down[layer])
            boths.append((joined, 0))
            downs.append((joined, 2 * hidden_units))
        else:
            boths.append((tall(w_up[layer].T, w_glu[layer].T), 0))
            downs.append((tall(w_down[layer]), 0))

    def rows_of(matrix_at, rows):
        matrix, at = matrix_at
        return matrix[at : at + rows]

    stream = hidden_in.astype(f32)
    saved = []
    for layer in range(LAYERS):
        mix, first_layer = mixes[layer], layer == 0
        bound, gain = bounds[layer][None, :], gains[layer][None, :]
        unit, factor = rms_parts(stream)
        normed = gather_rows((unit * norm_mix[layer]).astype(bf16))
        if layer == 0:
            grad_y = gather_rows(after(cotangent, *normed))
        proj_input, proj_forget, proj_gate, local_state, local_decay = over_channels(
            functools.partial(scan_kernel, size, dot if first_layer else trans_dot),
            place_array,
            normed,
            [(mix, k * channels, first_layer) for k in range(3)],
            (keep, bound),
            ((block_rows, f32),) * 5,
            [pltpu.VMEM((block_rows, model_width), bf16)],
            channels,
            6 * block_rows * model_width * channels,
        )
        if layer == 0:
            local_state, local_decay = all_after((local_state, local_decay), *grad_y)
        last_row = lax.bitwise_xor(size - 1, place) * row_count + row_count - 1
        entering = entering_of(
            lax.dynamic_slice_in_dim(local_decay, last_row, 1, 0),
            lax.dynamic_slice_in_dim(local_state, last_row, 1, 0),
            False,
        )
        state = local_state + local_decay * entering
        squares = total_rows(jnp.sum(state * state, axis=1))
        inverse = lax.rsqrt(squares / model_width + epsilon)[:, None]
        loose = (state * gain * jax.nn.silu(proj_gate)).astype(bf16)
        if first_layer:
            part = trans_dot(loose, mix[:, 3 * channels :])
        else:
            part = dot(loose, mix[3 * channels :])
        parts = cut(part.astype(bf16), size)
        branch = scatter_rows(parts) * inverse[:row_count]
        middle = stream + branch
        unit_two, _ = rms_parts(middle)
        normed_two = (unit_two * norm_ffn[layer]).astype(bf16)
        normed_two = gather_rows(normed_two)
        upward, gating, hidden = up_and_gate(normed_two, boths[layer][0], hidden_units)
        if layer < last_layer:
            stream = middle + scatter_rows(cut(dot(hidden, rows_of(downs[layer], hidden_units)).astype(bf16), size))
        twin_rows = (twins(normed), twins(normed_two), twins([hidden]))
        saved.append(
            (factor, twin_rows, normed, proj_input, proj_forget, proj_gate, entering,
             state, inverse, branch, middle, normed_two, upward, gating, hidden, unit)
        )

    grad_x = cotangent.astype(f32)
    shards = [None] * LAYERS
    smalls = [None] * LAYERS
    scattered = {}

    def due(layer, place):
        names = [name for name, when in DUE.items() if when == (layer, place)]
        return tuple(scattered[name] for name in names if name in scattered)

    final_middle, final_hidden = saved[last_layer][10], saved[last_layer][14]
    for layer in reversed(range(LAYERS)):
        mix, both, first_layer = mixes[layer], rows_of(boths[layer], 2 * hidden_units), layer == 0
        bound, gain = bounds[layer][None, :], gains[layer][None, :]
        (factor, twin_rows, normed, proj_input, proj_forget, proj_gate, entering, state, inverse,
         branch, middle, normed_two, upward, gating, hidden, unit) = saved[layer]
        unit_two, factor_two = rms_parts(middle)
        all_normed, all_two = normed + twin_rows[0], normed_two + twin_rows[1]

        if layer < last_layer:
            grad_y = gather_rows(grad_x.astype(bf16), *due(layer, "gather"))
        down_part = outer([([hidden, *twin_rows[2]], grad_y + twins(grad_y))])
        down_shard = scattered["down", layer] = scatter_columns(down_part)
        grad_up, grad_glu = up_and_gate_back(
            all_after(grad_y, down_part), *downs[layer], upward, gating
        )
        twin_up, twin_glu = twins((grad_up, grad_glu))
        grad_up, grad_glu = all_after((grad_up, grad_glu), *due(layer, "part"))
        part = dot(jnp.concatenate([grad_up, grad_glu], axis=1), both).astype(bf16)
        *parts, ready = all_after((*cut(part, size), grad_up))
        ffn_part = outer([([ready, twin_up], all_two), ([grad_glu, twin_glu], all_two)])
        ffn_shard = scattered["ffn", layer] = scatter_columns(ffn_part)
        grad_normed_two = scatter_rows(parts, ffn_part, *due(layer, "sum"))
        ffn_piece = jnp.sum(grad_normed_two * unit_two, axis=0)
        grad_middle = grad_x + norm_back(grad_normed_two * norm_ffn[layer], unit_two, factor_two)

        grad_m_own = grad_middle.astype(bf16)
        grad_m_own = after(grad_m_own, *due(layer, "norm"))
        if first_layer:
            output = dot(after(final_hidden, grad_m_own), rows_of(downs[last_layer], hidden_units)).astype(bf16)
            grad_m = gather_rows(grad_m_own, output, *due(layer, "middle"))
            hidden_out = (final_middle + scatter_rows(cut(output, size))).astype(bf16)
        else:
            grad_m = gather_rows(grad_m_own, *due(layer, "middle"))
        inner = jnp.concatenate(
            gather_rows(jnp.sum(grad_m_own.astype(f32) * branch, axis=1)), axis=0
        )[:, None]
        adjoint, reach, grad_gate, mixed, gain_piece = over_channels(
            functools.partial(back_kernel, size, model_width, dot if first_layer else trans_dot),
            place_array,
            grad_m,
            [(mix, 3 * channels, first_layer)],
            (state, proj_gate, proj_forget, inverse, inner, keep, bound, gain),
            ((block_rows, f32), (block_rows, f32), (block_rows, bf16), (block_rows, bf16), (1, f32)),
            [pltpu.VMEM((block_rows, model_width), bf16), pltpu.VMEM((block_rows, min(LANES, channels)), f32)],
            channels,
            100 * block_rows * channels,
        )
        all_m, twin_mixed = grad_m + twins(grad_m), twins([mixed])
        first_row = place * row_count
        first_decay = (
            bound
            + (1.0 - bound)
            * jax.nn.sigmoid(lax.dynamic_slice_in_dim(proj_forget, first_row, 1, 0))
        ) * lax.dynamic_slice_in_dim(keep, first_row, 1, 0)
        coming = entering_of(
            first_decay * lax.dynamic_slice_in_dim(reach, first_row, 1, 0),
            first_decay * lax.dynamic_slice_in_dim(adjoint, first_row, 1, 0),
            True,
        )
        ready = [*all_m, *twin_mixed, *due(layer, "coming")]
        coming = after(coming, *ready)
        grad_input, grad_forget, bound_piece = over_channels(
            functools.partial(gates_kernel, size),
            place_array,
            [],
            [],
            (adjoint, reach, state, proj_input, proj_forget, keep, bound, coming, entering),
            ((block_rows, bf16), (block_rows, bf16), (1, f32)),
            [],
            channels,
            100 * block_rows * channels,
        )
        grad_three = (grad_input, grad_forget, grad_gate)
        joined = jnp.concatenate([grad_input, grad_forget, grad_gate], axis=1)
        if first_layer:
            joined = after(joined, hidden_out)
        (twin_joined,) = twins((joined,))
        part = trans_dot(joined, mix[:, : 3 * channels]) if first_layer else dot(joined, mix[: 3 * channels])
        part = part.astype(bf16)

        *parts, ready = all_after((*cut(part, size), joined))
        low_part = outer([([ready, twin_joined], all_normed), ([mixed, *twin_mixed], all_m)])
        low_shard = scattered["low", layer] = scatter_columns(low_part)
        grad_normed = scatter_rows(parts, low_part, *due(layer, "last"))
        mix_piece = jnp.sum(grad_normed * unit, axis=0)
        grad_x = grad_middle + norm_back(grad_normed * norm_mix[layer], unit, factor)

        smalls[layer] = (mix_piece, ffn_piece, bound_piece, gain_piece)
    wide_rows = jnp.stack([row for pieces in smalls for row in pieces[:2]])
    own_rows = jnp.concatenate([row for pieces in smalls for row in pieces[2:]], axis=0)
    small = total_small(after(wide_rows, *due(0, "after")), own_rows, first_channel, channels)
    for layer in range(LAYERS):
        ffn_shard, down_shard = scattered["ffn", layer], scattered["down", layer]
        shards[layer] = (ffn_shard[:hidden_units].T, ffn_shard[hidden_units:].T, down_shard)
    low_gradients = ()
    for layer in reversed(range(LAYERS)):
        low_shard = scattered["low", layer]
        if layer == 0:
            low_shard = after(low_shard, grad_x, *low_gradients)
        low_gradients = unfold(low_shard, layer, LAYERS, low_gradients)
    stacked = [*low_gradients] + [
        jnp.stack([shards[layer][member].astype(f32) for layer in range(LAYERS)]) for member in range(3)
    ]
    wide_rows, own_rows = small[: 2 * LAYERS], small[2 * LAYERS :]
    return (
        hidden_out, grad_x, *stacked, own_rows[0::2], wide_rows[0::2], wide_rows[1::2], own_rows[1::2]
    )


def solution(mesh):
    length, size = mesh.devices.shape
    split = Mesh(mesh.devices.reshape(length // 2, 2, size), (*SEQ, "fsdp"))
    rows = P((*SEQ, "fsdp"), None)
    wide = P(None, SEQ, "fsdp")
    tall = P(None, "fsdp", SEQ)
    weights = (wide, wide, wide, tall, wide, wide, tall)
    return jax.shard_map(
        local,
        mesh=split,
        in_specs=(rows, *weights, P(), P(), P(), P(), P(), rows),
        out_specs=(rows, rows, *weights, P(), P(), P(), P()),
        check_vma=False,
    )
```
